32 devices in a mesh: section: 4 (over y, x), rows: 8 (over z, core).
Axes of the slice: x: 2, y: 2, z: 4, core: 2. Of those that a mesh axis runs over, the one named last changes fastest.
Arguments:
- node_in: bfloat16 [4, 1024, 512], P(None, 'rows'), may hold values from -27 to 27
- edge_in: bfloat16 [4, 8192, 512], P(None, 'rows'), may hold values from -27 to 27
- node_cot: bfloat16 [4, 1024, 512], P(None, 'rows'), may hold values from -6 to 6
- edge_cot: bfloat16 [4, 8192, 512], P(None, 'rows'), may hold values from -6 to 6
- own_weight: bfloat16 [4, 512, 512], P('section'), may hold values from -0.15625 to 0.15625
- other_weight: bfloat16 [4, 512, 512], P('section'), may hold values from -0.15625 to 0.15625
- recv_weight: bfloat16 [2, 512, 512], P(None, 'section'), may hold values from -0.15625 to 0.15625
- first_bias: float32 [4, 512], P('section'), may hold values from -3 to 3
- out_weight: bfloat16 [4, 512, 512], P('section'), may hold values from -0.25 to 0.25
- out_bias: float32 [4, 512], P('section'), may hold values from -3 to 3
- norm_gain: float32 [4, 512], P('section'), may hold values from 0.25 to 1.75
- norm_bias: float32 [4, 512], P('section'), may hold values from -2 to 2
- senders: int32 [8192], P('rows'), may hold values from 0 to 1023, as said below
- receivers: int32 [8192], P('rows'), may hold values from 0 to 1023, as said below
- node_valid: int32 [1024], P('rows'), may hold values 0 or 1
- edge_valid: int32 [8192], P('rows'), may hold values 0 or 1
Outputs:
- node_out: bfloat16 [4, 4, 1024, 512], P('section', None, 'rows')
- edge_out: bfloat16 [4, 4, 8192, 512], P('section', None, 'rows')
- node_grad: bfloat16 [4, 4, 1024, 512], P('section', None, 'rows')
- edge_grad: bfloat16 [4, 4, 8192, 512], P('section', None, 'rows')
- grad_own: float32 [4, 512, 512], P('section')
- grad_other: float32 [4, 512, 512], P('section')
- grad_recv: float32 [2, 512, 512], P(None, 'section')
- grad_first_bias: float32 [4, 512], P('section')
- grad_out_weight: float32 [4, 512, 512], P('section')
- grad_out_bias: float32 [4, 512], P('section')
- grad_gain: float32 [4, 512], P('section')
- grad_norm_bias: float32 [4, 512], P('section')
- branch_rms: float32 [4, 4], P('section')
- stream_rms: float32 [4, 4], P('section')
The draws below stay inside these ranges and needn't reach their ends.
Inputs may be any that keep to these rules, and one draw needn't show every extreme that they name: `senders`: the sender of edge slot i lies among the 128 nodes of block (i mod 1024) // 128. `receivers`: the receiver of edge slot i lies among the 128 nodes of block i // 1024.
All inputs are finite; a program needn't handle non-finite values. No bound on the sum of `node_valid` or of `edge_valid` on one device may be relied on, other than what follows from the above.
Results may differ from the reference program's by a relative error of at most 0.012.
Values may be sent and summed in bfloat16 or wider, within the bound.
No kernel may reach another device: no remote copies, remote signals or barrier semaphores. Data moves between devices by JAX's collectives and lax.ppermute only.
A program may use at most 256 MiB of HBM per device.

```python
from functools import partial
import jax
import jax.numpy as jnp
from jax import lax

D = 512
LAYERS = 2
MICRO = 4
NODE_DEV = 128
EDGE_DEV = 1024
CAP = 128
NODES = 1024
EDGES = 8192
N_SECTION = 4


def rise_profile(total_rows):
    position = jnp.arange(total_rows, dtype=jnp.float32) / (total_rows - 1)
    return jnp.exp(position * jnp.log(3.0))[None, :, None]


def draw_node_in(key, part):
    key = jax.random.fold_in(key, 3)
    rising = rise_profile(NODES)
    values = jnp.clip(jax.random.normal(key, (MICRO, NODES, D), jnp.float32), -6.0, 6.0) * rising
    return values.astype(jnp.bfloat16)


def draw_edge_in(key, part):
    key = jax.random.fold_in(key, 4)
    rising = rise_profile(EDGES)
    values = jnp.clip(jax.random.normal(key, (MICRO, EDGES, D), jnp.float32), -6.0, 6.0) * rising
    return values.astype(jnp.bfloat16)


def draw_senders(key, part):
    key = jax.random.fold_in(key, 1)
    position = jnp.arange(EDGES, dtype=jnp.int32)
    bucket = position % EDGE_DEV // CAP
    local_node = jax.random.randint(key, (EDGES,), 0, NODE_DEV, dtype=jnp.int32)
    local_node = jnp.where(position == 0, 0, jnp.where(position == EDGES - 1, NODE_DEV - 1, local_node))
    return bucket * NODE_DEV + local_node


def draw_receivers(key, part):
    key = jax.random.fold_in(key, 2)
    position = jnp.arange(EDGES, dtype=jnp.int32)
    block = position // EDGE_DEV
    local_node = jax.random.randint(key, (EDGES,), 0, NODE_DEV, dtype=jnp.int32)
    local_node = jnp.where(position == 0, 0, jnp.where(position == EDGES - 1, NODE_DEV - 1, local_node))
    return block * NODE_DEV + local_node


def place_ends(values, stream_key, least, largest):
    longest = values.shape.index(max(values.shape))
    spots = []
    for shift in (0, 1):
        where = [jax.random.randint(jax.random.fold_in(stream_key, axis), (), 0, length) for axis, length in enumerate(values.shape)]
        where[longest] = (where[longest] + shift) % values.shape[longest]
        spots.append(tuple(where))
    return values.at[spots[0]].set(least).at[spots[1]].set(largest)


def level_of(key, dims, shards, low, high):
    level = 1.0
    for axis_at, blocks in shards:
        draws = jax.random.uniform(jax.random.fold_in(jax.random.fold_in(key, 6), axis_at), (blocks,), jnp.float32, low / len(shards), high / len(shards))
        level = level * jnp.repeat(jnp.exp(draws), dims[axis_at] // blocks).reshape((-1,) + (1,) * (len(dims) - 1 - axis_at))
    return level


def normal_values(stream_key, dims, scale, reach, shards=(), held_as=jnp.bfloat16):
    level = level_of(stream_key, dims, shards, -0.22, 0.18) if shards else 1.0
    values = jax.random.normal(stream_key, dims, jnp.float32) * scale * level
    return jnp.minimum(jnp.maximum(values, -reach), reach).astype(held_as)


def setup_inputs(seed: int = 0) -> dict:
    key_list = jax.random.split(jax.random.key(seed), 17)
    node_in = draw_node_in(jax.random.fold_in(key_list[16], 71), 0)
    edge_in = draw_edge_in(jax.random.fold_in(key_list[16], 71), 0)
    node_cot = normal_values(key_list[2], (MICRO, NODES, D), 1.0, 6.0, ((1, 8),))
    edge_cot = normal_values(key_list[3], (MICRO, EDGES, D), 1.0, 6.0, ((1, 8),))
    own_weight = normal_values(key_list[4], (N_SECTION, D, D), (3 * D) ** -0.5, 0.15625, ((0, 4),))
    other_weight = normal_values(key_list[5], (N_SECTION, D, D), (3 * D) ** -0.5, 0.15625, ((0, 4),))
    recv_weight = normal_values(key_list[6], (LAYERS, D, D), (3 * D) ** -0.5, 0.15625, ((1, 4),))
    first_bias = normal_values(key_list[7], (N_SECTION, D), 0.5, 3.0, ((0, 4),), jnp.float32)
    out_weight = normal_values(key_list[8], (N_SECTION, D, D), D ** -0.5, 0.25, ((0, 4),))
    out_bias = normal_values(key_list[9], (N_SECTION, D), 0.5, 3.0, ((0, 4),), jnp.float32)
    norm_gain = jnp.clip(1.0 + 0.15 * jax.random.normal(key_list[10], (N_SECTION, D), jnp.float32), 0.25, 1.75)
    norm_bias = normal_values(key_list[11], (N_SECTION, D), 0.3, 2.0, ((0, 4),), jnp.float32)
    senders = draw_senders(jax.random.fold_in(key_list[16], 71), 0)
    receivers = draw_receivers(jax.random.fold_in(key_list[16], 71), 0)
    node_valid = place_ends((jax.random.randint(key_list[14], (NODES,), 0, 8) < 7).astype(jnp.int32), jax.random.fold_in(key_list[14], 1), 0, 1)
    edge_valid = place_ends((jax.random.randint(key_list[15], (EDGES,), 0, 5) < 4).astype(jnp.int32), jax.random.fold_in(key_list[15], 1), 0, 1)
    return {"node_in": node_in, "edge_in": edge_in, "node_cot": node_cot, "edge_cot": edge_cot, "own_weight": own_weight, "other_weight": other_weight, "recv_weight": recv_weight, "first_bias": first_bias, "out_weight": out_weight, "out_bias": out_bias, "norm_gain": norm_gain, "norm_bias": norm_bias, "senders": senders, "receivers": receivers, "node_valid": node_valid, "edge_valid": edge_valid}


@jax.custom_vjp
def low(v):
    return lax.optimization_barrier(v.astype(jnp.bfloat16)).astype(jnp.float32)

@jax.custom_vjp
def low_back(v):
    return v

def low_keep(v):
    return (low(v), None)

def low_pass(kept, grad):
    return (grad,)

def back_keep(v):
    return (v, None)

def back_low(kept, grad):
    return (low(grad),)
low.defvjp(low_keep, low_pass)
low_back.defvjp(back_keep, back_low)

def matmul(left, right):
    return jnp.dot(left, right, precision=lax.Precision.HIGHEST, preferred_element_type=jnp.float32)

def normalize(update, norm_scale, norm_shift):
    centre = update - lax.optimization_barrier(jnp.mean(update, axis=-1, keepdims=True))
    spread = lax.optimization_barrier(jnp.mean(centre * centre, axis=-1, keepdims=True))
    return centre * lax.rsqrt(spread + 1e-05) * norm_scale + norm_shift

def forward_micro(weights, node_probes, edge_probes, node_lat, edge_lat, sender_ids, receiver_ids, node_mask, edge_mask):
    wide_own, wide_other, bias_first, wide_out, bias_out, norm_scale, norm_shift, wide_recv = weights
    edge_column = edge_mask[:, None]
    node_column = node_mask[:, None]
    node_outs = []
    edge_outs = []
    branch_parts = []
    stream_parts = []
    for section_id in range(N_SECTION):
        node_lat = low_back(node_lat + node_probes[section_id])
        edge_lat = low_back(edge_lat + edge_probes[section_id])
        if section_id % 2 == 0:
            pre_act = matmul(edge_lat, wide_own[section_id]) + matmul(node_lat[sender_ids], wide_other[section_id])
            pre_act = pre_act + matmul(node_lat[receiver_ids], wide_recv[section_id // 2]) + bias_first[section_id]
        else:
            summed = low(jax.ops.segment_sum(edge_column * edge_lat, receiver_ids, num_segments=NODES))
            pre_act = matmul(node_lat, wide_own[section_id]) + matmul(summed, wide_other[section_id]) + bias_first[section_id]
        pre_act = low_back(pre_act)
        hidden = low(jax.nn.silu(pre_act))
        update = low_back(matmul(hidden, wide_out[section_id]) + bias_out[section_id])
        normed = normalize(update, norm_scale[section_id], norm_shift[section_id])
        if section_id % 2 == 0:
            stream = edge_lat + edge_column * normed
            column = edge_column
            edge_lat = low(stream)
        else:
            stream = node_lat + node_column * normed
            column = node_column
            node_lat = low(stream)
        node_outs.append(node_lat)
        edge_outs.append(edge_lat)
        branch_parts.append(jnp.sum(column * update * update))
        stream_parts.append(jnp.sum(column * stream * stream))
    return ((node_lat, edge_lat), (node_outs, edge_outs, branch_parts, stream_parts))

def reference(node_in, edge_in, node_cot, edge_cot, own_weight, other_weight, recv_weight, first_bias, out_weight, out_bias, norm_gain, norm_bias, senders, receivers, node_valid, edge_valid):
    weights = (own_weight.astype(jnp.float32), other_weight.astype(jnp.float32), first_bias.astype(jnp.float32), out_weight.astype(jnp.float32), out_bias.astype(jnp.float32), norm_gain.astype(jnp.float32), norm_bias.astype(jnp.float32), recv_weight.astype(jnp.float32))
    node_mask = node_valid.astype(jnp.float32)
    edge_mask = edge_valid.astype(jnp.float32)
    node_zero = jnp.zeros((N_SECTION, NODES, D), jnp.float32)
    edge_zero = jnp.zeros((N_SECTION, EDGES, D), jnp.float32)
    grads = jax.tree.map(jnp.zeros_like, weights)
    node_outs, edge_outs, node_grads, edge_grads, branch_all, stream_all = ([], [], [], [], [], [])
    for micro in range(MICRO):
        func = partial(forward_micro, node_lat=node_in[micro].astype(jnp.float32), edge_lat=edge_in[micro].astype(jnp.float32), sender_ids=senders, receiver_ids=receivers, node_mask=node_mask, edge_mask=edge_mask)
        finals, back_fn, extras = jax.vjp(func, weights, node_zero, edge_zero, has_aux=True)
        weight_grad, node_probe_grad, edge_probe_grad = back_fn((node_cot[micro].astype(jnp.float32), edge_cot[micro].astype(jnp.float32)))
        grads = jax.tree.map(lambda total, piece: total + piece, grads, weight_grad)
        node_outs.append(jnp.stack(extras[0]).astype(jnp.bfloat16))
        edge_outs.append(jnp.stack(extras[1]).astype(jnp.bfloat16))
        node_grads.append(node_probe_grad.astype(jnp.bfloat16))
        edge_grads.append(edge_probe_grad.astype(jnp.bfloat16))
        branch_all.append(jnp.stack(extras[2]))
        stream_all.append(jnp.stack(extras[3]))
    node_out = jnp.stack(node_outs, axis=1)
    edge_out = jnp.stack(edge_outs, axis=1)
    node_grad = jnp.stack(node_grads, axis=1)
    edge_grad = jnp.stack(edge_grads, axis=1)
    counts = jnp.stack([jnp.sum(edge_mask) if section_id % 2 == 0 else jnp.sum(node_mask) for section_id in range(N_SECTION)])[:, None] * D
    branch_rms = jnp.sqrt(jnp.stack(branch_all, axis=1) / counts)
    stream_rms = jnp.sqrt(jnp.stack(stream_all, axis=1) / counts)
    return (node_out, edge_out, node_grad, edge_grad, grads[0], grads[1], grads[7], grads[2], grads[3], grads[4], grads[5], grads[6], branch_rms, stream_rms)
```

```python
import functools

import jax
import jax.numpy as jnp
from jax import lax
from jax.experimental import pallas as pl
from jax.experimental.pallas import tpu as pltpu
from jax.sharding import PartitionSpec as P

F32 = jnp.float32
BF = jnp.bfloat16
CHUNK = 256
LANES = 128
OWN, OTHER, OUT, RECV, VEC = 0, 1, 2, 3, 4


def dot(left, right):
    return jnp.dot(left, right, preferred_element_type=F32)


def dot_nt(left, right):
    return lax.dot_general(left, right, (((1,), (1,)), ((), ())), preferred_element_type=F32)


def dot_tn(left, right):
    return lax.dot_general(left, right, (((0,), (0,)), ((), ())), preferred_element_type=F32)


def sigmoid(value):
    return 0.5 * jnp.tanh(0.5 * value) + 0.5


def widen(column, width):
    return jnp.concatenate([column] * (width // column.shape[1]), axis=1)


def normalized(update):
    centre = update - jnp.mean(update, axis=-1, keepdims=True)
    spread = jnp.mean(centre * centre, axis=-1, keepdims=True)
    inverse = lax.rsqrt(spread + 1e-05)
    return centre * inverse, inverse


def norm_back(grad_normed, scaled, inverse, gain):
    weighted = grad_normed * gain
    mean_grad = jnp.mean(weighted, axis=-1, keepdims=True)
    mean_both = jnp.mean(weighted * scaled, axis=-1, keepdims=True)
    return inverse * (weighted - mean_grad - scaled * mean_both)


def row_sum(value):
    return jnp.sum(value, axis=0, keepdims=True)


class Weights:
    def __init__(self, pack, halves, others):
        self.arrays = [pack] + halves + others

    def fetch(self, refs, info, parts, wbuf, pvec, sem, width):
        section, core = info[0], info[1]
        half = width // 2
        near = pl.multiple_of(core * half, half)
        far = pl.multiple_of((1 - core) * half, half)

        def one(step, section_id, source, rows, buffer, target):
            for rel in range(4):

                @pl.when((section ^ section_id) == rel)
                def _():
                    if rel == 0:
                        step(refs[0].at[pl.ds(source, rows)], buffer.at[pl.ds(target, rows)])
                    else:
                        place = pl.ds(target, rows)
                        step(refs[rel].at[pl.ds(source, rows)], buffer.at[place, pl.ds(near, half)])
                        step(refs[3 + rel].at[pl.ds(source, rows)], buffer.at[place, pl.ds(far, half)])

        def start(source, target):
            pltpu.make_async_copy(source, target, sem).start()

        quarter = width // 4
        total = 0
        for place, (section_id, part) in enumerate(parts):
            if part == RECV:
                layer = section_id // 2
                for piece in range(4):
                    one(start, piece, 3 * width + layer * quarter, quarter, wbuf, place * width + piece * quarter)
            else:
                one(start, section_id, part * width, width, wbuf, place * width)
        for section_id in range(4):
            one(start, section_id, 3 * width + 2 * quarter, 16, pvec, section_id * 16)
        for place in range(len(parts)):
            pltpu.make_async_copy(
                refs[0].at[pl.ds(0, width)], wbuf.at[pl.ds(place * width, width)], sem
            ).wait()
        pltpu.make_async_copy(refs[0].at[pl.ds(0, 64)], pvec, sem).wait()


def vectors(pvec, section_id):
    block = pvec[pl.ds(section_id * 16, 16), :].astype(F32)
    return [block[k : k + 1] + block[4 + k : 5 + k] for k in range(4)]


def run_kernel(body, steps, info, inputs, outputs, scratch, flops):
    def spec(shape, kind):
        if kind == "a":
            return pl.BlockSpec(memory_space=pl.ANY)
        rest = (0,) * (len(shape) - 1)
        if kind == "c":
            return pl.BlockSpec(tuple(shape), lambda i, info: (0,) + rest)
        block = (1,) + tuple(shape[1:])
        if kind == "m":
            return pl.BlockSpec(block, lambda i, info: (i,) + rest)
        return pl.BlockSpec(block, lambda i, info: (info[2 + i],) + rest)

    names = [name for name, _, _ in inputs]
    aliases = {}
    for index, entry in enumerate(outputs):
        if entry[4] is not None:
            aliases[1 + names.index(entry[4])] = index
    all_names = ["info"] + names + [entry[0] for entry in outputs] + [name for name, _ in scratch]

    def kernel(*refs):
        body(pl.program_id(0), dict(zip(all_names, refs)))

    moved = sum(array.size * array.dtype.itemsize for _, array, kind in inputs if kind != "a")
    results = pl.pallas_call(
        kernel,
        out_shape=[jax.ShapeDtypeStruct(entry[1], entry[2]) for entry in outputs],
        grid_spec=pltpu.PrefetchScalarGridSpec(
            num_scalar_prefetch=1,
            grid=(steps,),
            in_specs=[spec(array.shape, kind) for _, array, kind in inputs],
            out_specs=[spec(entry[1], entry[3]) for entry in outputs],
            scratch_shapes=[shape for _, shape in scratch],
        ),
        input_output_aliases=aliases,
        compiler_params=pltpu.CompilerParams(
            vmem_limit_bytes=58 * 1024 * 1024, dimension_semantics=("arbitrary",)
        ),
        cost_estimate=pl.CostEstimate(flops=flops, bytes_accessed=2 * moved, transcendentals=0),
    )(info, *[array for _, array, _ in inputs])
    return {entry[0]: result for entry, result in zip(outputs, results)}


class Graph:
    def __init__(self, node_rows, edge_rows, blocks, width):
        self.node_rows = node_rows
        self.edge_rows = edge_rows
        self.blocks = blocks
        self.width = width
        self.cap = edge_rows // blocks
        self.chunk = min(CHUNK, edge_rows)


def place_blocks(graph, refs, info, first, hall):
    row = 0
    for ref in refs:
        rows = ref.shape[1]
        count = rows // graph.node_rows
        if len(refs) == 1:
            hall[...] = ref[0]
        else:
            offset = pl.multiple_of(info[first + row] * graph.node_rows, graph.node_rows)
            hall[pl.ds(offset, rows), :] = ref[0]
        row += count


def gather_rows(graph, onehot, hall, chunk_id):
    per_chunk = graph.chunk // graph.cap
    pieces = []
    for piece in range(per_chunk):
        bucket = chunk_id * per_chunk + piece
        rows = pl.ds(bucket * graph.cap, graph.cap)
        nodes = pl.ds(bucket * graph.node_rows, graph.node_rows)
        pieces.append(dot(onehot[rows, :], hall[nodes, :]))
    return jnp.concatenate(pieces, axis=0) if len(pieces) > 1 else pieces[0]


def add_stats(stat, row, inverse, mean_sq, stream, mask):
    branch = jnp.sum(mask * mean_sq, axis=0, keepdims=True)
    total = jnp.sum(mask * jnp.sum(stream * stream, axis=-1, keepdims=True), axis=0, keepdims=True)
    stat[0, 0:1, :] += jnp.broadcast_to(branch, (1, LANES))
    stat[0, 1:2, :] += jnp.broadcast_to(total, (1, LANES))


def tail(pre_act, weight_out, vecs):
    hidden = (pre_act * sigmoid(pre_act)).astype(BF)
    update = dot(hidden, weight_out) + vecs[1]
    scaled, inverse = normalized(update)
    square = jnp.sum(update * update, axis=-1, keepdims=True)
    return hidden, scaled, inverse, square, scaled * vecs[2] + vecs[3]


def first_kernel(graph, steps, info, edge_in, node_in, blocks, consts, weights):
    rows_e, rows_n, width = graph.edge_rows, graph.node_rows, graph.width
    parts = [(0, OWN), (0, OTHER), (0, OUT), (0, RECV), (1, OWN), (1, OTHER), (1, OUT), (2, OTHER)]
    inputs = [("edge", edge_in, "o"), ("node", node_in, "o")]
    inputs += [(f"block{k}", array, "m") for k, array in enumerate(blocks)]
    inputs += [(name, array, "c") for name, array in consts.items()]
    inputs += [(f"w{k}", array, "a") for k, array in enumerate(weights.arrays)]
    outputs = [
        ("edge1", (steps, rows_e, width), BF, "m", None),
        ("z0", (steps, rows_e, width), BF, "m", None),
        ("x0", (steps, rows_e, width), BF, "m", None),
        ("q0", (steps, rows_e, LANES), F32, "m", None),
        ("s0", (steps, rows_e, width), BF, "m", None),
        ("node1", (steps, rows_n, width), BF, "m", None),
        ("g1", (steps, rows_n, width), BF, "m", None),
        ("z1", (steps, rows_n, width), F32, "m", None),
        ("x1", (steps, rows_n, width), F32, "m", None),
        ("q1", (steps, rows_n, LANES), F32, "m", None),
        ("t2", (steps, rows_n, width), BF, "m", None),
        ("stat", (steps, 8, LANES), F32, "m", None),
    ]
    scratch = [
        ("wbuf", pltpu.VMEM((len(parts) * width, width), BF)),
        ("pvec", pltpu.VMEM((64, width), BF)),
        ("hall", pltpu.VMEM((graph.blocks * rows_n, width), BF)),
        ("sem", pltpu.SemaphoreType.DMA),
    ]

    def body(step, R):
        info = R["info"]

        @pl.when(step == 0)
        def _():
            weights.fetch(
                [R[f"w{k}"] for k in range(7)], info, parts, R["wbuf"], R["pvec"], R["sem"], width
            )

        W = [R["wbuf"].at[pl.ds(k * width, width)] for k in range(len(parts))]
        place_blocks(graph, [R[f"block{k}"] for k in range(len(blocks))], info, 6, R["hall"])
        section = info[0]
        R["stat"][...] = jnp.zeros_like(R["stat"])
        vecs = vectors(R["pvec"], 0)
        node = R["node"][0]
        recv_node = dot(node, W[3][...]).astype(BF)
        summed = jnp.zeros((rows_n, width), F32)
        for c in range(rows_e // graph.chunk):
            rows = pl.ds(c * graph.chunk, graph.chunk)
            mask = R["emask"][rows, :]
            edge = R["edge"][0, rows, :]
            send = gather_rows(graph, R["ohs"], R["hall"], c).astype(BF)
            R["s0"][0, rows, :] = send
            pre_act = dot(edge, W[0][...]) + dot(send, W[1][...]) + dot(R["ohr"][rows, :], recv_node) + vecs[0]
            hidden, scaled, inverse, square, normed = tail(pre_act, W[2][...], vecs)
            stream = edge.astype(F32) + widen(mask, width) * normed
            low = stream.astype(BF)
            R["edge1"][0, rows, :] = low
            R["z0"][0, rows, :] = pre_act.astype(BF)
            R["x0"][0, rows, :] = scaled.astype(BF)
            R["q0"][0, rows, :] = jnp.broadcast_to(inverse, (graph.chunk, LANES))
            summed = summed + dot(R["ohrt"][:, rows], low)

            @pl.when(section == 0)
            def _():
                add_stats(R["stat"], 0, inverse, square, stream, mask[:, :1])

        vecs = vectors(R["pvec"], 1)
        summed = summed.astype(BF)
        R["g1"][0] = summed
        pre_act = dot(node, W[4][...]) + dot(summed, W[5][...]) + vecs[0]
        hidden, scaled, inverse, square, normed = tail(pre_act, W[6][...], vecs)
        nmask = R["nmask"][...]
        stream = node.astype(F32) + widen(nmask, width) * normed
        low = stream.astype(BF)
        R["node1"][0] = low
        R["z1"][0] = pre_act
        R["x1"][0] = scaled
        R["q1"][0] = jnp.broadcast_to(inverse, (rows_n, LANES))
        R["t2"][0] = dot(low, W[7][...]).astype(BF)

        @pl.when(section == 1)
        def _():
            add_stats(R["stat"], 0, inverse, square, stream, nmask[:, :1])

    return run_kernel(body, steps, info, inputs, outputs, scratch, steps * 4 * 10**9)


def wg_shapes(width):
    return [("wg", (4 * width, width), F32, "c", None), ("vec", (16, width), F32, "c", None)]


def second_kernel(graph, steps, info, first, blocks, cots, before, consts, weights, own_first):
    rows_e, rows_n, width = graph.edge_rows, graph.node_rows, graph.width
    parts = [(2, OWN), (2, OUT), (2, RECV), (3, OWN), (3, OTHER), (3, OUT)]
    node_cot, edge_cot = cots
    inputs = [("edge", first["edge1"], "m"), ("node", first["node1"], "m"), ("node_in", first["node_in"], "o")]
    inputs += [("gn", node_cot, "o"), ("ge", edge_cot, "o")]
    inputs += [(f"block{k}", array, "m") for k, array in enumerate(blocks)]
    inputs += [(name, array, "c") for name, array in consts.items()]
    inputs += [(f"w{k}", array, "a") for k, array in enumerate(weights.arrays)]
    micro = node_cot.shape[0]
    if before is not None:
        inputs += [("old_edge", before["edge_out"], "a"), ("old_node", before["node_out"], "a")]
    outputs = [
        ("edge_out", (micro, rows_e, width), BF, "o", None if before is None else "old_edge"),
        ("node_out", (micro, rows_n, width), BF, "o", None if before is None else "old_node"),
        ("eg", (steps, rows_e, width), BF, "m", None),
        ("ng", (steps, rows_n, width), BF, "m", None),
        ("gr", (steps, rows_n, width), BF, "m", None),
        ("stat", (steps, 8, LANES), F32, "m", None),
    ] + wg_shapes(width)
    if own_first:
        outputs.append(("gs", (graph.blocks * rows_n, width), BF, "c", None))
        outputs.append(("eg2", (steps, rows_e, width), BF, "m", None))
    scratch = [
        ("wbuf", pltpu.VMEM((len(parts) * width, width), BF)),
        ("pvec", pltpu.VMEM((64, width), BF)),
        ("hall", pltpu.VMEM((graph.blocks * rows_n, width), BF)),
        ("z", pltpu.VMEM((rows_e, width), F32)),
        ("x", pltpu.VMEM((rows_e, width), F32)),
        ("q", pltpu.VMEM((rows_e, LANES), F32)),
        ("a", pltpu.VMEM((rows_e, width), BF)),
        ("gz", pltpu.VMEM((rows_e, width), BF)),
        ("sem", pltpu.SemaphoreType.DMA),
    ]

    def body(step, R):
        info = R["info"]
        section = info[0]

        @pl.when(step == 0)
        def _():
            weights.fetch(
                [R[f"w{k}"] for k in range(7)], info, parts, R["wbuf"], R["pvec"], R["sem"], width
            )
            R["wg"][...] = jnp.zeros_like(R["wg"])
            R["vec"][...] = jnp.zeros_like(R["vec"])

        W = [R["wbuf"].at[pl.ds(k * width, width)] for k in range(len(parts))]
        place_blocks(graph, [R[f"block{k}"] for k in range(len(blocks))], info, 6, R["hall"])
        R["stat"][...] = jnp.zeros_like(R["stat"])
        vecs = vectors(R["pvec"], 2)
        node = R["node"][0]
        recv_node = dot(node, W[2][...]).astype(BF)
        summed = jnp.zeros((rows_n, width), F32)
        for c in range(rows_e // graph.chunk):
            rows = pl.ds(c * graph.chunk, graph.chunk)
            mask = R["emask"][rows, :]
            edge = R["edge"][0, rows, :]
            send = gather_rows(graph, R["ohs"], R["hall"], c)
            pre_act = dot(edge, W[0][...]) + send + dot(R["ohr"][rows, :], recv_node) + vecs[0]
            hidden, scaled, inverse, square, normed = tail(pre_act, W[1][...], vecs)
            stream = edge.astype(F32) + widen(mask, width) * normed
            low = stream.astype(BF)
            R["edge_out"][0, rows, :] = jnp.where(section >= 2, low, edge)
            R["z"][rows, :] = pre_act
            R["x"][rows, :] = scaled
            R["q"][rows, :] = jnp.broadcast_to(inverse, (graph.chunk, LANES))
            R["a"][rows, :] = hidden
            summed = summed + dot(R["ohrt"][:, rows], low)

            @pl.when(section == 2)
            def _():
                add_stats(R["stat"], 0, inverse, square, stream, mask[:, :1])

        vecs = vectors(R["pvec"], 3)
        summed = summed.astype(BF)
        pre_act = dot(node, W[3][...]) + dot(summed, W[4][...]) + vecs[0]
        hidden, scaled, inverse, square, normed = tail(pre_act, W[5][...], vecs)
        nmask = R["nmask"][...]
        wide_mask = widen(nmask, width)
        stream = node.astype(F32) + wide_mask * normed
        R["node_out"][0] = jnp.where(
            section == 0, R["node_in"][0], jnp.where(section == 3, stream.astype(BF), node)
        )

        @pl.when(section == 3)
        def _():
            add_stats(R["stat"], 0, inverse, square, stream, nmask[:, :1])

        grad = R["gn"][0].astype(F32)
        grad_normed = wide_mask * grad
        grad_update = norm_back(grad_normed, scaled, inverse, vecs[2]).astype(BF)
        sig = sigmoid(pre_act)
        grad_pre = (dot_nt(grad_update, W[5][...]) * (sig * (1.0 + pre_act * (1.0 - sig)))).astype(BF)
        R["ng"][0] = (grad + dot_nt(grad_pre, W[3][...])).astype(BF)
        grad_sum = dot_nt(grad_pre, W[4][...])
        grad_high = grad_sum.astype(BF)
        grad_both = jnp.concatenate([grad_high, (grad_sum - grad_high.astype(F32)).astype(BF)], axis=0)

        @pl.when(section == 3)
        def _():
            R["wg"][0:width, :] += dot_tn(node, grad_pre)
            R["wg"][width : 2 * width, :] += dot_tn(summed, grad_pre)
            R["wg"][2 * width : 3 * width, :] += dot_tn(hidden, grad_update)
            R["vec"][0:1, :] += row_sum(grad_pre.astype(F32))
            R["vec"][1:2, :] += row_sum(grad_update.astype(F32))
            R["vec"][2:3, :] += row_sum(grad_normed * scaled)
            R["vec"][3:4, :] += row_sum(grad_normed)

        vecs = vectors(R["pvec"], 2)
        for c in range(rows_e // graph.chunk):
            rows = pl.ds(c * graph.chunk, graph.chunk)
            onehot = R["ohr"][rows, :]
            mask = widen(R["emask"][rows, :], width)
            spread = dot(jnp.concatenate([onehot, onehot], axis=1), grad_both)
            grad = (R["ge"][0, rows, :].astype(F32) + mask * spread).astype(BF)

            @pl.when(section == 3)
            def _():
                R["eg"][0, rows, :] = grad

            @pl.when(jnp.logical_or(section != 3, own_first))
            def _():
                wide = grad.astype(F32)
                grad_normed = mask * wide
                scaled = R["x"][rows, :]
                inverse = R["q"][rows, 0:1]
                pre_act = R["z"][rows, :]
                grad_update = norm_back(grad_normed, scaled, inverse, vecs[2]).astype(BF)
                sig = sigmoid(pre_act)
                grad_pre = (dot_nt(grad_update, W[1][...]) * (sig * (1.0 + pre_act * (1.0 - sig)))).astype(BF)
                R["gz"][rows, :] = grad_pre
                grad_edge = (wide + dot_nt(grad_pre, W[0][...])).astype(BF)
                if own_first:
                    R["eg2"][0, rows, :] = grad_edge

                @pl.when(section != 3)
                def _():
                    R["eg"][0, rows, :] = grad_edge

                @pl.when(section == 2)
                def _():
                    R["wg"][0:width, :] += dot_tn(R["edge"][0, rows, :], grad_pre)
                    R["wg"][2 * width : 3 * width, :] += dot_tn(R["a"][rows, :], grad_update)
                    R["vec"][0:1, :] += row_sum(grad_pre.astype(F32))
                    R["vec"][1:2, :] += row_sum(grad_update.astype(F32))
                    R["vec"][2:3, :] += row_sum(grad_normed * scaled)
                    R["vec"][3:4, :] += row_sum(grad_normed)

        grad_recv = dot(R["ohrt"][...], R["gz"][...]).astype(BF)
        R["gr"][0] = grad_recv

        @pl.when(section == 2)
        def _():
            R["wg"][3 * width : 4 * width, :] += dot_tn(node, grad_recv)

        if own_first:
            sender_sums(graph, R["ohs"], R["gz"], info, R["gs"])

    return run_kernel(body, steps, info, inputs, outputs, scratch, steps * 8 * 10**9)


def sender_sums(graph, onehot, grads, info, target):
    for place in range(graph.blocks):
        bucket = info[6 + place]
        rows = pl.ds(pl.multiple_of(bucket * graph.cap, graph.cap), graph.cap)
        target[pl.ds(place * graph.node_rows, graph.node_rows), :] = dot_tn(
            onehot[rows, :], grads[rows, :]
        ).astype(BF)


def third_kernel(graph, steps, info, first, second, sums, edge_in, node_in, before, consts, weights, own_first):
    rows_e, rows_n, width = graph.edge_rows, graph.node_rows, graph.width
    parts = [(2, RECV), (2, OTHER), (1, OWN), (1, OTHER), (1, OUT), (0, OWN), (0, OUT), (0, RECV)]
    inputs = [("edge", edge_in, "o"), ("node", node_in, "o")]
    inputs += [(name, second[name], "m") for name in ("eg", "ng", "gr")]
    inputs += [(name, first[name], "m") for name in ("z0", "x0", "q0", "s0", "node1", "g1", "z1", "x1", "q1")]
    inputs += [("gs2", sums, "m")]
    if own_first:
        inputs.append(("eg2", second["eg2"], "m"))
    inputs += [(name, array, "c") for name, array in consts.items()]
    inputs += [(f"w{k}", array, "a") for k, array in enumerate(weights.arrays)]
    micro = node_in.shape[0]
    if before is not None:
        inputs += [("old_edge", before["edge_grad"], "a"), ("old_node", before["node_grad"], "a"), ("old_part", before["node_part"], "a")]
    outputs = [
        ("edge_grad", (micro, rows_e, width), BF, "o", None if before is None else "old_edge"),
        ("node_grad", (micro, rows_n, width), BF, "o", None if before is None else "old_node"),
        ("node_part", (micro, rows_n, width), F32, "o", None if before is None else "old_part"),
    ] + wg_shapes(width)
    if own_first:
        outputs.append(("gs", (graph.blocks * rows_n, width), BF, "c", None))
    scratch = [
        ("wbuf", pltpu.VMEM((len(parts) * width, width), BF)),
        ("pvec", pltpu.VMEM((64, width), BF)),
        ("gz", pltpu.VMEM((rows_e, width), BF)),
        ("dg", pltpu.VMEM((2 * rows_n, width), BF)),
        ("ng1", pltpu.VMEM((rows_n, width), F32)),
        ("sem", pltpu.SemaphoreType.DMA),
    ]

    def body(step, R):
        info = R["info"]
        section = info[0]

        @pl.when(step == 0)
        def _():
            weights.fetch(
                [R[f"w{k}"] for k in range(7)], info, parts, R["wbuf"], R["pvec"], R["sem"], width
            )
            R["wg"][...] = jnp.zeros_like(R["wg"])
            R["vec"][...] = jnp.zeros_like(R["vec"])

        W = [R["wbuf"].at[pl.ds(k * width, width)] for k in range(len(parts))]
        gs2 = R["gs2"][0]
        grad_mid = (
            R["ng"][0].astype(F32) + dot_nt(R["gr"][0], W[0][...]) + dot_nt(gs2, W[1][...])
        ).astype(BF)
        R["node_grad"][0] = jnp.where(section == 3, R["ng"][0], grad_mid)

        @pl.when(section == 2)
        def _():
            R["wg"][width : 2 * width, :] += dot_tn(R["node1"][0], gs2)

        @pl.when(section >= 2)
        def _():
            R["edge_grad"][0] = R["eg"][0]

        @pl.when(jnp.logical_or(section <= 1, own_first))
        def _():
            vecs = vectors(R["pvec"], 1)
            wide = grad_mid.astype(F32)
            grad_normed = widen(R["nmask"][...], width) * wide
            scaled = R["x1"][0]
            pre_act = R["z1"][0]
            grad_update = norm_back(grad_normed, scaled, R["q1"][0][:, 0:1], vecs[2]).astype(BF)
            sig = sigmoid(pre_act)
            grad_pre = (dot_nt(grad_update, W[4][...]) * (sig * (1.0 + pre_act * (1.0 - sig)))).astype(BF)
            grad_node = (wide + dot_nt(grad_pre, W[2][...])).astype(BF)
            R["ng1"][...] = grad_node.astype(F32)
            grad_sum = dot_nt(grad_pre, W[3][...])
            grad_high = grad_sum.astype(BF)
            R["dg"][0:rows_n, :] = grad_high
            R["dg"][rows_n : 2 * rows_n, :] = (grad_sum - grad_high.astype(F32)).astype(BF)

            @pl.when(section == 1)
            def _():
                R["node_grad"][0] = grad_node
                R["wg"][0:width, :] += dot_tn(R["node"][0], grad_pre)
                R["wg"][width : 2 * width, :] += dot_tn(R["g1"][0], grad_pre)
                R["wg"][2 * width : 3 * width, :] += dot_tn((pre_act * sig).astype(BF), grad_update)
                R["vec"][0:1, :] += row_sum(grad_pre.astype(F32))
                R["vec"][1:2, :] += row_sum(grad_update.astype(F32))
                R["vec"][2:3, :] += row_sum(grad_normed * scaled)
                R["vec"][3:4, :] += row_sum(grad_normed)

            vecs = vectors(R["pvec"], 0)
            for c in range(rows_e // graph.chunk):
                rows = pl.ds(c * graph.chunk, graph.chunk)
                onehot = R["ohr"][rows, :]
                mask = widen(R["emask"][rows, :], width)
                spread = dot(jnp.concatenate([onehot, onehot], axis=1), R["dg"][...])
                arriving = R["eg2" if own_first else "eg"][0, rows, :].astype(F32)
                grad = (arriving + mask * spread).astype(BF)

                @pl.when(section == 1)
                def _():
                    R["edge_grad"][0, rows, :] = grad

                @pl.when(jnp.logical_or(section == 0, own_first))
                def _():
                    wide = grad.astype(F32)
                    grad_normed = mask * wide
                    scaled = R["x0"][0, rows, :].astype(F32)
                    pre_act = R["z0"][0, rows, :].astype(F32)
                    inverse = R["q0"][0, rows, 0:1]
                    grad_update = norm_back(grad_normed, scaled, inverse, vecs[2]).astype(BF)
                    sig = sigmoid(pre_act)
                    grad_pre = (dot_nt(grad_update, W[6][...]) * (sig * (1.0 + pre_act * (1.0 - sig)))).astype(BF)
                    R["gz"][rows, :] = grad_pre

                    @pl.when(section == 0)
                    def _():
                        R["edge_grad"][0, rows, :] = (wide + dot_nt(grad_pre, W[5][...])).astype(BF)
                        R["wg"][0:width, :] += dot_tn(R["edge"][0, rows, :], grad_pre)
                        R["wg"][width : 2 * width, :] += dot_tn(R["s0"][0, rows, :], grad_pre)
                        R["wg"][2 * width : 3 * width, :] += dot_tn((pre_act * sig).astype(BF), grad_update)
                        R["vec"][0:1, :] += row_sum(grad_pre.astype(F32))
                        R["vec"][1:2, :] += row_sum(grad_update.astype(F32))
                        R["vec"][2:3, :] += row_sum(grad_normed * scaled)
                        R["vec"][3:4, :] += row_sum(grad_normed)

            @pl.when(section == 0)
            def _():
                grad_recv = dot(R["ohrt"][...], R["gz"][...]).astype(BF)
                R["node_part"][0] = R["ng1"][...] + dot_nt(grad_recv, W[7][...])
                R["wg"][3 * width : 4 * width, :] += dot_tn(R["node"][0], grad_recv)

        if own_first:
            sender_sums(graph, R["ohs"], R["gz"], info, R["gs"])

    return run_kernel(body, steps, info, inputs, outputs, scratch, steps * 8 * 10**9)


def on_device(
    node_in,
    edge_in,
    node_cot,
    edge_cot,
    own_weight,
    other_weight,
    recv_weight,
    first_bias,
    out_weight,
    out_bias,
    norm_gain,
    norm_bias,
    senders,
    receivers,
    node_valid,
    edge_valid,
):
    micro, rows_n, width = node_in.shape
    rows_e = edge_in.shape[1]
    blocks = lax.axis_size("rows")
    section = lax.axis_index("section")
    row_pos = lax.axis_index("rows")
    core = row_pos % 2
    graph = Graph(rows_n, rows_e, blocks, width)
    lines = blocks // 2
    direct = lines == 4
    here = row_pos // 2

    def swap(value):
        return lax.ppermute(value, "rows", [(i, i ^ 1) for i in range(blocks)])

    def along(value, distance):
        route = [(i, (i // 2 + distance) % lines * 2 + i % 2) for i in range(blocks)]
        return lax.ppermute(value, "rows", route)

    def across(value, rel):
        return lax.ppermute(value, "section", [(i, i ^ rel) for i in range(4)])

    def gathered_lines(value):
        return [value] + [along(value, r) for r in range(1, 4)]

    def gathered(value):
        if not direct:
            return [lax.all_gather(value, "rows", axis=1, tiled=True)]
        mine = gathered_lines(value)
        return mine + [swap(block) for block in mine]

    def scattered(value):
        if not direct:
            return lax.psum_scatter(value, "rows", scatter_dimension=0, tiled=True)
        half = 4 * rows_n
        summed = value[:half] + swap(value[half:])
        total = summed[:rows_n].astype(F32)
        for r in range(1, 4):
            total = total + along(summed[r * rows_n : (r + 1) * rows_n], -r).astype(F32)
        return total.astype(BF)

    vecs = jnp.concatenate([first_bias, out_bias, norm_gain, norm_bias], axis=0)
    vec_high = vecs.astype(BF)
    vec_low = (vecs - vec_high.astype(F32)).astype(BF)
    pack = jnp.concatenate(
        [own_weight[0], other_weight[0], out_weight[0], recv_weight[0], recv_weight[1], vec_high, vec_low, vec_high, vec_low],
        axis=0,
    )
    half_pack = lax.dynamic_slice_in_dim(pack, core * (width // 2), width // 2, axis=1)
    halves = [across(half_pack, rel) for rel in range(1, 4)]
    weights = Weights(pack, halves, [swap(half) for half in halves])

    if direct:
        places = [((here - r) % 4) * 2 + core for r in range(4)] + [((here - r) % 4) * 2 + 1 - core for r in range(4)]
    else:
        places = [jnp.int32(k) for k in range(blocks)]

    def info_of(order):
        order = list(order) + [jnp.int32(0)] * (4 - len(order))
        return jnp.stack([section, core] + order + places).astype(jnp.int32)

    others = [section ^ rel for rel in range(1, 4)]
    info_own = info_of([section])
    info_rest = info_of(others)

    send_local = senders % rows_n
    recv_local = receivers % rows_n
    node_ids = jnp.arange(rows_n, dtype=jnp.int32)
    emask = edge_valid.astype(F32)
    consts = {
        "ohs": (send_local[:, None] == node_ids[None, :]).astype(BF),
        "ohr": (recv_local[:, None] == node_ids[None, :]).astype(BF),
        "ohrt": ((recv_local[None, :] == node_ids[:, None]) & (edge_valid[None, :] != 0)).astype(BF),
        "emask": jnp.broadcast_to(emask[:, None], (rows_e, LANES)),
        "nmask": jnp.broadcast_to(node_valid.astype(F32)[:, None], (rows_n, LANES)),
    }

    def pick(array, index):
        return lax.dynamic_index_in_dim(array, index, 0, keepdims=True)

    own_blocks = gathered(pick(node_in, section))
    rest_blocks = gathered(jnp.concatenate([pick(node_in, k) for k in others], axis=0))
    first_own = first_kernel(graph, 1, info_own, edge_in, node_in, own_blocks, consts, weights)
    blocks2_own = gathered(first_own["t2"])
    first_rest = first_kernel(graph, 3, info_rest, edge_in, node_in, rest_blocks, consts, weights)
    first_own["node_in"] = node_in
    first_rest["node_in"] = node_in
    if direct:
        mine = jnp.concatenate([block[0] for block in blocks2_own[1:4]], axis=0)
        shared = jnp.stack([across(mine, rel) for rel in range(1, 4)])
        far = swap(jnp.concatenate([first_rest["t2"], shared], axis=1))
        blocks2_rest = [first_rest["t2"]] + [shared[:, r * rows_n : (r + 1) * rows_n] for r in range(3)]
        blocks2_rest += [far[:, r * rows_n : (r + 1) * rows_n] for r in range(4)]
    else:
        blocks2_rest = gathered(first_rest["t2"])
    cots = (node_cot, edge_cot)
    second_own = second_kernel(graph, 1, info_own, first_own, blocks2_own, cots, None, consts, weights, True)
    sums_own = scattered(second_own["gs"])
    second_rest = second_kernel(graph, 3, info_rest, first_rest, blocks2_rest, cots, second_own, consts, weights, False)
    sums_rest = jnp.stack([across(sums_own, rel) for rel in range(1, 4)])
    third_own = third_kernel(
        graph, 1, info_own, first_own, second_own, sums_own[None], edge_in, node_in, None, consts, weights, True
    )
    low_own = scattered(third_own["gs"])
    third_rest = third_kernel(
        graph, 3, info_rest, first_rest, second_rest, sums_rest, edge_in, node_in, third_own, consts, weights, False
    )
    low_rest = [lax.ppermute(low_own, "section", [(rel, 0)]) for rel in range(1, 4)]
    sums_low = jnp.stack([low_own] + low_rest)
    node_zero = third_rest["node_part"] + dot_nt(sums_low.reshape(micro * rows_n, width), other_weight[0]).reshape(
        micro, rows_n, width
    )
    node_grad = jnp.where(section == 0, node_zero.astype(BF), third_rest["node_grad"])

    wg = third_own["wg"] + third_rest["wg"] + jnp.where(section >= 2, second_own["wg"] + second_rest["wg"], 0.0)
    vec = third_own["vec"] + third_rest["vec"] + jnp.where(section >= 2, second_own["vec"] + second_rest["vec"], 0.0)
    quarter = width // 4
    recv = wg[3 * width :].astype(BF)

    def recv_block(rel):
        return lax.dynamic_slice_in_dim(recv, (section ^ rel) * quarter, quarter, axis=0)

    recv_x = lax.ppermute(recv_block(1), "section", [(0, 1), (2, 3)])
    recv_y = lax.ppermute(recv_block(2), "section", [(0, 2), (2, 0)])
    recv_d = lax.ppermute(recv_block(3), "section", [(0, 3), (2, 1)])
    mine = recv_block(0)
    recv_l0 = jnp.where(section == 0, mine, jnp.where(section == 1, recv_x, jnp.where(section == 2, recv_y, recv_d)))
    recv_l1 = jnp.where(section == 0, recv_y, jnp.where(section == 1, recv_d, jnp.where(section == 2, mine, recv_x)))
    stat_own = jnp.where(section >= 2, second_own["stat"], first_own["stat"])
    stat_rest = jnp.where(section >= 2, second_rest["stat"], first_rest["stat"])
    valid = jnp.where(section % 2 == 0, jnp.sum(emask), jnp.sum(node_valid.astype(F32)))
    parts = jnp.concatenate([stat_own, stat_rest], axis=0)[:, :2, 0]
    small = jnp.concatenate([parts.T.reshape(8), valid[None], jnp.zeros((width - 9,), F32)])[None]
    tail_rows = jnp.concatenate([vec[:4], small, jnp.zeros((3, width), F32)], axis=0)
    if direct:
        pad = jnp.zeros((128 - 8, width), BF)
        flat = jnp.concatenate([wg[: 3 * width].astype(BF), recv_l0, recv_l1, tail_rows.astype(BF), pad], axis=0)
        count = flat.shape[0]
        half = count // 2
        piece = half // 4
        summed = lax.dynamic_slice_in_dim(flat, core * half, half, axis=0) + swap(
            lax.dynamic_slice_in_dim(flat, (1 - core) * half, half, axis=0)
        )

        def line_piece(r):
            return lax.dynamic_slice_in_dim(summed, ((here - r) % 4) * piece, piece, axis=0)

        total = line_piece(0).astype(F32)
        for r in range(1, 4):
            total = total + along(line_piece(r), -r).astype(F32)
        lines_all = gathered_lines(total.astype(BF))
        mine_half = jnp.zeros((half, width), BF)
        for r in range(4):
            mine_half = lax.dynamic_update_slice_in_dim(mine_half, lines_all[r], ((here - r) % 4) * piece, axis=0)
        other_half = swap(mine_half)
        full = jnp.concatenate(
            [jnp.where(core == 0, mine_half, other_half), jnp.where(core == 0, other_half, mine_half)], axis=0
        ).astype(F32)
    else:
        flat = jnp.concatenate(
            [wg[: 3 * width], recv_l0.astype(F32), recv_l1.astype(F32), tail_rows], axis=0
        )
        full = lax.psum(flat, "rows")
    grad_recv = full[3 * width : 3 * width + 2 * quarter].reshape(2, quarter, width)
    base = 3 * width + 2 * quarter
    stats = full[base + 4, :9]
    denominator = stats[8] * width
    rms = jnp.sqrt(stats[:8] / denominator).reshape(2, 4)
    relative = jnp.arange(4, dtype=jnp.int32) ^ section
    rms = jnp.take(rms, relative, axis=1)
    return (
        second_rest["node_out"][None],
        second_rest["edge_out"][None],
        node_grad[None],
        third_rest["edge_grad"][None],
        full[None, :width],
        full[None, width : 2 * width],
        grad_recv,
        full[base : base + 1],
        full[None, 2 * width : 3 * width],
        full[base + 1 : base + 2],
        full[base + 2 : base + 3],
        full[base + 3 : base + 4],
        rms[0:1],
        rms[1:2],
    )


def solution(mesh):
    return jax.shard_map(
        on_device,
        mesh=mesh,
        in_specs=(
            P(None, "rows", None),
            P(None, "rows", None),
            P(None, "rows", None),
            P(None, "rows", None),
            P("section", None, None),
            P("section", None, None),
            P(None, "section", None),
            P("section", None),
            P("section", None, None),
            P("section", None),
            P("section", None),
            P("section", None),
            P("rows"),
            P("rows"),
            P("rows"),
            P("rows"),
        ),
        out_specs=(
            P("section", None, "rows", None),
            P("section", None, "rows", None),
            P("section", None, "rows", None),
            P("section", None, "rows", None),
            P("section", None, None),
            P("section", None, None),
            P(None, "section", None),
            P("section", None),
            P("section", None, None),
            P("section", None),
            P("section", None),
            P("section", None),
            P("section", None),
            P("section", None),
        ),
        check_vma=False,
    )
```

```python
import jax
import jax.numpy as jnp
from jax import lax
from jax.experimental import pallas as pl
from jax.experimental.pallas import tpu as pltpu
from jax.sharding import PartitionSpec as P

F32 = jnp.float32
BF = jnp.bfloat16
CHUNK = 512
LANES = 128
VEC_ROWS = 16
ANY = pl.ANY
VMEM = pltpu.VMEM
HBM = pltpu.HBM


def dot(left, right):
    return jnp.dot(left, right, preferred_element_type=F32)


def dot_nt(left, right):
    return lax.dot_general(left, right, (((1,), (1,)), ((), ())), preferred_element_type=F32)


def dot_tn(left, right):
    return lax.dot_general(left, right, (((0,), (0,)), ((), ())), preferred_element_type=F32)


def sigmoid(value):
    return 0.5 * jnp.tanh(0.5 * value) + 0.5


def widen(column, width):
    return jnp.concatenate([column] * (width // column.shape[1]), axis=1)


def col_sum(value):
    return jnp.sum(value, axis=0, keepdims=True)


def tail(pre_act, weight_out, vecs):
    hidden = (pre_act * sigmoid(pre_act)).astype(BF)
    update = dot(hidden, weight_out) + vecs[1]
    mean = jnp.mean(update, axis=-1, keepdims=True)
    centre = update - mean
    spread = jnp.mean(centre * centre, axis=-1, keepdims=True)
    inverse = lax.rsqrt(spread + 1e-05)
    scaled = centre * inverse
    return hidden, scaled, inverse, spread + mean * mean, scaled * vecs[2] + vecs[3]


def norm_back(grad_normed, scaled, inverse, gain):
    weighted = grad_normed * gain
    mean_grad = jnp.mean(weighted, axis=-1, keepdims=True)
    mean_both = jnp.mean(weighted * scaled, axis=-1, keepdims=True)
    return inverse * (weighted - mean_grad - scaled * mean_both)


def silu_back(grad_hidden, pre_act):
    sig = sigmoid(pre_act)
    return grad_hidden * (sig * (1.0 + pre_act * (1.0 - sig))), sig


def run_kernel(body, info, inputs, outputs, scratch, micros, limit=24):
    place = {"v": VMEM, "h": HBM}
    names = [name for name, _, _ in inputs]
    aliases = {}
    for index, entry in enumerate(outputs):
        if entry[4] is not None:
            aliases[1 + names.index(entry[4])] = index
    all_names = ["info"] + names + [entry[0] for entry in outputs] + [name for name, _ in scratch]

    def kernel(*refs):
        body(dict(zip(all_names, refs)))

    arrays = [pltpu.with_memory_space_constraint(array, place[kind]) for _, array, kind in inputs]
    results = pl.pallas_call(
        kernel,
        out_shape=[
            jax.ShapeDtypeStruct(entry[1], entry[2]) if entry[3] == "b" else place[entry[3]](entry[1], entry[2])
            for entry in outputs
        ],
        in_specs=[pl.BlockSpec(memory_space=pltpu.SMEM)]
        + [pl.BlockSpec(memory_space=place[kind]) for _, _, kind in inputs],
        out_specs=[
            pl.BlockSpec() if entry[3] == "b" else pl.BlockSpec(memory_space=place[entry[3]]) for entry in outputs
        ],
        scratch_shapes=[shape for _, shape in scratch],
        input_output_aliases=aliases,
        compiler_params=pltpu.CompilerParams(vmem_limit_bytes=limit * 1024 * 1024),
        cost_estimate=pl.CostEstimate(flops=int(micros * 1.15e9), bytes_accessed=0, transcendentals=0),
    )(info, *arrays)
    return {entry[0]: result for entry, result in zip(outputs, results)}


def copy(source, target, sem):
    return pltpu.make_async_copy(source, target, sem)


def after_inputs(after):
    return [(f"after{k}", array, "h") for k, array in enumerate(after)]


class Graph:
    def __init__(self, rows_n, rows_e, blocks, width):
        self.rows_n, self.rows_e, self.blocks, self.width = rows_n, rows_e, blocks, width
        self.cap = rows_e // blocks
        self.chunk = min(CHUNK, rows_e)
        self.starts = range(0, rows_e, self.chunk)
        self.consts = {}

    def const_inputs(self):
        return [(name, array, "v") for name, array in self.consts.items()]

    def weight_row(self, section_id, part):
        return (section_id * 3 + part) * self.width

    def weight(self, R, section_id, part, count=1):
        return R["wall"][pl.ds(self.weight_row(section_id, part), count * self.width), :]

    def recv_weight(self, R, layer):
        return R["wall"][pl.ds((12 + layer) * self.width, self.width), :]

    def vectors(self, R, section_id):
        block = R["wall"][pl.ds(14 * self.width + section_id * VEC_ROWS, VEC_ROWS), :].astype(F32)
        return [block[k : k + 1] + block[4 + k : 5 + k] for k in range(4)]


OWN, OTHER, OUT = 0, 1, 2


def half_rows(width):
    half, eighth = width // 2, width // 8
    return half, eighth, 3 * half + 2 * eighth, 3 * half + 2 * eighth + VEC_ROWS


def half_kernel(graph, info, own, other, out, recv, vec):
    half, eighth, vec_row, rows = half_rows(graph.width)
    quarter = 2 * eighth

    def body(R):
        core, sem, stage = R["info"][1], R["sem"], R["stage"]
        for k, name in enumerate(("own", "other", "out")):
            source = R[name].at[pl.ds(pl.multiple_of(core * half, half), half)]
            copy(source, stage.at[pl.ds(k * half, half)], sem).start()
        for layer in range(2):
            source = R["recv"].at[pl.ds(pl.multiple_of(layer * quarter + core * eighth, eighth), eighth)]
            copy(source, stage.at[pl.ds(3 * half + layer * eighth, eighth)], sem).start()
        copy(R["vec"], stage.at[pl.ds(vec_row, VEC_ROWS)], sem).start()
        copy(stage, stage, sem).wait()
        move = copy(stage, R["half"], sem)
        move.start()
        move.wait()

    inputs = [(name, array, "h") for name, array in zip(("own", "other", "out", "recv", "vec"), (own, other, out, recv, vec))]
    outputs = [("half", (rows, graph.width), BF, "h", None)]
    scratch = [("stage", VMEM((rows, graph.width), BF)), ("sem", pltpu.SemaphoreType.DMA)]
    return run_kernel(body, info, inputs, outputs, scratch, 1)["half"]


def wall_kernel(graph, info, own, other, out, recv, vec, near, far):
    width = graph.width
    half, eighth, vec_row, rows = half_rows(width)
    quarter = 2 * eighth
    mine = [("own", own), ("other", other), ("out", out), ("recv", recv), ("vec", vec)]
    inputs = [(name, array, "h") for name, array in mine] + [("far", far, "h")]
    inputs += [(f"near{rel}_{k}", piece[0], "h") for rel, pieces in near.items() for k, piece in enumerate(pieces)]
    total = 14 * width + 4 * VEC_ROWS

    def body(R):
        section, core = R["info"][0], R["info"][1]
        wall, sem = R["wall"], R["sem"]

        def put(source, row, count, unit):
            copy(source, wall.at[pl.ds(pl.multiple_of(row, unit), count)], sem).start()

        for k, (name, _) in enumerate(mine[:3]):
            put(R[name], section * 3 * width + k * width, width, width)
        for layer in range(2):
            put(R["recv"].at[pl.ds(layer * quarter, quarter)], (12 + layer) * width + section * quarter, quarter, quarter)
        put(R["vec"], 14 * width + section * VEC_ROWS, VEC_ROWS, VEC_ROWS)
        for rel in range(1, 4):
            there = section ^ rel
            for side in (core, 1 - core):
                parts = [(k * half, half, (there * 3 + k) * width + side * half, half) for k in range(3)]
                parts += [
                    (3 * half + layer * eighth, eighth, (12 + layer) * width + there * quarter + side * eighth, eighth)
                    for layer in range(2)
                ]
                if side is core:
                    parts.append((vec_row, VEC_ROWS, 14 * width + there * VEC_ROWS, VEC_ROWS))
                for row, count, target, unit in parts:
                    if side is not core:
                        put(R["far"].at[pl.ds((rel - 1) * rows + row, count)], target, count, unit)
                        continue
                    first = 0
                    for k, (_, begin, held) in enumerate(near[rel]):
                        low, high = max(row, first), min(row + count, first + held)
                        if low < high:
                            source = R[f"near{rel}_{k}"].at[pl.ds(begin + low - first, high - low)]
                            put(source, target + low - row, high - low, 16)
                        first += held
        copy(wall, wall, sem).wait()

    outputs = [("wall", (total, width), BF, "v", None)]
    return run_kernel(body, info, inputs, outputs, [("sem", pltpu.SemaphoreType.DMA)], 3)["wall"]


def glue_kernel(graph, info, sources, plan, rows, after=()):
    width = graph.width
    inputs = [(f"in{k}", array, "h") for k, array in enumerate(sources)] + after_inputs(after)
    outputs = [(f"out{k}", (count, width), BF, "h", None) for k, count in enumerate(rows)]
    scratch = [(f"stage{k}", VMEM((count, width), BF)) for k, count in enumerate(rows)]
    scratch.append(("sem", pltpu.SemaphoreType.DMA((len(rows),))))

    def body(R):
        for source, index, row, count, target, place in plan:
            ref = R[f"in{source}"] if index is None else R[f"in{source}"].at[R["info"][0] ^ index]
            copy(ref.at[pl.ds(row, count)], R[f"stage{target}"].at[pl.ds(place, count)], R["sem"].at[target]).start()
        moves = []
        for k in range(len(rows)):
            stage = R[f"stage{k}"]
            copy(stage, stage, R["sem"].at[k]).wait()
            moves.append(copy(stage, R[f"out{k}"], R["sem"].at[k]))
            moves[-1].start()
        for move in moves:
            move.wait()

    results = run_kernel(body, info, inputs, outputs, scratch, 2)
    return [results[f"out{k}"] for k in range(len(rows))]


def add_kernel(graph, info, arrays, rows, after=()):
    count, width = arrays[0].shape
    inputs = [(f"in{k}", array, "h") for k, array in enumerate(arrays)] + after_inputs(after)
    outputs = [(f"out{k}", (rows, width), BF, "h", None) for k in range(count // rows)]
    scratch = [(f"stage{k}", VMEM((count, width), BF)) for k in range(len(arrays))]
    scratch.append(("sem", pltpu.SemaphoreType.DMA((len(arrays),))))

    def body(R):
        moves = [copy(R[f"in{k}"], R[f"stage{k}"], R["sem"].at[k]) for k in range(len(arrays))]
        for move in moves:
            move.start()
        for move in moves:
            move.wait()
        moves = []
        for k in range(count // rows):
            here = pl.ds(k * rows, rows)
            total = R["stage0"][here, :].astype(F32)
            for other in range(1, len(arrays)):
                total = total + R[f"stage{other}"][here, :].astype(F32)
            R["stage0"][here, :] = total.astype(BF)
            moves.append(copy(R["stage0"].at[here], R[f"out{k}"], R["sem"].at[0]))
            moves[-1].start()
        for move in moves:
            move.wait()

    results = run_kernel(body, info, inputs, outputs, scratch, 2)
    return [results[f"out{k}"] for k in range(count // rows)]


def node_zero_kernel(graph, info, parts, sums, node_grad, wall):
    rows_n, width = graph.rows_n, graph.width
    inputs = [(f"part{k}", array, "h") for k, array in enumerate(parts)]
    inputs += [(f"sum{k}", array, "h") for k, array in enumerate(sums)]
    inputs += [("old", node_grad, "h"), ("wall", wall, "v")]
    outputs = [("node_grad", node_grad.shape, BF, "h", "old")]
    scratch = [
        ("part", VMEM((4 * rows_n, width), F32)),
        ("sum", VMEM((4 * rows_n, width), BF)),
        ("total", VMEM((4, rows_n, width), BF)),
        ("sem", pltpu.SemaphoreType.DMA((3,))),
    ]

    def body(R):
        @pl.when(R["info"][0] == 0)
        def _():
            for k in range(4):
                here = pl.ds(k * rows_n, rows_n)
                copy(R[f"part{k}"], R["part"].at[here], R["sem"].at[0]).start()
                copy(R[f"sum{k}"], R["sum"].at[here], R["sem"].at[1]).start()
            copy(R["part"], R["part"], R["sem"].at[0]).wait()
            copy(R["sum"], R["sum"], R["sem"].at[1]).wait()
            total = R["part"][...] + dot_nt(R["sum"][...], graph.weight(R, 0, OTHER))
            R["total"][...] = total.astype(BF).reshape(4, rows_n, width)
            move = copy(R["total"], R["node_grad"], R["sem"].at[2])
            move.start()
            move.wait()

    return run_kernel(body, info, inputs, outputs, scratch, 2)["node_grad"]


def const_kernel(graph, info, arrays):
    inputs = [(f"{name}_in", array, "h") for name, array in arrays.items()]
    outputs = [(name, array.shape, array.dtype, "v", None) for name, array in arrays.items()]

    def body(R):
        moves = [copy(R[f"{name}_in"], R[name], R["sem"].at[k]) for k, name in enumerate(arrays)]
        for move in moves:
            move.start()
        for move in moves:
            move.wait()

    return run_kernel(body, info, inputs, outputs, [("sem", pltpu.SemaphoreType.DMA((len(arrays),)))], 2)


def block_inputs(blocks):
    return [(f"block{k}", array, "h") for k, (array, _, _, _) in enumerate(blocks)]


def block_copies(graph, R, blocks, sem):
    moves = []
    place = 0
    for k, (_, index, row, rows) in enumerate(blocks):
        source = R[f"block{k}"]
        if index is not None:
            source = source.at[R["info"][2] if index == "micro" else index]
        if rows == graph.rows_n:
            start = pl.multiple_of(R["info"][3 + place] * graph.rows_n, graph.rows_n)
        else:
            start = 0
        moves.append(copy(source.at[pl.ds(row, rows)], R["hall"].at[pl.ds(start, rows)], sem))
        place += rows // graph.rows_n
    return moves


def bucket_rows(graph, start):
    for bucket in range(start // graph.cap, (start + graph.chunk) // graph.cap):
        yield pl.ds(bucket * graph.cap, graph.cap), pl.ds(bucket * graph.rows_n, graph.rows_n)


def stack(pieces):
    return jnp.concatenate(pieces, axis=0) if len(pieces) > 1 else pieces[0]


def stat_pair(square, stream, mask):
    branch = col_sum(mask * square)
    total = col_sum(mask * jnp.sum(stream * stream, axis=-1, keepdims=True))
    return branch, total


def put_stats(stat, pairs, width):
    branch, total = pairs[0]
    for pair in pairs[1:]:
        branch, total = branch + pair[0], total + pair[1]
    stat[0:1, :] = jnp.broadcast_to(branch * width, (1, LANES))
    stat[1:2, :] = jnp.broadcast_to(total, (1, LANES))


def first_kernel(graph, info, edge_in, node_in, blocks, after):
    rows_e, rows_n, width = graph.rows_e, graph.rows_n, graph.width
    inputs = [("edges", edge_in, "h"), ("nodes", node_in, "h")] + block_inputs(blocks) + graph.const_inputs()
    inputs += after_inputs(after)
    outputs = [
        ("edge1", (rows_e, width), BF, "v", None),
        ("z0", (rows_e, width), BF, "v", None),
        ("x0", (rows_e, width), BF, "v", None),
        ("q0", (rows_e, LANES), F32, "v", None),
        ("s0", (rows_e, width), BF, "v", None),
        ("node0", (rows_n, width), BF, "v", None),
        ("node1", (rows_n, width), BF, "v", None),
        ("g1", (rows_n, width), BF, "v", None),
        ("z1", (rows_n, width), BF, "v", None),
        ("x1", (rows_n, width), BF, "v", None),
        ("q1", (rows_n, LANES), F32, "v", None),
        ("stat", (8, LANES), F32, "v", None),
        ("t2", (rows_n, width), BF, "h", None),
    ]
    scratch = [
        ("edge", VMEM((rows_e, width), BF)),
        ("hall", VMEM((graph.blocks * rows_n, width), BF)),
        ("t2_here", VMEM((rows_n, width), BF)),
        ("sem", pltpu.SemaphoreType.DMA((4,))),
    ]

    def body(R):
        info = R["info"]
        section, micro = info[0], info[2]
        node_copy = copy(R["nodes"].at[micro], R["node0"], R["sem"].at[0])
        hall_copies = block_copies(graph, R, blocks, R["sem"].at[1])
        edge_copy = copy(R["edges"].at[micro], R["edge"], R["sem"].at[2])
        node_copy.start()
        for move in hall_copies:
            move.start()
        edge_copy.start()
        node_copy.wait()
        node = R["node0"][...]
        recv_node = dot(node, graph.recv_weight(R, 0)).astype(BF)
        copy(R["hall"], R["hall"], R["sem"].at[1]).wait()
        edge_copy.wait()
        vecs = graph.vectors(R, 0)
        pairs = []
        for start in graph.starts:
            rows = pl.ds(start, graph.chunk)
            mask = R["emask"][rows, :]
            edge = R["edge"][rows, :]
            send = stack([dot(R["ohs"][e, :], R["hall"][n, :]).astype(BF) for e, n in bucket_rows(graph, start)])
            R["s0"][rows, :] = send
            pre_act = dot(jnp.concatenate([edge, send], axis=1), graph.weight(R, 0, OWN, 2))
            pre_act = pre_act + dot(R["ohr"][rows, :], recv_node) + vecs[0]
            hidden, scaled, inverse, square, normed = tail(pre_act, graph.weight(R, 0, OUT), vecs)
            stream = edge.astype(F32) + widen(mask, width) * normed
            R["edge1"][rows, :] = stream.astype(BF)
            R["z0"][rows, :] = pre_act.astype(BF)
            R["x0"][rows, :] = scaled.astype(BF)
            R["q0"][rows, :] = jnp.broadcast_to(inverse, (graph.chunk, LANES))
            pairs.append(stat_pair(square, stream, mask[:, :1]))
        summed = dot(R["ohrt"][...], R["edge1"][...]).astype(BF)
        R["g1"][...] = summed
        vecs = graph.vectors(R, 1)
        pre_act = dot(jnp.concatenate([node, summed], axis=1), graph.weight(R, 1, OWN, 2)) + vecs[0]
        hidden, scaled, inverse, square, normed = tail(pre_act, graph.weight(R, 1, OUT), vecs)
        nmask = R["nmask"][...]
        stream = node.astype(F32) + widen(nmask, width) * normed
        low = stream.astype(BF)
        R["t2_here"][...] = dot(low, graph.weight(R, 2, OTHER)).astype(BF)
        out_copy = copy(R["t2_here"], R["t2"], R["sem"].at[3])
        out_copy.start()
        R["node1"][...] = low
        R["z1"][...] = pre_act.astype(BF)
        R["x1"][...] = scaled.astype(BF)
        R["q1"][...] = jnp.broadcast_to(inverse, (rows_n, LANES))

        @pl.when(section == 0)
        def _():
            put_stats(R["stat"], pairs, width)

        @pl.when(section != 0)
        def _():
            put_stats(R["stat"], [stat_pair(square, stream, nmask[:, :1])], width)

        out_copy.wait()

    return run_kernel(body, info, inputs, outputs, scratch, 8)


def sender_outputs(graph, direct):
    rows = graph.blocks * graph.rows_n
    if direct:
        rows //= 2
        return [(name, (rows, graph.width), BF, "h", None) for name in ("gs_mine", "gs_far")]
    return [("gs_mine", (rows, graph.width), BF, "h", None)]


def sender_sums(graph, R, grads, stage, sem):
    for place in range(graph.blocks):
        bucket = R["info"][3 + place]
        rows = pl.ds(pl.multiple_of(bucket * graph.cap, graph.cap), graph.cap)
        here = pl.ds(place * graph.rows_n, graph.rows_n)
        stage[here, :] = dot_tn(R["ohs"][rows, :], grads[rows, :]).astype(BF)
    for name in ("gs_far", "gs_mine"):
        if name in R:
            rows = R[name].shape[0]
            start = stage.shape[0] - rows if name == "gs_far" else 0
            copy(stage.at[pl.ds(start, rows)], R[name], sem).start()
    copy(stage, stage, sem).wait()


def add_recv(graph, R, layer, node, grad_recv):
    quarter = graph.width // 4
    start = pl.multiple_of(R["info"][0] * quarter, quarter)
    rows = pl.ds(3 * graph.width + layer * quarter, quarter)
    R["wg"][rows, :] += dot_tn(node[:, pl.ds(start, quarter)], grad_recv)


def second_kernel(graph, info, first, blocks, node_cot, edge_cot, before, own_first, direct, after):
    rows_e, rows_n, width = graph.rows_e, graph.rows_n, graph.width
    micro_count = node_cot.shape[0]
    inputs = [(name, first[name], "v") for name in ("edge1", "node0", "node1")]
    inputs += [("edge_cot", edge_cot, "h"), ("node_cot", node_cot, "h")] + block_inputs(blocks) + graph.const_inputs()
    inputs += after_inputs(after)
    if before is not None:
        inputs += [("old_edge", before["edge_out"], "h"), ("old_node", before["node_out"], "h")]
        inputs += [("old_wg", before["wg"], "v"), ("old_vec", before["vec"], "v")]

    def chain(name):
        return None if before is None else name

    outputs = [
        ("edge_out", (micro_count, rows_e, width), BF, "h", chain("old_edge")),
        ("node_out", (micro_count, rows_n, width), BF, "h", chain("old_node")),
        ("wg", (3 * width + width // 2, width), F32, "v", chain("old_wg")),
        ("vec", (8, width), F32, "v", chain("old_vec")),
        ("eg2", (rows_e, width), BF, "v", None),
        ("eg", (rows_e, width), BF, "v", None),
        ("ng", (rows_n, width), BF, "v", None),
        ("gr", (rows_n, width), BF, "v", None),
        ("stat", (8, LANES), F32, "v", None),
    ]
    if own_first:
        outputs += sender_outputs(graph, direct)
    scratch = [
        ("hall", VMEM((graph.blocks * rows_n, width), BF)),
        ("cot", VMEM((rows_e, width), BF)),
        ("ncot", VMEM((rows_n, width), BF)),
        ("edge2", VMEM((rows_e, width), BF)),
        ("node_here", VMEM((rows_n, width), BF)),
        ("z", VMEM((rows_e, width), BF)),
        ("x", VMEM((rows_e, width), BF)),
        ("q", VMEM((rows_e, LANES), F32)),
        ("a", VMEM((rows_e, width), BF)),
        ("gu", VMEM((rows_e, width), BF)),
        ("gz", VMEM((rows_e, width), BF)),
        ("sem", pltpu.SemaphoreType.DMA((8,))),
    ]

    def body(R):
        info = R["info"]
        section, micro = info[0], info[2]
        sem = R["sem"]
        hall_copies = block_copies(graph, R, blocks, sem.at[0])
        cot_copy = copy(R["edge_cot"].at[micro], R["cot"], sem.at[1])
        ncot_copy = copy(R["node_cot"].at[micro], R["ncot"], sem.at[2])
        for move in hall_copies:
            move.start()
        ncot_copy.start()
        cot_copy.start()
        if own_first:
            R["wg"][...] = jnp.zeros_like(R["wg"])
            R["vec"][...] = jnp.zeros_like(R["vec"])
        node = R["node1"][...]
        recv_node = dot(node, graph.recv_weight(R, 1)).astype(BF)
        copy(R["hall"], R["hall"], sem.at[0]).wait()
        vecs = graph.vectors(R, 2)
        pairs = []
        for start in graph.starts:
            rows = pl.ds(start, graph.chunk)
            mask = R["emask"][rows, :]
            edge = R["edge1"][rows, :]
            ends = stack(
                [
                    dot(
                        jnp.concatenate([R["ohs"][e, :], R["ohr"][e, :]], axis=1),
                        jnp.concatenate([R["hall"][n, :], recv_node], axis=0),
                    )
                    for e, n in bucket_rows(graph, start)
                ]
            )
            pre_act = dot(edge, graph.weight(R, 2, OWN)) + ends + vecs[0]
            hidden, scaled, inverse, square, normed = tail(pre_act, graph.weight(R, 2, OUT), vecs)
            stream = edge.astype(F32) + widen(mask, width) * normed
            R["edge2"][rows, :] = stream.astype(BF)
            R["z"][rows, :] = pre_act.astype(BF)
            R["x"][rows, :] = scaled.astype(BF)
            R["q"][rows, :] = jnp.broadcast_to(inverse, (graph.chunk, LANES))
            R["a"][rows, :] = hidden
            pairs.append(stat_pair(square, stream, mask[:, :1]))

        @pl.when(section >= 2)
        def _():
            copy(R["edge2"], R["edge_out"].at[micro], sem.at[3]).start()

        @pl.when(section < 2)
        def _():
            copy(R["edge1"], R["edge_out"].at[micro], sem.at[3]).start()

        vecs = graph.vectors(R, 3)
        summed = dot(R["ohrt"][...], R["edge2"][...]).astype(BF)
        weight_out = graph.weight(R, 3, OUT)
        pre_act = dot(jnp.concatenate([node, summed], axis=1), graph.weight(R, 3, OWN, 2)) + vecs[0]
        hidden, scaled, inverse, square, normed = tail(pre_act, weight_out, vecs)
        nmask = R["nmask"][...]
        wide_mask = widen(nmask, width)
        stream = node.astype(F32) + wide_mask * normed
        R["node_here"][...] = jnp.where(
            section == 0, R["node0"][...], jnp.where(section == 3, stream.astype(BF), node)
        )
        node_copy = copy(R["node_here"], R["node_out"].at[micro], sem.at[4])
        node_copy.start()

        @pl.when(section == 3)
        def _():
            put_stats(R["stat"], [stat_pair(square, stream, nmask[:, :1])], width)

        @pl.when(section != 3)
        def _():
            put_stats(R["stat"], pairs, width)

        ncot_copy.wait()
        grad = R["ncot"][...].astype(F32)
        grad_normed = wide_mask * grad
        grad_update = norm_back(grad_normed, scaled, inverse, vecs[2])
        grad_low = grad_update.astype(BF)
        grad_pre, _ = silu_back(dot_nt(grad_low, weight_out), pre_act)
        pre_low = grad_pre.astype(BF)
        R["ng"][...] = (grad + dot_nt(pre_low, graph.weight(R, 3, OWN))).astype(BF)
        grad_sum = dot_nt(pre_low, graph.weight(R, 3, OTHER))
        grad_high = grad_sum.astype(BF)
        grad_both = jnp.concatenate([grad_high, (grad_sum - grad_high.astype(F32)).astype(BF)], axis=0)

        @pl.when(section == 3)
        def _():
            R["wg"][0:width, :] += dot_tn(node, pre_low)
            R["wg"][width : 2 * width, :] += dot_tn(summed, pre_low)
            R["wg"][2 * width : 3 * width, :] += dot_tn(hidden, grad_low)
            R["vec"][0:1, :] += col_sum(grad_pre)
            R["vec"][1:2, :] += col_sum(grad_update)
            R["vec"][2:3, :] += col_sum(grad_normed * scaled)
            R["vec"][3:4, :] += col_sum(grad_normed)

        cot_copy.wait()
        vecs = graph.vectors(R, 2)

        def arriving(rows, mask):
            onehot = R["ohr"][rows, :]
            spread = dot(jnp.concatenate([onehot, onehot], axis=1), grad_both)
            return (R["cot"][rows, :].astype(F32) + mask * spread).astype(BF)

        def edge_back(sums):
            totals = [jnp.zeros((1, width), F32)] * 4
            for start in graph.starts:
                rows = pl.ds(start, graph.chunk)
                mask = R["emask"][rows, :]
                wide = arriving(rows, widen(mask, width)).astype(F32)
                scaled = R["x"][rows, :].astype(F32)
                pre_act = R["z"][rows, :].astype(F32)
                inverse = widen(R["q"][rows, :] * mask, width)
                grad_update = norm_back(wide, scaled, inverse, vecs[2])
                grad_low = grad_update.astype(BF)
                grad_pre, _ = silu_back(dot_nt(grad_low, graph.weight(R, 2, OUT)), pre_act)
                pre_low = grad_pre.astype(BF)
                R["gz"][rows, :] = pre_low
                R["eg2"][rows, :] = (wide + dot_nt(pre_low, graph.weight(R, 2, OWN))).astype(BF)
                if sums:
                    R["gu"][rows, :] = grad_low
                    normed = widen(mask, width) * wide
                    parts = (grad_pre, grad_update, normed * scaled, normed)
                    totals = [total + col_sum(part) for total, part in zip(totals, parts)]
            if sums:
                R["wg"][0:width, :] += dot_tn(R["edge1"][...], R["gz"][...])
                R["wg"][2 * width : 3 * width, :] += dot_tn(R["a"][...], R["gu"][...])
                for k in range(4):
                    R["vec"][k : k + 1, :] += totals[k]

        @pl.when(section == 2)
        def _():
            edge_back(True)

        @pl.when(section != 2)
        def _():
            edge_back(False)

        @pl.when(section == 3)
        def _():
            for start in graph.starts:
                rows = pl.ds(start, graph.chunk)
                R["eg"][rows, :] = arriving(rows, widen(R["emask"][rows, :], width))

        grad_recv = dot(R["ohrt"][...], R["gz"][...]).astype(BF)
        R["gr"][...] = grad_recv
        add_recv(graph, R, 1, R["node1"], grad_recv)
        if own_first:
            sender_sums(graph, R, R["gz"], R["hall"], sem.at[5])
        node_copy.wait()
        copy(R["edge2"], R["edge_out"].at[micro], sem.at[3]).wait()

    return run_kernel(body, info, inputs, outputs, scratch, 14)


def third_kernel(graph, info, first, second, sums, edge_in, micro_count, before, wg, vec, own_first, direct, after):
    rows_e, rows_n, width = graph.rows_e, graph.rows_n, graph.width
    inputs = [(name, second[name], "v") for name in ("eg", "eg2", "ng", "gr")]
    inputs += [(name, first[name], "v") for name in ("z0", "x0", "q0", "s0", "node0", "node1", "g1", "z1", "x1", "q1")]
    inputs += [("sums", sums, "h"), ("edges", edge_in, "h"), ("old_wg", wg, "v"), ("old_vec", vec, "v")]
    inputs += graph.const_inputs()
    inputs += after_inputs(after)
    if before is not None:
        inputs += [("old_edge", before["edge_grad"], "h"), ("old_node", before["node_grad"], "h")]

    def chain(name):
        return None if before is None else name

    outputs = [
        ("edge_grad", (micro_count, rows_e, width), BF, "h", chain("old_edge")),
        ("node_grad", (micro_count, rows_n, width), BF, "h", chain("old_node")),
        ("wg", wg.shape, F32, "v", "old_wg"),
        ("vec", (8, width), F32, "v", "old_vec"),
        ("node_part", (rows_n, width), F32, "h", None),
    ]
    if own_first:
        outputs += sender_outputs(graph, direct)
    scratch = [
        ("edge", VMEM((rows_e, width), BF)),
        ("sum2", VMEM((rows_n, width), BF)),
        ("out_edge", VMEM((rows_e, width), BF)),
        ("out_node", VMEM((rows_n, width), BF)),
        ("gu", VMEM((rows_e, width), BF)),
        ("a", VMEM((rows_e, width), BF)),
        ("gz", VMEM((rows_e, width), BF)),
        ("part", VMEM((rows_n, width), F32)),
        ("sem", pltpu.SemaphoreType.DMA((6,))),
    ]
    if own_first:
        scratch.append(("stage", VMEM((graph.blocks * rows_n, width), BF)))

    def body(R):
        info = R["info"]
        section, micro = info[0], info[2]
        sem = R["sem"]
        sums_copy = copy(R["sums"], R["sum2"], sem.at[0])
        sums_copy.start()
        edge_copy = copy(R["edges"].at[micro], R["edge"], sem.at[1])

        @pl.when(section == 0)
        def _():
            edge_copy.start()

        sums_copy.wait()
        gs2 = R["sum2"][...]
        grad_mid = (
            R["ng"][...].astype(F32) + dot_nt(R["gr"][...], graph.recv_weight(R, 1)) + dot_nt(gs2, graph.weight(R, 2, OTHER))
        ).astype(BF)
        R["out_node"][...] = jnp.where(section == 3, R["ng"][...], grad_mid)

        @pl.when(section == 2)
        def _():
            R["wg"][width : 2 * width, :] += dot_tn(R["node1"][...], gs2)

        @pl.when(section == 2)
        def _():
            copy(R["eg2"], R["edge_grad"].at[micro], sem.at[2]).start()

        @pl.when(section == 3)
        def _():
            copy(R["eg"], R["edge_grad"].at[micro], sem.at[2]).start()

        vecs = graph.vectors(R, 1)
        wide = grad_mid.astype(F32)
        grad_normed = widen(R["nmask"][...], width) * wide
        scaled = R["x1"][...].astype(F32)
        pre_act = R["z1"][...].astype(F32)
        grad_update = norm_back(grad_normed, scaled, widen(R["q1"][...], width), vecs[2])
        grad_low = grad_update.astype(BF)
        grad_pre, sig = silu_back(dot_nt(grad_low, graph.weight(R, 1, OUT)), pre_act)
        pre_low = grad_pre.astype(BF)
        grad_node = (wide + dot_nt(pre_low, graph.weight(R, 1, OWN))).astype(BF)
        grad_sum = dot_nt(pre_low, graph.weight(R, 1, OTHER))
        grad_high = grad_sum.astype(BF)
        grad_both = jnp.concatenate([grad_high, (grad_sum - grad_high.astype(F32)).astype(BF)], axis=0)

        @pl.when(section == 1)
        def _():
            R["out_node"][...] = grad_node
            R["wg"][0:width, :] += dot_tn(R["node0"][...], pre_low)
            R["wg"][width : 2 * width, :] += dot_tn(R["g1"][...], pre_low)
            R["wg"][2 * width : 3 * width, :] += dot_tn((pre_act * sig).astype(BF), grad_low)
            R["vec"][0:1, :] += col_sum(grad_pre)
            R["vec"][1:2, :] += col_sum(grad_update)
            R["vec"][2:3, :] += col_sum(grad_normed * scaled)
            R["vec"][3:4, :] += col_sum(grad_normed)

        vecs = graph.vectors(R, 0)

        def arriving(rows, mask):
            onehot = R["ohr"][rows, :]
            spread = dot(jnp.concatenate([onehot, onehot], axis=1), grad_both)
            return (R["eg2"][rows, :].astype(F32) + mask * spread).astype(BF)

        def edge_back(sums):
            totals = [jnp.zeros((1, width), F32)] * 4
            for start in graph.starts:
                rows = pl.ds(start, graph.chunk)
                mask = R["emask"][rows, :]
                wide = arriving(rows, widen(mask, width)).astype(F32)
                scaled = R["x0"][rows, :].astype(F32)
                pre_act = R["z0"][rows, :].astype(F32)
                inverse = widen(R["q0"][rows, :] * mask, width)
                grad_update = norm_back(wide, scaled, inverse, vecs[2])
                grad_low = grad_update.astype(BF)
                grad_pre, sig = silu_back(dot_nt(grad_low, graph.weight(R, 0, OUT)), pre_act)
                pre_low = grad_pre.astype(BF)
                R["gz"][rows, :] = pre_low
                if sums:
                    R["out_edge"][rows, :] = (wide + dot_nt(pre_low, graph.weight(R, 0, OWN))).astype(BF)
                    R["gu"][rows, :] = grad_low
                    R["a"][rows, :] = (pre_act * sig).astype(BF)
                    normed = widen(mask, width) * wide
                    parts = (grad_pre, grad_update, normed * scaled, normed)
                    totals = [total + col_sum(part) for total, part in zip(totals, parts)]
            return totals

        @pl.when(section == 0)
        def _():
            totals = edge_back(True)
            copy(R["out_edge"], R["edge_grad"].at[micro], sem.at[2]).start()
            edge_copy.wait()
            R["wg"][0:width, :] += dot_tn(R["edge"][...], R["gz"][...])
            R["wg"][width : 2 * width, :] += dot_tn(R["s0"][...], R["gz"][...])
            R["wg"][2 * width : 3 * width, :] += dot_tn(R["a"][...], R["gu"][...])
            for k in range(4):
                R["vec"][k : k + 1, :] += totals[k]

        @pl.when(section == 1)
        def _():
            for start in graph.starts:
                rows = pl.ds(start, graph.chunk)
                R["out_edge"][rows, :] = arriving(rows, widen(R["emask"][rows, :], width))
            copy(R["out_edge"], R["edge_grad"].at[micro], sem.at[2]).start()

        @pl.when(section > 0)
        def _():
            edge_back(False)

        grad_recv = dot(R["ohrt"][...], R["gz"][...]).astype(BF)
        add_recv(graph, R, 0, R["node0"], grad_recv)

        @pl.when(section == 0)
        def _():
            R["part"][...] = grad_node.astype(F32) + dot_nt(grad_recv, graph.recv_weight(R, 0))

        node_copy = copy(R["out_node"], R["node_grad"].at[micro], sem.at[3])
        node_copy.start()
        part_copy = copy(R["part"], R["node_part"], sem.at[5])
        part_copy.start()
        if own_first:
            sender_sums(graph, R, R["gz"], R["stage"], sem.at[4])
        node_copy.wait()
        part_copy.wait()
        copy(R["out_edge"], R["edge_grad"].at[micro], sem.at[2]).wait()

    return run_kernel(body, info, inputs, outputs, scratch, 10)


PIECES = 8
TAIL_ROWS = 16


def stats_block(graph, R, firsts, seconds):
    section = R["info"][0]
    edge_count = col_sum(R["emask"][...])
    node_count = col_sum(R["nmask"][...])
    even = (section & 1) == 0
    valid = jnp.where(even, edge_count, node_count)
    rows = [R["vec"][0:4, :]]
    for k in range(4):
        pair = jnp.where(section < 2, R[f"first{k}"][0:2, :], R[f"second{k}"][0:2, :])
        rows.append(jnp.concatenate([pair[0:1], pair[1:2], valid, jnp.zeros_like(valid)], axis=1))
    rows.append(jnp.zeros((TAIL_ROWS - 8, graph.width), F32))
    return jnp.concatenate(rows, axis=0)


def pack_kernel(graph, info, wg, vec, stats, direct, after):
    width = graph.width
    held = wg.shape[0]
    piece = -(-(held + TAIL_ROWS) // (16 * PIECES)) * 16
    inputs = [("wg", wg, "v"), ("vec", vec, "v"), ("emask", graph.consts["emask"], "v"), ("nmask", graph.consts["nmask"], "v")]
    for k in range(4):
        inputs += [(f"first{k}", stats[0][k], "v"), (f"second{k}", stats[1][k], "v")]
    inputs += after_inputs(after)
    low = BF if direct else F32
    if direct:
        outputs = [("mine", (4 * piece, width), BF, "h", None), ("other", (4 * piece, width), BF, "h", None)]
    else:
        outputs = [("flat", (PIECES * piece, width), F32, "h", None)]
    scratch = [
        ("stage", VMEM((PIECES * piece, width), low)),
        ("sem", pltpu.SemaphoreType.DMA),
    ]

    def body(R):
        info, sem = R["info"], R["sem"]
        core = info[1]
        R["stage"][0:held, :] = R["wg"][...].astype(low)
        R["stage"][held : held + TAIL_ROWS, :] = stats_block(graph, R, *stats).astype(low)
        rest = PIECES * piece - held - TAIL_ROWS
        if rest:
            R["stage"][held + TAIL_ROWS :, :] = jnp.zeros((rest, width), low)
        if direct:
            for name, side in (("other", 1 - core), ("mine", core)):
                for r in range(4):
                    line = lax.shift_right_logical(info[3 + r], 1)
                    start = pl.multiple_of((side * 4 + line) * piece, 16)
                    copy(R["stage"].at[pl.ds(start, piece)], R[name].at[pl.ds(r * piece, piece)], sem).start()
        else:
            copy(R["stage"], R["flat"], sem).start()
        copy(R["stage"], R["stage"], sem).wait()

    return run_kernel(body, info, inputs, outputs, scratch, 3), piece


def unpack_kernel(graph, info, mine, far, piece):
    width = graph.width
    quarter = width // 4
    inputs = [(f"mine{r}", array, "h") for r, array in enumerate(mine)] + [("far", far, "h")]
    outputs = [
        ("own", (width, width), F32, "h", None),
        ("other", (width, width), F32, "h", None),
        ("out", (width, width), F32, "h", None),
        ("recv", (2 * quarter, width), F32, "h", None),
    ]
    outputs += [(f"vec{k}", (1, width), F32, "b", None) for k in range(4)]
    outputs += [(f"rms{k}", (1, 4), F32, "b", None) for k in range(2)]
    scratch = [
        ("stage", VMEM((PIECES * piece, width), BF)),
        ("wide", VMEM((3 * width, width), F32)),
        ("wide_recv", VMEM((2 * quarter, width), F32)),
        ("sem", pltpu.SemaphoreType.DMA((7,))),
    ]

    def body(R):
        info, sem = R["info"], R["sem"]
        core = info[1]
        for r in range(4):
            line = lax.shift_right_logical(info[3 + r], 1)
            for name, row, side in ((f"mine{r}", 0, core), ("far", r * piece, 1 - core)):
                start = pl.multiple_of((side * 4 + line) * piece, 16)
                copy(R[name].at[pl.ds(row, piece)], R["stage"].at[pl.ds(start, piece)], sem.at[0]).start()
        copy(R["stage"], R["stage"], sem.at[0]).wait()
        moves = []
        for k, name in enumerate(("own", "other", "out")):
            rows = pl.ds(k * width, width)
            R["wide"][rows, :] = R["stage"][rows, :].astype(F32)
            moves.append(copy(R["wide"].at[rows], R[name], sem.at[2 + k]))
            moves[-1].start()
        base = 3 * width + 2 * quarter
        sums = R["stage"][base : base + TAIL_ROWS, :].astype(F32)
        micro = lax.broadcasted_iota(jnp.int32, (1, 4), 1) ^ info[0]
        for k in range(4):
            R[f"vec{k}"][...] = sums[k : k + 1]
        for which in range(2):
            total = jnp.zeros((1, 4), F32)
            for k in range(4):
                row = sums[4 + k : 5 + k]
                square = row[:, which * LANES : which * LANES + 4] / (row[:, 2 * LANES : 2 * LANES + 4] * width)
                total = total + jnp.where(micro == k, jnp.sqrt(square), 0.0)
            R[f"rms{which}"][...] = total
        R["wide_recv"][...] = R["stage"][3 * width : base, :].astype(F32)
        moves.append(copy(R["wide_recv"], R["recv"], sem.at[6]))
        moves[-1].start()
        for move in moves:
            move.wait()

    return run_kernel(body, info, inputs, outputs, scratch, 3)


def on_device(
    node_in,
    edge_in,
    node_cot,
    edge_cot,
    own_weight,
    other_weight,
    recv_weight,
    first_bias,
    out_weight,
    out_bias,
    norm_gain,
    norm_bias,
    senders,
    receivers,
    node_valid,
    edge_valid,
):
    micro_count, rows_n, width = node_in.shape
    rows_e = edge_in.shape[1]
    blocks = lax.axis_size("rows")
    section = lax.axis_index("section")
    row_pos = lax.axis_index("rows")
    core = row_pos % 2
    here = row_pos // 2
    graph = Graph(rows_n, rows_e, blocks, width)
    lines = blocks // 2
    direct = lines == 4
    quarter = width // 4

    def swap(value):
        return lax.ppermute(value, "rows", [(i, i ^ 1) for i in range(blocks)])

    def along(value, distance, flip=0):
        route = [(i, (i // 2 + distance) % lines * 2 + (i % 2 ^ flip)) for i in range(blocks)]
        return lax.ppermute(value, "rows", route)

    def across(value, rel):
        return lax.ppermute(value, "section", [(i, i ^ rel) for i in range(4)])

    if direct:
        places = [((here - r) % 4) * 2 + core for r in range(4)] + [((here - r) % 4) * 2 + 1 - core for r in range(4)]
    else:
        places = [jnp.int32(k) for k in range(blocks)]
    infos = [jnp.stack([section, core, section ^ rel] + places).astype(jnp.int32) for rel in range(4)]

    vecs = jnp.concatenate([first_bias, out_bias, norm_gain, norm_bias], axis=0)
    vec_high = vecs.astype(BF)
    vec_low = (vecs - vec_high.astype(F32)).astype(BF)
    vec_rows = jnp.concatenate([vec_high, vec_low, vec_high, vec_low], axis=0)
    recv_rows = recv_weight.reshape(2 * quarter, width)
    def pick(array, rel):
        return lax.dynamic_index_in_dim(array, section ^ rel, 0, keepdims=False)

    def as_blocks(arrays, index):
        return [(array, index, 0, array.shape[-2]) for array in arrays]

    def lined_up(value):
        return [along(value, r) for r in range(1, 4)]

    half = half_kernel(graph, infos[0], own_weight[0], other_weight[0], out_weight[0], recv_rows, vec_rows)
    half_x, half_y = across(half, 1), across(half, 2)
    held = half.shape[0]
    cut = held // 32 * 16
    after = []
    if direct:
        own_nodes = pick(node_in, 0)
        own_lines = [own_nodes] + lined_up(own_nodes)
        plan = [(r, None, 0, rows_n, 0, r * rows_n) for r in range(4)]
        (own_cat,) = glue_kernel(graph, infos[0], own_lines, plan, [4 * rows_n])
        own_far = swap(own_cat)
        after = [own_cat]
    else:
        node_all = lax.all_gather(jnp.stack([pick(node_in, rel) for rel in range(4)]), "rows", axis=1, tiled=True)
    plan = [(0, None, 0, cut, 0, 0), (1, None, cut, held - cut, 1, 0)]
    send_da, send_db = glue_kernel(graph, infos[0], [half_x, half_y], plan, [cut, held - cut], after)
    half_da, half_db = across(send_da, 2), across(send_db, 1)
    plan = [(0, None, 0, held, 0, 0), (1, None, 0, held, 0, held)]
    plan += [(2, None, 0, cut, 0, 2 * held), (3, None, 0, held - cut, 0, 2 * held + cut)]
    sources = [half_x, half_y, half_da, half_db]
    rows = [3 * held]
    if direct:
        plan.append((4, None, rows_n, 3 * rows_n, 1, 0))
        sources.append(own_cat)
        rows.append(3 * rows_n)
    glued = glue_kernel(graph, infos[0], sources, plan, rows)
    far = swap(glued[0])
    if direct:
        own_shared = [across(glued[1], rel) for rel in range(1, 4)]
    near = {
        1: [(half_x, 0, held)],
        2: [(half_y, 0, held)],
        3: [(half_da, 0, cut), (half_db, 0, held - cut)],
    }

    send_local = senders % rows_n
    recv_local = receivers % rows_n
    node_ids = jnp.arange(rows_n, dtype=jnp.int32)
    emask = edge_valid.astype(F32)
    consts = {
        "ohs": (send_local[:, None] == node_ids[None, :]).astype(BF),
        "ohr": (recv_local[:, None] == node_ids[None, :]).astype(BF),
        "ohrt": ((recv_local[None, :] == node_ids[:, None]) & (edge_valid[None, :] != 0)).astype(BF),
        "emask": jnp.broadcast_to(emask[:, None], (rows_e, LANES)),
        "nmask": jnp.broadcast_to(node_valid.astype(F32)[:, None], (rows_n, LANES)),
    }
    graph.consts = const_kernel(graph, infos[0], consts)
    weights = (own_weight[0], other_weight[0], out_weight[0], recv_rows, vec_rows)
    graph.consts["wall"] = wall_kernel(graph, infos[0], *weights, near, far)
    rest_far = []

    def first_blocks(rel):
        if not direct:
            return as_blocks([node_all], rel)
        if rel == 0:
            return as_blocks(own_lines, None) + [(own_far, None, r * rows_n, rows_n) for r in range(4)]
        entry = [(node_in, "micro", 0, rows_n)]
        entry += [(own_shared[rel - 1], None, r * rows_n, rows_n) for r in range(3)]
        return entry + [(rest_far[0], None, (4 * (rel - 1) + r) * rows_n, rows_n) for r in range(4)]

    first = []
    blocks2 = []

    def add_first(rel, after):
        first.append(first_kernel(graph, infos[rel], edge_in, node_in, first_blocks(rel), after))

    add_first(0, [])
    if direct:
        plan = []
        for k in range(3):
            plan.append((0, k + 1, 0, rows_n, 0, 4 * k * rows_n))
            plan.append((1 + k, None, 0, 3 * rows_n, 0, (4 * k + 1) * rows_n))
        (cat,) = glue_kernel(graph, infos[0], [node_in] + own_shared, plan, [12 * rows_n], [first[0]["t2"]])
        rest_far.append(swap(cat))
        lines2 = [first[0]["t2"]] + lined_up(first[0]["t2"])
        add_first(1, [first[0]["t2"]])
        add_first(2, [first[1]["t2"]])
        plan = [(r, None, 0, rows_n, 0, r * rows_n) for r in range(4)]
        plan += [(r, None, 0, rows_n, 1, (r - 1) * rows_n) for r in range(1, 4)]
        cat, share = glue_kernel(graph, infos[0], lines2, plan, [4 * rows_n, 3 * rows_n], [first[2]["t2"]])
        far2 = swap(cat)
        shared = [across(share, rel) for rel in range(1, 4)]
        add_first(3, [cat])
        blocks2.append(as_blocks(lines2, None) + [(far2, None, r * rows_n, rows_n) for r in range(4)])
    else:
        for rel in range(1, 4):
            add_first(rel, [first[-1]["t2"]])
        for rel in range(4):
            blocks2.append(as_blocks([lax.all_gather(first[rel]["t2"], "rows", axis=0, tiled=True)], None))

    second = []
    third = []

    def add_second(rel, after):
        before = second[-1] if second else None
        second.append(
            second_kernel(graph, infos[rel], first[rel], blocks2[rel], node_cot, edge_cot, before, rel == 0, direct, after)
        )

    def add_third(rel, after):
        before = third[-1] if third else None
        last = third[-1] if third else second[-1]
        third.append(
            third_kernel(
                graph, infos[rel], first[rel], second[rel], sums[rel], edge_in, micro_count, before, last["wg"], last["vec"], rel == 0, direct, after
            )
        )

    add_second(0, [first[3]["t2"]])
    if direct:
        got = swap(second[0]["gs_far"])
        plan = []
        for k in range(3):
            plan.append((k, None, 0, rows_n, 0, 4 * k * rows_n))
            plan.append((3 + k, None, 0, 3 * rows_n, 0, (4 * k + 1) * rows_n))
        sources = [first[rel]["t2"] for rel in range(1, 4)] + shared
        (cat,) = glue_kernel(graph, infos[0], sources, plan, [12 * rows_n], [second[0]["gs_mine"]])
        far2 = swap(cat)
        for rel in range(1, 4):
            entry = [(first[rel]["t2"], None, 0, rows_n)] + [(shared[rel - 1], None, r * rows_n, rows_n) for r in range(3)]
            entry += [(far2, None, (4 * (rel - 1) + r) * rows_n, rows_n) for r in range(4)]
            blocks2.append(entry)
        add_second(1, [])
        parts = add_kernel(graph, infos[0], [second[0]["gs_mine"], got], rows_n, [second[1]["edge_out"]])
        arrived = [along(parts[r], -r) for r in range(1, 4)]
        add_second(2, [parts[0]])
        add_second(3, [])
        (total,) = add_kernel(graph, infos[0], [parts[0]] + arrived, rows_n, [second[3]["edge_out"]])
    else:
        for rel in range(1, 4):
            add_second(rel, [])
        total = lax.psum_scatter(second[0]["gs_mine"], "rows", scatter_dimension=0, tiled=True)
    sums = [total] + [across(total, rel) for rel in range(1, 4)]
    add_third(0, [])
    if direct:
        got = swap(third[0]["gs_far"])
        add_third(1, [])
        parts = add_kernel(graph, infos[0], [third[0]["gs_mine"], got], rows_n, [third[1]["edge_grad"]])
        arrived = [along(parts[r], -r) for r in range(1, 4)]
        add_third(2, [parts[0]])
        add_third(3, [])
        (total,) = add_kernel(graph, infos[0], [parts[0]] + arrived, rows_n, [third[3]["edge_grad"]])
    else:
        for rel in range(1, 4):
            add_third(rel, [])
        total = lax.psum_scatter(third[0]["gs_mine"], "rows", scatter_dimension=0, tiled=True)
    low = [total] + [lax.ppermute(total, "section", [(rel, 0)]) for rel in range(1, 4)]
    wg, vec = third[3]["wg"], third[3]["vec"]

    stats = ([entry["stat"] for entry in first], [entry["stat"] for entry in second])
    packed, piece = pack_kernel(graph, infos[0], wg, vec, stats, direct, [total])
    if direct:
        pieces = add_kernel(graph, infos[0], [packed["mine"], swap(packed["other"])], piece)
        (whole,) = add_kernel(graph, infos[0], [pieces[0]] + [along(pieces[r], -r) for r in range(1, 4)], piece)
        near = [whole] + lined_up(whole)
        plan = [(r, None, 0, piece, 0, r * piece) for r in range(4)]
        (cat,) = glue_kernel(graph, infos[0], near, plan, [4 * piece])
        grads = unpack_kernel(graph, infos[0], near, swap(cat), piece)
    else:
        flat = lax.psum(packed["flat"], "rows")
        base = 3 * width + 2 * quarter
        sums_all = flat[base : base + TAIL_ROWS]
        rms = jnp.sqrt(sums_all[4:8, 0 : 2 * LANES : LANES] / (sums_all[4:8, 2 * LANES : 2 * LANES + 1] * width))
        rms = jnp.take(rms, jnp.arange(4, dtype=jnp.int32) ^ section, axis=0)
        grads = {
            "own": flat[:width],
            "other": flat[width : 2 * width],
            "out": flat[2 * width : 3 * width],
            "recv": flat[3 * width : base],
            "rms0": rms[:, 0][None],
            "rms1": rms[:, 1][None],
        }
        grads.update({f"vec{k}": sums_all[k : k + 1] for k in range(4)})
    node_grad = node_zero_kernel(
        graph, infos[0], [entry["node_part"] for entry in third], low, third[3]["node_grad"], graph.consts["wall"]
    )
    return (
        second[3]["node_out"][None],
        second[3]["edge_out"][None],
        node_grad[None],
        third[3]["edge_grad"][None],
        grads["own"][None],
        grads["other"][None],
        grads["recv"].reshape(2, quarter, width),
        grads["vec0"],
        grads["out"][None],
        grads["vec1"],
        grads["vec2"],
        grads["vec3"],
        grads["rms0"],
        grads["rms1"],
    )


def solution(mesh):
    whole = P("section", None, None)
    line = P("section", None)
    latents = P(None, "rows", None)
    outs = P("section", None, "rows", None)
    recv = P(None, "section", None)
    ends = P("rows")
    return jax.shard_map(
        on_device,
        mesh=mesh,
        in_specs=(latents,) * 4 + (whole, whole, recv, line, whole, line, line, line) + (ends,) * 4,
        out_specs=(outs,) * 4 + (whole, whole, recv, line, whole, line, line, line, line, line),
        check_vma=False,
    )
```

```python
import jax
import jax.numpy as jnp
from jax import lax
from jax.experimental import pallas as pl
from jax.experimental.pallas import tpu as pltpu
from jax.sharding import PartitionSpec as P

F32 = jnp.float32
BF = jnp.bfloat16
CHUNK = 512
LANES = 128
VEC_ROWS = 16
ANY = pl.ANY
VMEM = pltpu.VMEM
HBM = pltpu.HBM


def dot(left, right):
    return jnp.dot(left, right, preferred_element_type=F32)


def dot_nt(left, right):
    return lax.dot_general(left, right, (((1,), (1,)), ((), ())), preferred_element_type=F32)


def dot_tn(left, right):
    return lax.dot_general(left, right, (((0,), (0,)), ((), ())), preferred_element_type=F32)


def sigmoid(value):
    return 0.5 * jnp.tanh(0.5 * value) + 0.5


def widen(column, width):
    return jnp.concatenate([column] * (width // column.shape[1]), axis=1)


def col_sum(value):
    return jnp.sum(value, axis=0, keepdims=True)


def tail(pre_act, weight_out, vecs):
    hidden = (pre_act * sigmoid(pre_act)).astype(BF)
    update = dot(hidden, weight_out) + vecs[1]
    mean = jnp.mean(update, axis=-1, keepdims=True)
    centre = update - mean
    spread = jnp.mean(centre * centre, axis=-1, keepdims=True)
    inverse = lax.rsqrt(spread + 1e-05)
    scaled = centre * inverse
    return hidden, scaled, inverse, spread + mean * mean, scaled * vecs[2] + vecs[3]


def norm_back(grad_normed, scaled, inverse, gain):
    weighted = grad_normed * gain
    mean_grad = jnp.mean(weighted, axis=-1, keepdims=True)
    mean_both = jnp.mean(weighted * scaled, axis=-1, keepdims=True)
    return inverse * (weighted - mean_grad - scaled * mean_both)


def silu_back(grad_hidden, pre_act):
    sig = sigmoid(pre_act)
    return grad_hidden * (sig * (1.0 + pre_act * (1.0 - sig))), sig


class Info:
    def __init__(self, table, rel):
        self.table, self.rel = table, rel

    def __getitem__(self, k):
        return self.table[self.rel, k]


def run_kernel(body, info, inputs, outputs, scratch, micros, limit=18):
    place = {"v": VMEM, "h": HBM, "a": pl.ANY}
    names = [name for name, _, _ in inputs]
    aliases = {}
    for index, entry in enumerate(outputs):
        if entry[4] is not None:
            aliases[1 + names.index(entry[4])] = index
    all_names = ["info"] + names + [entry[0] for entry in outputs] + [name for name, _ in scratch]

    def kernel(*refs):
        body(dict(zip(all_names, (Info(refs[0], info.rel),) + refs[1:])))

    arrays = [pltpu.with_memory_space_constraint(array, place[kind]) for _, array, kind in inputs]
    results = pl.pallas_call(
        kernel,
        out_shape=[
            jax.ShapeDtypeStruct(entry[1], entry[2]) if entry[3] in "ab" else place[entry[3]](entry[1], entry[2])
            for entry in outputs
        ],
        in_specs=[pl.BlockSpec(memory_space=pltpu.SMEM)]
        + [pl.BlockSpec(memory_space=place[kind]) for _, _, kind in inputs],
        out_specs=[
            pl.BlockSpec() if entry[3] == "b" else pl.BlockSpec(memory_space=place[entry[3]]) for entry in outputs
        ],
        scratch_shapes=[shape for _, shape in scratch],
        input_output_aliases=aliases,
        compiler_params=pltpu.CompilerParams(vmem_limit_bytes=limit * 1024 * 1024),
        cost_estimate=pl.CostEstimate(flops=int(micros * 1.15e9), bytes_accessed=0, transcendentals=0),
    )(info.table, *arrays)
    return {entry[0]: result for entry, result in zip(outputs, results)}


def copy(source, target, sem):
    return pltpu.make_async_copy(source, target, sem)


def after_inputs(after):
    return [(f"after{k}", array, "a") for k, array in enumerate(after)]


class Graph:
    def __init__(self, rows_n, rows_e, blocks, width):
        self.rows_n, self.rows_e, self.blocks, self.width = rows_n, rows_e, blocks, width
        self.cap = rows_e // blocks
        self.chunk = min(CHUNK, rows_e)
        self.starts = range(0, rows_e, self.chunk)
        self.consts = {}
        self.extra = max(blocks - 8, 0) * rows_n * width * 2 >> 20

    def const_inputs(self):
        return [(name, array, "v") for name, array in self.consts.items()]

    def weight_row(self, section_id, part):
        return (section_id * 3 + part) * self.width

    def weight(self, R, section_id, part, count=1):
        return R["wall"][pl.ds(self.weight_row(section_id, part), count * self.width), :]

    def recv_weight(self, R, layer):
        return R["wall"][pl.ds((12 + layer) * self.width, self.width), :]

    def vectors(self, R, section_id):
        block = R["wall"][pl.ds(14 * self.width + section_id * VEC_ROWS, VEC_ROWS), :].astype(F32)
        return [block[k : k + 1] + block[4 + k : 5 + k] for k in range(4)]


OWN, OTHER, OUT = 0, 1, 2


def half_rows(width):
    half, eighth = width // 2, width // 8
    return half, eighth, 3 * half + 2 * eighth, 3 * half + 2 * eighth + VEC_ROWS


def half_kernel(graph, info, own, other, out, recv, vec):
    half, eighth, vec_row, rows = half_rows(graph.width)
    quarter = 2 * eighth

    def body(R):
        core, sem, stage = R["info"][1], R["sem"], R["stage"]
        for k, name in enumerate(("own", "other", "out")):
            source = R[name].at[pl.ds(pl.multiple_of(core * half, half), half)]
            copy(source, stage.at[pl.ds(k * half, half)], sem).start()
        for layer in range(2):
            source = R["recv"].at[pl.ds(pl.multiple_of(layer * quarter + core * eighth, eighth), eighth)]
            copy(source, stage.at[pl.ds(3 * half + layer * eighth, eighth)], sem).start()
        copy(R["vec"], stage.at[pl.ds(vec_row, VEC_ROWS)], sem).start()
        copy(stage, stage, sem).wait()
        move = copy(stage, R["half"], sem)
        move.start()
        move.wait()

    inputs = [(name, array, "h") for name, array in zip(("own", "other", "out", "recv", "vec"), (own, other, out, recv, vec))]
    outputs = [("half", (rows, graph.width), BF, "a", None)]
    scratch = [("stage", VMEM((rows, graph.width), BF)), ("sem", pltpu.SemaphoreType.DMA)]
    return run_kernel(body, info, inputs, outputs, scratch, 1, 2)["half"]


def wall_kernel(graph, info, own, other, out, recv, vec, near, far):
    width = graph.width
    half, eighth, vec_row, rows = half_rows(width)
    quarter = 2 * eighth
    mine = [("own", own), ("other", other), ("out", out), ("recv", recv), ("vec", vec)]
    inputs = [(name, array, "h") for name, array in mine] + [("far", far, "a")]
    inputs += [(f"near{rel}_{k}", piece[0], "a") for rel, pieces in near.items() for k, piece in enumerate(pieces)]
    total = 14 * width + 4 * VEC_ROWS

    def body(R):
        section, core = R["info"][0], R["info"][1]
        wall, sem = R["wall"], R["sem"]

        def put(source, row, count, unit):
            copy(source, wall.at[pl.ds(pl.multiple_of(row, unit), count)], sem).start()

        for k, (name, _) in enumerate(mine[:3]):
            put(R[name], section * 3 * width + k * width, width, width)
        for layer in range(2):
            put(R["recv"].at[pl.ds(layer * quarter, quarter)], (12 + layer) * width + section * quarter, quarter, quarter)
        put(R["vec"], 14 * width + section * VEC_ROWS, VEC_ROWS, VEC_ROWS)
        for rel in range(1, 4):
            there = section ^ rel
            for side in (core, 1 - core):
                parts = [(k * half, half, (there * 3 + k) * width + side * half, half) for k in range(3)]
                parts += [
                    (3 * half + layer * eighth, eighth, (12 + layer) * width + there * quarter + side * eighth, eighth)
                    for layer in range(2)
                ]
                if side is core:
                    parts.append((vec_row, VEC_ROWS, 14 * width + there * VEC_ROWS, VEC_ROWS))
                for row, count, target, unit in parts:
                    if side is not core:
                        put(R["far"].at[pl.ds((rel - 1) * rows + row, count)], target, count, unit)
                        continue
                    first = 0
                    for k, (_, begin, held) in enumerate(near[rel]):
                        low, high = max(row, first), min(row + count, first + held)
                        if low < high:
                            source = R[f"near{rel}_{k}"].at[pl.ds(begin + low - first, high - low)]
                            put(source, target + low - row, high - low, 16)
                        first += held
        copy(wall, wall, sem).wait()

    outputs = [("wall", (total, width), BF, "v", None)]
    return run_kernel(body, info, inputs, outputs, [("sem", pltpu.SemaphoreType.DMA)], 3, 1)["wall"]


def glue_kernel(graph, info, sources, plan, rows, after=()):
    width = graph.width
    inputs = [(f"in{k}", array, "h" if array.ndim > 2 else "a") for k, array in enumerate(sources)]
    inputs += after_inputs(after)
    outputs = [(f"out{k}", (count, width), BF, "a", None) for k, count in enumerate(rows)]
    scratch = [(f"stage{k}", VMEM((count, width), BF)) for k, count in enumerate(rows)]
    scratch.append(("sem", pltpu.SemaphoreType.DMA((len(rows),))))

    def body(R):
        for source, index, row, count, target, place in plan:
            ref = R[f"in{source}"] if index is None else R[f"in{source}"].at[R["info"][0] ^ index]
            copy(ref.at[pl.ds(row, count)], R[f"stage{target}"].at[pl.ds(place, count)], R["sem"].at[target]).start()
        moves = []
        for k in range(len(rows)):
            stage = R[f"stage{k}"]
            copy(stage, stage, R["sem"].at[k]).wait()
            moves.append(copy(stage, R[f"out{k}"], R["sem"].at[k]))
            moves[-1].start()
        for move in moves:
            move.wait()

    results = run_kernel(body, info, inputs, outputs, scratch, 2, 4)
    return [results[f"out{k}"] for k in range(len(rows))]


def add_kernel(graph, info, arrays, rows, after=()):
    count, width = arrays[0].shape
    inputs = [(f"in{k}", array, "a") for k, array in enumerate(arrays)] + after_inputs(after)
    outputs = [(f"out{k}", (rows, width), BF, "a", None) for k in range(count // rows)]
    scratch = [(f"stage{k}", VMEM((count, width), BF)) for k in range(len(arrays))]
    scratch.append(("sem", pltpu.SemaphoreType.DMA((len(arrays),))))

    def body(R):
        moves = [copy(R[f"in{k}"], R[f"stage{k}"], R["sem"].at[k]) for k in range(len(arrays))]
        for move in moves:
            move.start()
        for move in moves:
            move.wait()
        moves = []
        for k in range(count // rows):
            here = pl.ds(k * rows, rows)
            total = R["stage0"][here, :].astype(F32)
            for other in range(1, len(arrays)):
                total = total + R[f"stage{other}"][here, :].astype(F32)
            R["stage0"][here, :] = total.astype(BF)
            moves.append(copy(R["stage0"].at[here], R[f"out{k}"], R["sem"].at[0]))
            moves[-1].start()
        for move in moves:
            move.wait()

    results = run_kernel(body, info, inputs, outputs, scratch, 2, 6)
    return [results[f"out{k}"] for k in range(count // rows)]


def node_zero_kernel(graph, info, parts, sums, node_grad, wall):
    rows_n, width = graph.rows_n, graph.width
    inputs = [(f"part{k}", array, "a") for k, array in enumerate(parts)]
    inputs += [(f"sum{k}", array, "a") for k, array in enumerate(sums)]
    inputs += [("old", node_grad, "h"), ("wall", wall, "v")]
    outputs = [("node_grad", node_grad.shape, BF, "h", "old")]
    scratch = [
        ("part", VMEM((4 * rows_n, width), F32)),
        ("sum", VMEM((4 * rows_n, width), BF)),
        ("total", VMEM((4, rows_n, width), BF)),
        ("sem", pltpu.SemaphoreType.DMA((3,))),
    ]

    def body(R):
        @pl.when(R["info"][0] == 0)
        def _():
            for k in range(4):
                here = pl.ds(k * rows_n, rows_n)
                copy(R[f"part{k}"], R["part"].at[here], R["sem"].at[0]).start()
                copy(R[f"sum{k}"], R["sum"].at[here], R["sem"].at[1]).start()
            copy(R["part"], R["part"], R["sem"].at[0]).wait()
            copy(R["sum"], R["sum"], R["sem"].at[1]).wait()
            total = R["part"][...] + dot_nt(R["sum"][...], graph.weight(R, 0, OTHER))
            R["total"][...] = total.astype(BF).reshape(4, rows_n, width)
            move = copy(R["total"], R["node_grad"], R["sem"].at[2])
            move.start()
            move.wait()

    return run_kernel(body, info, inputs, outputs, scratch, 2, 6)["node_grad"]


def const_kernel(graph, info, arrays):
    inputs = [(f"{name}_in", array, "h") for name, array in arrays.items()]
    outputs = [(name, array.shape, array.dtype, "v", None) for name, array in arrays.items()]

    def body(R):
        moves = [copy(R[f"{name}_in"], R[name], R["sem"].at[k]) for k, name in enumerate(arrays)]
        for move in moves:
            move.start()
        for move in moves:
            move.wait()

    return run_kernel(body, info, inputs, outputs, [("sem", pltpu.SemaphoreType.DMA((len(arrays),)))], 2, 1)


def block_inputs(blocks):
    return [(f"block{k}", array, "h" if index == "micro" else "a") for k, (array, index, _, _) in enumerate(blocks)]


def block_copies(graph, R, blocks, sem):
    moves = []
    place = 0
    for k, (_, index, row, rows) in enumerate(blocks):
        source = R[f"block{k}"]
        if index is not None:
            source = source.at[R["info"][2] if index == "micro" else index]
        if rows == graph.rows_n:
            start = pl.multiple_of(R["info"][3 + place] * graph.rows_n, graph.rows_n)
        else:
            start = 0
        moves.append(copy(source.at[pl.ds(row, rows)], R["hall"].at[pl.ds(start, rows)], sem))
        place += rows // graph.rows_n
    return moves


def bucket_rows(graph, start):
    for bucket in range(start // graph.cap, (start + graph.chunk) // graph.cap):
        yield pl.ds(bucket * graph.cap, graph.cap), pl.ds(bucket * graph.rows_n, graph.rows_n)


def stack(pieces):
    return jnp.concatenate(pieces, axis=0) if len(pieces) > 1 else pieces[0]


def stat_pair(square, stream, mask):
    branch = col_sum(mask * square)
    total = col_sum(mask * jnp.sum(stream * stream, axis=-1, keepdims=True))
    return branch, total


def put_stats(stat, pairs, width):
    branch, total = pairs[0]
    for pair in pairs[1:]:
        branch, total = branch + pair[0], total + pair[1]
    stat[0:1, :] = jnp.broadcast_to(branch * width, (1, LANES))
    stat[1:2, :] = jnp.broadcast_to(total, (1, LANES))


def first_kernel(graph, info, edge_in, node_in, blocks, after):
    rows_e, rows_n, width = graph.rows_e, graph.rows_n, graph.width
    inputs = [("edges", edge_in, "h"), ("nodes", node_in, "h")] + block_inputs(blocks) + graph.const_inputs()
    inputs += after_inputs(after)
    outputs = [
        ("edge1", (rows_e, width), BF, "v", None),
        ("z0", (rows_e, width), BF, "v", None),
        ("x0", (rows_e, width), BF, "v", None),
        ("q0", (rows_e, LANES), F32, "v", None),
        ("s0", (rows_e, width), BF, "v", None),
        ("node0", (rows_n, width), BF, "v", None),
        ("node1", (rows_n, width), BF, "v", None),
        ("g1", (rows_n, width), BF, "v", None),
        ("z1", (rows_n, width), BF, "v", None),
        ("x1", (rows_n, width), BF, "v", None),
        ("q1", (rows_n, LANES), F32, "v", None),
        ("stat", (8, LANES), F32, "v", None),
        ("t2", (rows_n, width), BF, "a", None),
    ]
    scratch = [
        ("edge", VMEM((rows_e, width), BF)),
        ("hall", VMEM((graph.blocks * rows_n, width), BF)),
        ("t2_here", VMEM((rows_n, width), BF)),
        ("sem", pltpu.SemaphoreType.DMA((4,))),
    ]

    def body(R):
        info = R["info"]
        section, micro = info[0], info[2]
        node_copy = copy(R["nodes"].at[micro], R["node0"], R["sem"].at[0])
        hall_copies = block_copies(graph, R, blocks, R["sem"].at[1])
        edge_copy = copy(R["edges"].at[micro], R["edge"], R["sem"].at[2])
        node_copy.start()
        for move in hall_copies:
            move.start()
        edge_copy.start()
        node_copy.wait()
        node = R["node0"][...]
        recv_node = dot(node, graph.recv_weight(R, 0)).astype(BF)
        copy(R["hall"], R["hall"], R["sem"].at[1]).wait()
        edge_copy.wait()
        vecs = graph.vectors(R, 0)
        pairs = []
        for start in graph.starts:
            rows = pl.ds(start, graph.chunk)
            mask = R["emask"][rows, :]
            edge = R["edge"][rows, :]
            send = stack([dot(R["ohs"][e, :], R["hall"][n, :]).astype(BF) for e, n in bucket_rows(graph, start)])
            R["s0"][rows, :] = send
            pre_act = dot(jnp.concatenate([edge, send], axis=1), graph.weight(R, 0, OWN, 2))
            pre_act = pre_act + dot(R["ohr"][rows, :], recv_node) + vecs[0]
            hidden, scaled, inverse, square, normed = tail(pre_act, graph.weight(R, 0, OUT), vecs)
            stream = edge.astype(F32) + widen(mask, width) * normed
            R["edge1"][rows, :] = stream.astype(BF)
            R["z0"][rows, :] = pre_act.astype(BF)
            R["x0"][rows, :] = scaled.astype(BF)
            R["q0"][rows, :] = jnp.broadcast_to(inverse, (graph.chunk, LANES))
            pairs.append(stat_pair(square, stream, mask[:, :1]))
        summed = dot(R["ohrt"][...], R["edge1"][...]).astype(BF)
        R["g1"][...] = summed
        vecs = graph.vectors(R, 1)
        pre_act = dot(jnp.concatenate([node, summed], axis=1), graph.weight(R, 1, OWN, 2)) + vecs[0]
        hidden, scaled, inverse, square, normed = tail(pre_act, graph.weight(R, 1, OUT), vecs)
        nmask = R["nmask"][...]
        stream = node.astype(F32) + widen(nmask, width) * normed
        low = stream.astype(BF)
        R["t2_here"][...] = dot(low, graph.weight(R, 2, OTHER)).astype(BF)
        out_copy = copy(R["t2_here"], R["t2"], R["sem"].at[3])
        out_copy.start()
        R["node1"][...] = low
        R["z1"][...] = pre_act.astype(BF)
        R["x1"][...] = scaled.astype(BF)
        R["q1"][...] = jnp.broadcast_to(inverse, (rows_n, LANES))

        @pl.when(section == 0)
        def _():
            put_stats(R["stat"], pairs, width)

        @pl.when(section != 0)
        def _():
            put_stats(R["stat"], [stat_pair(square, stream, nmask[:, :1])], width)

        out_copy.wait()

    return run_kernel(body, info, inputs, outputs, scratch, 8, 10 + graph.extra)


def sender_outputs(graph, direct):
    rows = graph.blocks * graph.rows_n
    if direct:
        rows //= 2
        return [(name, (rows, graph.width), BF, "a", None) for name in ("gs_mine", "gs_far")]
    return [("gs_mine", (rows, graph.width), BF, "a", None)]


def sender_sums(graph, R, grads, stage, sem):
    for place in range(graph.blocks):
        bucket = R["info"][3 + place]
        rows = pl.ds(pl.multiple_of(bucket * graph.cap, graph.cap), graph.cap)
        here = pl.ds(place * graph.rows_n, graph.rows_n)
        stage[here, :] = dot_tn(R["ohs"][rows, :], grads[rows, :]).astype(BF)
    for name in ("gs_far", "gs_mine"):
        if name in R:
            rows = R[name].shape[0]
            start = stage.shape[0] - rows if name == "gs_far" else 0
            copy(stage.at[pl.ds(start, rows)], R[name], sem).start()
    copy(stage, stage, sem).wait()


def add_recv(graph, R, layer, node, grad_recv):
    quarter = graph.width // 4
    start = pl.multiple_of(R["info"][0] * quarter, quarter)
    rows = pl.ds(3 * graph.width + layer * quarter, quarter)
    R["wg"][rows, :] += dot_tn(node[:, pl.ds(start, quarter)], grad_recv)


def second_kernel(graph, info, first, blocks, node_cot, edge_cot, before, own_first, direct, after):
    rows_e, rows_n, width = graph.rows_e, graph.rows_n, graph.width
    micro_count = node_cot.shape[0]
    inputs = [(name, first[name], "v") for name in ("edge1", "node0", "node1")]
    inputs += [("edge_cot", edge_cot, "h"), ("node_cot", node_cot, "h")] + block_inputs(blocks) + graph.const_inputs()
    inputs += after_inputs(after)
    if before is not None:
        inputs += [("old_edge", before["edge_out"], "h"), ("old_node", before["node_out"], "h")]
        inputs += [("old_grad", before["edge_grad"], "h")]
        inputs += [("old_wg", before["wg"], "v"), ("old_vec", before["vec"], "v")]

    def chain(name):
        return None if before is None else name

    outputs = [
        ("edge_out", (micro_count, rows_e, width), BF, "h", chain("old_edge")),
        ("node_out", (micro_count, rows_n, width), BF, "h", chain("old_node")),
        ("wg", (3 * width + width // 2, width), F32, "v", chain("old_wg")),
        ("vec", (8, width), F32, "v", chain("old_vec")),
        ("edge_grad", (micro_count, rows_e, width), BF, "h", chain("old_grad")),
        ("eg2", (rows_e, width), BF, "v", None),
        ("ng", (rows_n, width), BF, "v", None),
        ("gr", (rows_n, width), BF, "v", None),
        ("stat", (8, LANES), F32, "v", None),
    ]
    if own_first:
        outputs += sender_outputs(graph, direct)
    scratch = [
        ("hall", VMEM((graph.blocks * rows_n, width), BF)),
        ("cot", VMEM((rows_e, width), BF)),
        ("ncot", VMEM((rows_n, width), BF)),
        ("edge2", VMEM((rows_e, width), BF)),
        ("eg", VMEM((rows_e, width), BF)),
        ("node_here", VMEM((rows_n, width), BF)),
        ("z", VMEM((rows_e, width), BF)),
        ("x", VMEM((rows_e, width), BF)),
        ("q", VMEM((rows_e, LANES), F32)),
        ("a", VMEM((rows_e, width), BF)),
        ("gu", VMEM((rows_e, width), BF)),
        ("gz", VMEM((rows_e, width), BF)),
        ("sem", pltpu.SemaphoreType.DMA((8,))),
    ]

    def body(R):
        info = R["info"]
        section, micro = info[0], info[2]
        sem = R["sem"]
        hall_copies = block_copies(graph, R, blocks, sem.at[0])
        cot_copy = copy(R["edge_cot"].at[micro], R["cot"], sem.at[1])
        ncot_copy = copy(R["node_cot"].at[micro], R["ncot"], sem.at[2])
        for move in hall_copies:
            move.start()
        ncot_copy.start()
        cot_copy.start()
        if own_first:
            R["wg"][...] = jnp.zeros_like(R["wg"])
            R["vec"][...] = jnp.zeros_like(R["vec"])
        node = R["node1"][...]
        recv_node = dot(node, graph.recv_weight(R, 1)).astype(BF)
        copy(R["hall"], R["hall"], sem.at[0]).wait()
        vecs = graph.vectors(R, 2)
        pairs = []
        for start in graph.starts:
            rows = pl.ds(start, graph.chunk)
            mask = R["emask"][rows, :]
            edge = R["edge1"][rows, :]
            ends = stack(
                [
                    dot(
                        jnp.concatenate([R["ohs"][e, :], R["ohr"][e, :]], axis=1),
                        jnp.concatenate([R["hall"][n, :], recv_node], axis=0),
                    )
                    for e, n in bucket_rows(graph, start)
                ]
            )
            pre_act = dot(edge, graph.weight(R, 2, OWN)) + ends + vecs[0]
            hidden, scaled, inverse, square, normed = tail(pre_act, graph.weight(R, 2, OUT), vecs)
            stream = edge.astype(F32) + widen(mask, width) * normed
            R["edge2"][rows, :] = stream.astype(BF)
            R["z"][rows, :] = pre_act.astype(BF)
            R["x"][rows, :] = scaled.astype(BF)
            R["q"][rows, :] = jnp.broadcast_to(inverse, (graph.chunk, LANES))
            R["a"][rows, :] = hidden
            pairs.append(stat_pair(square, stream, mask[:, :1]))

        @pl.when(section >= 2)
        def _():
            copy(R["edge2"], R["edge_out"].at[micro], sem.at[3]).start()

        @pl.when(section < 2)
        def _():
            copy(R["edge1"], R["edge_out"].at[micro], sem.at[3]).start()

        vecs = graph.vectors(R, 3)
        summed = dot(R["ohrt"][...], R["edge2"][...]).astype(BF)
        weight_out = graph.weight(R, 3, OUT)
        pre_act = dot(jnp.concatenate([node, summed], axis=1), graph.weight(R, 3, OWN, 2)) + vecs[0]
        hidden, scaled, inverse, square, normed = tail(pre_act, weight_out, vecs)
        nmask = R["nmask"][...]
        wide_mask = widen(nmask, width)
        stream = node.astype(F32) + wide_mask * normed
        R["node_here"][...] = jnp.where(
            section == 0, R["node0"][...], jnp.where(section == 3, stream.astype(BF), node)
        )
        node_copy = copy(R["node_here"], R["node_out"].at[micro], sem.at[4])
        node_copy.start()

        @pl.when(section == 3)
        def _():
            put_stats(R["stat"], [stat_pair(square, stream, nmask[:, :1])], width)

        @pl.when(section != 3)
        def _():
            put_stats(R["stat"], pairs, width)

        ncot_copy.wait()
        grad = R["ncot"][...].astype(F32)
        grad_normed = wide_mask * grad
        grad_update = norm_back(grad_normed, scaled, inverse, vecs[2])
        grad_low = grad_update.astype(BF)
        grad_pre, _ = silu_back(dot_nt(grad_low, weight_out), pre_act)
        pre_low = grad_pre.astype(BF)
        R["ng"][...] = (grad + dot_nt(pre_low, graph.weight(R, 3, OWN))).astype(BF)
        grad_sum = dot_nt(pre_low, graph.weight(R, 3, OTHER))
        grad_high = grad_sum.astype(BF)
        grad_both = jnp.concatenate([grad_high, (grad_sum - grad_high.astype(F32)).astype(BF)], axis=0)

        @pl.when(section == 3)
        def _():
            R["wg"][0:width, :] += dot_tn(node, pre_low)
            R["wg"][width : 2 * width, :] += dot_tn(summed, pre_low)
            R["wg"][2 * width : 3 * width, :] += dot_tn(hidden, grad_low)
            R["vec"][0:1, :] += col_sum(grad_pre)
            R["vec"][1:2, :] += col_sum(grad_update)
            R["vec"][2:3, :] += col_sum(grad_normed * scaled)
            R["vec"][3:4, :] += col_sum(grad_normed)

        cot_copy.wait()
        vecs = graph.vectors(R, 2)

        def arriving(rows, mask):
            onehot = R["ohr"][rows, :]
            spread = dot(jnp.concatenate([onehot, onehot], axis=1), grad_both)
            return (R["cot"][rows, :].astype(F32) + mask * spread).astype(BF)

        def edge_back(sums):
            totals = [jnp.zeros((1, width), F32)] * 4
            for start in graph.starts:
                rows = pl.ds(start, graph.chunk)
                mask = R["emask"][rows, :]
                low = arriving(rows, widen(mask, width))
                R["eg"][rows, :] = low
                wide = low.astype(F32)
                scaled = R["x"][rows, :].astype(F32)
                pre_act = R["z"][rows, :].astype(F32)
                inverse = widen(R["q"][rows, :] * mask, width)
                grad_update = norm_back(wide, scaled, inverse, vecs[2])
                grad_low = grad_update.astype(BF)
                grad_pre, _ = silu_back(dot_nt(grad_low, graph.weight(R, 2, OUT)), pre_act)
                pre_low = grad_pre.astype(BF)
                R["gz"][rows, :] = pre_low
                R["eg2"][rows, :] = (wide + dot_nt(pre_low, graph.weight(R, 2, OWN))).astype(BF)
                if sums:
                    R["gu"][rows, :] = grad_low
                    normed = widen(mask, width) * wide
                    parts = (grad_pre, grad_update, normed * scaled, normed)
                    totals = [total + col_sum(part) for total, part in zip(totals, parts)]
            if sums:
                R["wg"][0:width, :] += dot_tn(R["edge1"][...], R["gz"][...])
                R["wg"][2 * width : 3 * width, :] += dot_tn(R["a"][...], R["gu"][...])
                for k in range(4):
                    R["vec"][k : k + 1, :] += totals[k]

        @pl.when(section == 2)
        def _():
            edge_back(True)

        @pl.when(section != 2)
        def _():
            edge_back(False)

        @pl.when(section == 2)
        def _():
            copy(R["eg2"], R["edge_grad"].at[micro], sem.at[6]).start()

        @pl.when(section == 3)
        def _():
            copy(R["eg"], R["edge_grad"].at[micro], sem.at[6]).start()

        grad_recv = dot(R["ohrt"][...], R["gz"][...]).astype(BF)
        R["gr"][...] = grad_recv
        add_recv(graph, R, 1, R["node1"], grad_recv)
        if own_first:
            sender_sums(graph, R, R["gz"], R["hall"], sem.at[5])
        node_copy.wait()
        copy(R["edge2"], R["edge_out"].at[micro], sem.at[3]).wait()

        @pl.when(section >= 2)
        def _():
            copy(R["eg"], R["edge_grad"].at[micro], sem.at[6]).wait()

    return run_kernel(body, info, inputs, outputs, scratch, 14, 15 + graph.extra)


def third_kernel(graph, info, first, second, sums, edge_in, micro_count, before, edge_grad, wg, vec, own_first, direct, after):
    rows_e, rows_n, width = graph.rows_e, graph.rows_n, graph.width
    inputs = [(name, second[name], "v") for name in ("eg2", "ng", "gr")]
    inputs += [(name, first[name], "v") for name in ("z0", "x0", "q0", "s0", "node0", "node1", "g1", "z1", "x1", "q1")]
    inputs += [("sums", sums, "a"), ("edges", edge_in, "h"), ("old_wg", wg, "v"), ("old_vec", vec, "v")]
    inputs += graph.const_inputs()
    inputs += after_inputs(after) + [("old_edge", edge_grad, "h")]
    if before is not None:
        inputs += [("old_node", before["node_grad"], "h")]

    def chain(name):
        return None if before is None else name

    outputs = [
        ("edge_grad", edge_grad.shape, BF, "h", "old_edge"),
        ("node_grad", (micro_count, rows_n, width), BF, "h", chain("old_node")),
        ("wg", wg.shape, F32, "v", "old_wg"),
        ("vec", (8, width), F32, "v", "old_vec"),
        ("node_part", (rows_n, width), F32, "a", None),
        ("token", (8, LANES), F32, "v", None),
    ]
    if own_first:
        outputs += sender_outputs(graph, direct)
    scratch = [
        ("edge", VMEM((rows_e, width), BF)),
        ("sum2", VMEM((rows_n, width), BF)),
        ("out_edge", VMEM((rows_e, width), BF)),
        ("out_node", VMEM((rows_n, width), BF)),
        ("gu", VMEM((rows_e, width), BF)),
        ("a", VMEM((rows_e, width), BF)),
        ("gz", VMEM((rows_e, width), BF)),
        ("part", VMEM((rows_n, width), F32)),
        ("sem", pltpu.SemaphoreType.DMA((6,))),
    ]
    if own_first:
        scratch.append(("stage", VMEM((graph.blocks * rows_n, width), BF)))

    def body(R):
        info = R["info"]
        section, micro = info[0], info[2]
        sem = R["sem"]
        R["token"][...] = jnp.zeros_like(R["token"])
        sums_copy = copy(R["sums"], R["sum2"], sem.at[0])
        sums_copy.start()
        edge_copy = copy(R["edges"].at[micro], R["edge"], sem.at[1])

        @pl.when(section == 0)
        def _():
            edge_copy.start()

        sums_copy.wait()
        gs2 = R["sum2"][...]
        grad_mid = (
            R["ng"][...].astype(F32) + dot_nt(R["gr"][...], graph.recv_weight(R, 1)) + dot_nt(gs2, graph.weight(R, 2, OTHER))
        ).astype(BF)
        R["out_node"][...] = jnp.where(section == 3, R["ng"][...], grad_mid)

        @pl.when(section == 2)
        def _():
            R["wg"][width : 2 * width, :] += dot_tn(R["node1"][...], gs2)

        vecs = graph.vectors(R, 1)
        wide = grad_mid.astype(F32)
        grad_normed = widen(R["nmask"][...], width) * wide
        scaled = R["x1"][...].astype(F32)
        pre_act = R["z1"][...].astype(F32)
        grad_update = norm_back(grad_normed, scaled, widen(R["q1"][...], width), vecs[2])
        grad_low = grad_update.astype(BF)
        grad_pre, sig = silu_back(dot_nt(grad_low, graph.weight(R, 1, OUT)), pre_act)
        pre_low = grad_pre.astype(BF)
        grad_node = (wide + dot_nt(pre_low, graph.weight(R, 1, OWN))).astype(BF)
        grad_sum = dot_nt(pre_low, graph.weight(R, 1, OTHER))
        grad_high = grad_sum.astype(BF)
        grad_both = jnp.concatenate([grad_high, (grad_sum - grad_high.astype(F32)).astype(BF)], axis=0)

        @pl.when(section == 1)
        def _():
            R["out_node"][...] = grad_node
            R["wg"][0:width, :] += dot_tn(R["node0"][...], pre_low)
            R["wg"][width : 2 * width, :] += dot_tn(R["g1"][...], pre_low)
            R["wg"][2 * width : 3 * width, :] += dot_tn((pre_act * sig).astype(BF), grad_low)
            R["vec"][0:1, :] += col_sum(grad_pre)
            R["vec"][1:2, :] += col_sum(grad_update)
            R["vec"][2:3, :] += col_sum(grad_normed * scaled)
            R["vec"][3:4, :] += col_sum(grad_normed)

        vecs = graph.vectors(R, 0)

        def arriving(rows, mask):
            onehot = R["ohr"][rows, :]
            spread = dot(jnp.concatenate([onehot, onehot], axis=1), grad_both)
            return (R["eg2"][rows, :].astype(F32) + mask * spread).astype(BF)

        def edge_back(sums):
            totals = [jnp.zeros((1, width), F32)] * 4
            for start in graph.starts:
                rows = pl.ds(start, graph.chunk)
                mask = R["emask"][rows, :]
                wide = arriving(rows, widen(mask, width)).astype(F32)
                scaled = R["x0"][rows, :].astype(F32)
                pre_act = R["z0"][rows, :].astype(F32)
                inverse = widen(R["q0"][rows, :] * mask, width)
                grad_update = norm_back(wide, scaled, inverse, vecs[2])
                grad_low = grad_update.astype(BF)
                grad_pre, sig = silu_back(dot_nt(grad_low, graph.weight(R, 0, OUT)), pre_act)
                pre_low = grad_pre.astype(BF)
                R["gz"][rows, :] = pre_low
                if sums:
                    R["out_edge"][rows, :] = (wide + dot_nt(pre_low, graph.weight(R, 0, OWN))).astype(BF)
                    R["gu"][rows, :] = grad_low
                    R["a"][rows, :] = (pre_act * sig).astype(BF)
                    normed = widen(mask, width) * wide
                    parts = (grad_pre, grad_update, normed * scaled, normed)
                    totals = [total + col_sum(part) for total, part in zip(totals, parts)]
            return totals

        @pl.when(section == 0)
        def _():
            totals = edge_back(True)
            copy(R["out_edge"], R["edge_grad"].at[micro], sem.at[2]).start()
            edge_copy.wait()
            R["wg"][0:width, :] += dot_tn(R["edge"][...], R["gz"][...])
            R["wg"][width : 2 * width, :] += dot_tn(R["s0"][...], R["gz"][...])
            R["wg"][2 * width : 3 * width, :] += dot_tn(R["a"][...], R["gu"][...])
            for k in range(4):
                R["vec"][k : k + 1, :] += totals[k]

        @pl.when(section == 1)
        def _():
            for start in graph.starts:
                rows = pl.ds(start, graph.chunk)
                R["out_edge"][rows, :] = arriving(rows, widen(R["emask"][rows, :], width))
            copy(R["out_edge"], R["edge_grad"].at[micro], sem.at[2]).start()

        @pl.when(section > 0)
        def _():
            edge_back(False)

        grad_recv = dot(R["ohrt"][...], R["gz"][...]).astype(BF)
        add_recv(graph, R, 0, R["node0"], grad_recv)

        @pl.when(section == 0)
        def _():
            R["part"][...] = grad_node.astype(F32) + dot_nt(grad_recv, graph.recv_weight(R, 0))

        node_copy = copy(R["out_node"], R["node_grad"].at[micro], sem.at[3])
        node_copy.start()
        part_copy = copy(R["part"], R["node_part"], sem.at[5])
        part_copy.start()
        if own_first:
            sender_sums(graph, R, R["gz"], R["stage"], sem.at[4])
        node_copy.wait()
        part_copy.wait()

        @pl.when(section < 2)
        def _():
            copy(R["out_edge"], R["edge_grad"].at[micro], sem.at[2]).wait()

    return run_kernel(body, info, inputs, outputs, scratch, 10, 13 + graph.extra)


PIECES = 8
TAIL_ROWS = 16


def stats_block(graph, R, firsts, seconds):
    section = R["info"][0]
    edge_count = col_sum(R["emask"][...])
    node_count = col_sum(R["nmask"][...])
    even = (section & 1) == 0
    valid = jnp.where(even, edge_count, node_count)
    rows = [R["vec"][0:4, :]]
    for k in range(4):
        pair = jnp.where(section < 2, R[f"first{k}"][0:2, :], R[f"second{k}"][0:2, :])
        rows.append(jnp.concatenate([pair[0:1], pair[1:2], valid, jnp.zeros_like(valid)], axis=1))
    rows.append(jnp.zeros((TAIL_ROWS - 8, graph.width), F32))
    return jnp.concatenate(rows, axis=0)


def pack_kernel(graph, info, wg, vec, stats, direct):
    width = graph.width
    held = wg.shape[0]
    piece = -(-(held + TAIL_ROWS) // (16 * PIECES)) * 16
    inputs = [("wg", wg, "v"), ("vec", vec, "v"), ("emask", graph.consts["emask"], "v"), ("nmask", graph.consts["nmask"], "v")]
    for k in range(4):
        inputs += [(f"first{k}", stats[0][k], "v"), (f"second{k}", stats[1][k], "v")]
    low = BF if direct else F32
    if direct:
        outputs = [("mine", (4 * piece, width), BF, "a", None), ("other", (4 * piece, width), BF, "a", None)]
    else:
        outputs = [("flat", (PIECES * piece, width), F32, "h", None)]
    scratch = [
        ("stage", VMEM((PIECES * piece, width), low)),
        ("sem", pltpu.SemaphoreType.DMA),
    ]

    def body(R):
        info, sem = R["info"], R["sem"]
        core = info[1]
        R["stage"][0:held, :] = R["wg"][...].astype(low)
        R["stage"][held : held + TAIL_ROWS, :] = stats_block(graph, R, *stats).astype(low)
        rest = PIECES * piece - held - TAIL_ROWS
        if rest:
            R["stage"][held + TAIL_ROWS :, :] = jnp.zeros((rest, width), low)
        if direct:
            for name, side in (("other", 1 - core), ("mine", core)):
                for r in range(4):
                    line = lax.shift_right_logical(info[3 + r], 1)
                    start = pl.multiple_of((side * 4 + line) * piece, 16)
                    copy(R["stage"].at[pl.ds(start, piece)], R[name].at[pl.ds(r * piece, piece)], sem).start()
        else:
            copy(R["stage"], R["flat"], sem).start()
        copy(R["stage"], R["stage"], sem).wait()

    return run_kernel(body, info, inputs, outputs, scratch, 3, 8), piece


def unpack_kernel(graph, info, mine, far, piece):
    width = graph.width
    quarter = width // 4
    inputs = [(f"mine{r}", array, "a") for r, array in enumerate(mine)]
    inputs += [(f"far{r}", array, "a") for r, array in enumerate(far)]
    outputs = [
        ("own", (width, width), F32, "h", None),
        ("other", (width, width), F32, "h", None),
        ("out", (width, width), F32, "h", None),
        ("recv", (2 * quarter, width), F32, "h", None),
    ]
    outputs += [(f"vec{k}", (1, width), F32, "b", None) for k in range(4)]
    outputs += [(f"rms{k}", (1, 4), F32, "b", None) for k in range(2)]
    scratch = [
        ("stage", VMEM((PIECES * piece, width), BF)),
        ("wide", VMEM((3 * width, width), F32)),
        ("wide_recv", VMEM((2 * quarter, width), F32)),
        ("sem", pltpu.SemaphoreType.DMA((7,))),
    ]

    def body(R):
        info, sem = R["info"], R["sem"]
        core = info[1]
        for r in range(4):
            line = lax.shift_right_logical(info[3 + r], 1)
            for name, side in ((f"mine{r}", core), (f"far{r}", 1 - core)):
                start = pl.multiple_of((side * 4 + line) * piece, 16)
                copy(R[name], R["stage"].at[pl.ds(start, piece)], sem.at[0]).start()
        copy(R["stage"], R["stage"], sem.at[0]).wait()
        moves = []
        for k, name in enumerate(("own", "other", "out")):
            rows = pl.ds(k * width, width)
            R["wide"][rows, :] = R["stage"][rows, :].astype(F32)
            moves.append(copy(R["wide"].at[rows], R[name], sem.at[2 + k]))
            moves[-1].start()
        base = 3 * width + 2 * quarter
        sums = R["stage"][base : base + TAIL_ROWS, :].astype(F32)
        micro = lax.broadcasted_iota(jnp.int32, (1, 4), 1) ^ info[0]
        for k in range(4):
            R[f"vec{k}"][...] = sums[k : k + 1]
        for which in range(2):
            total = jnp.zeros((1, 4), F32)
            for k in range(4):
                row = sums[4 + k : 5 + k]
                square = row[:, which * LANES : which * LANES + 4] / (row[:, 2 * LANES : 2 * LANES + 4] * width)
                total = total + jnp.where(micro == k, jnp.sqrt(square), 0.0)
            R[f"rms{which}"][...] = total
        R["wide_recv"][...] = R["stage"][3 * width : base, :].astype(F32)
        moves.append(copy(R["wide_recv"], R["recv"], sem.at[6]))
        moves[-1].start()
        for move in moves:
            move.wait()

    return run_kernel(body, info, inputs, outputs, scratch, 3, 10)


def on_device(
    node_in,
    edge_in,
    node_cot,
    edge_cot,
    own_weight,
    other_weight,
    recv_weight,
    first_bias,
    out_weight,
    out_bias,
    norm_gain,
    norm_bias,
    senders,
    receivers,
    node_valid,
    edge_valid,
):
    micro_count, rows_n, width = node_in.shape
    rows_e = edge_in.shape[1]
    blocks = lax.axis_size("rows")
    section = lax.axis_index("section")
    row_pos = lax.axis_index("rows")
    core = row_pos % 2
    here = row_pos // 2
    graph = Graph(rows_n, rows_e, blocks, width)
    lines = blocks // 2
    direct = lines == 4
    quarter = width // 4

    def swap(value):
        return lax.ppermute(value, "rows", [(i, i ^ 1) for i in range(blocks)])

    def along(value, distance, flip=0):
        route = [(i, (i // 2 + distance) % lines * 2 + (i % 2 ^ flip)) for i in range(blocks)]
        return lax.ppermute(value, "rows", route)

    def across(value, rel):
        return lax.ppermute(value, "section", [(i, i ^ rel) for i in range(4)])

    if direct:
        places = [((here - r) % 4) * 2 + core for r in range(4)] + [((here - r) % 4) * 2 + 1 - core for r in range(4)]
    else:
        places = [jnp.int32(k) for k in range(blocks)]
    table = jnp.stack([jnp.stack([section, core, section ^ rel] + places) for rel in range(4)]).astype(jnp.int32)
    infos = [Info(table, rel) for rel in range(4)]

    vecs = jnp.concatenate([first_bias, out_bias, norm_gain, norm_bias], axis=0)
    vec_high = vecs.astype(BF)
    vec_low = (vecs - vec_high.astype(F32)).astype(BF)
    vec_rows = jnp.concatenate([vec_high, vec_low, vec_high, vec_low], axis=0)
    recv_rows = recv_weight.reshape(2 * quarter, width)
    def pick(array, rel):
        return lax.dynamic_index_in_dim(array, section ^ rel, 0, keepdims=False)

    def as_blocks(arrays, index):
        return [(array, index, 0, array.shape[-2]) for array in arrays]

    def lined_up(value):
        return [along(value, r) for r in range(1, 4)]

    half = half_kernel(graph, infos[0], own_weight[0], other_weight[0], out_weight[0], recv_rows, vec_rows)
    half_x, half_y = across(half, 1), across(half, 2)
    held = half.shape[0]
    cut = held // 32 * 16
    after = []
    if direct:
        own_nodes = pick(node_in, 0)
        own_lines = [own_nodes] + lined_up(own_nodes)
        plan = [(r, None, 0, rows_n, 0, r * rows_n) for r in range(4)]
        (own_cat,) = glue_kernel(graph, infos[0], own_lines, plan, [4 * rows_n])
        own_far = swap(own_cat)
        after = [own_cat]
    else:
        node_all = lax.all_gather(jnp.stack([pick(node_in, rel) for rel in range(4)]), "rows", axis=1, tiled=True)
    plan = [(0, None, 0, cut, 0, 0), (1, None, cut, held - cut, 1, 0)]
    send_da, send_db = glue_kernel(graph, infos[0], [half_x, half_y], plan, [cut, held - cut], after)
    half_da, half_db = across(send_da, 2), across(send_db, 1)
    plan = [(0, None, 0, held, 0, 0), (1, None, 0, held, 0, held)]
    plan += [(2, None, 0, cut, 0, 2 * held), (3, None, 0, held - cut, 0, 2 * held + cut)]
    sources = [half_x, half_y, half_da, half_db]
    rows = [3 * held]
    if direct:
        plan.append((4, None, rows_n, 3 * rows_n, 1, 0))
        sources.append(own_cat)
        rows.append(3 * rows_n)
    glued = glue_kernel(graph, infos[0], sources, plan, rows)
    far = swap(glued[0])
    if direct:
        own_shared = [across(glued[1], rel) for rel in range(1, 4)]
    near = {
        1: [(half_x, 0, held)],
        2: [(half_y, 0, held)],
        3: [(half_da, 0, cut), (half_db, 0, held - cut)],
    }

    send_local = senders % rows_n
    recv_local = receivers % rows_n
    node_ids = jnp.arange(rows_n, dtype=jnp.int32)
    emask = edge_valid.astype(F32)
    consts = {
        "ohs": (send_local[:, None] == node_ids[None, :]).astype(BF),
        "ohr": (recv_local[:, None] == node_ids[None, :]).astype(BF),
        "ohrt": ((recv_local[None, :] == node_ids[:, None]) & (edge_valid[None, :] != 0)).astype(BF),
        "emask": jnp.broadcast_to(emask[:, None], (rows_e, LANES)),
        "nmask": jnp.broadcast_to(node_valid.astype(F32)[:, None], (rows_n, LANES)),
    }
    graph.consts = const_kernel(graph, infos[0], consts)
    weights = (own_weight[0], other_weight[0], out_weight[0], recv_rows, vec_rows)
    graph.consts["wall"] = wall_kernel(graph, infos[0], *weights, near, far)
    rest_far = []

    def first_blocks(rel):
        if not direct:
            return as_blocks([node_all], rel)
        if rel == 0:
            return as_blocks(own_lines, None) + [(own_far, None, r * rows_n, rows_n) for r in range(4)]
        entry = [(node_in, "micro", 0, rows_n)]
        entry += [(own_shared[rel - 1], None, r * rows_n, rows_n) for r in range(3)]
        return entry + [(rest_far[0], None, (4 * (rel - 1) + r) * rows_n, rows_n) for r in range(4)]

    first = []
    blocks2 = []

    def add_first(rel, after):
        first.append(first_kernel(graph, infos[rel], edge_in, node_in, first_blocks(rel), after))

    add_first(0, [])
    if direct:
        plan = []
        for k in range(3):
            plan.append((0, k + 1, 0, rows_n, 0, 4 * k * rows_n))
            plan.append((1 + k, None, 0, 3 * rows_n, 0, (4 * k + 1) * rows_n))
        (cat,) = glue_kernel(graph, infos[0], [node_in] + own_shared, plan, [12 * rows_n], [first[0]["stat"]])
        rest_far.append(swap(cat))
        lines2 = [first[0]["t2"]] + lined_up(first[0]["t2"])
        add_first(1, [first[0]["stat"]])
        add_first(2, [first[1]["stat"]])
        plan = [(r, None, 0, rows_n, 0, r * rows_n) for r in range(4)]
        plan += [(r, None, 0, rows_n, 1, (r - 1) * rows_n) for r in range(1, 4)]
        cat, share = glue_kernel(graph, infos[0], lines2, plan, [4 * rows_n, 3 * rows_n], [first[2]["stat"]])
        far2 = swap(cat)
        shared = [across(share, rel) for rel in range(1, 4)]
        add_first(3, [cat])
        blocks2.append(as_blocks(lines2, None) + [(far2, None, r * rows_n, rows_n) for r in range(4)])
    else:
        for rel in range(1, 4):
            add_first(rel, [first[-1]["stat"]])
        for rel in range(4):
            blocks2.append(as_blocks([lax.all_gather(first[rel]["t2"], "rows", axis=0, tiled=True)], None))

    second = []
    third = []

    def add_second(rel, after):
        before = second[-1] if second else None
        second.append(
            second_kernel(graph, infos[rel], first[rel], blocks2[rel], node_cot, edge_cot, before, rel == 0, direct, after)
        )

    def add_third(rel, after):
        before = third[-1] if third else None
        last = third[-1] if third else second[-1]
        third.append(
            third_kernel(
                graph, infos[rel], first[rel], second[rel], sums[rel], edge_in, micro_count, before, last["edge_grad"], last["wg"], last["vec"], rel == 0, direct, after
            )
        )

    add_second(0, [first[3]["stat"]])
    if direct:
        got = swap(second[0]["gs_far"])
        plan = []
        for k in range(3):
            plan.append((k, None, 0, rows_n, 0, 4 * k * rows_n))
            plan.append((3 + k, None, 0, 3 * rows_n, 0, (4 * k + 1) * rows_n))
        sources = [first[rel]["t2"] for rel in range(1, 4)] + shared
        (cat,) = glue_kernel(graph, infos[0], sources, plan, [12 * rows_n], [second[0]["stat"]])
        far2 = swap(cat)
        for rel in range(1, 4):
            entry = [(first[rel]["t2"], None, 0, rows_n)] + [(shared[rel - 1], None, r * rows_n, rows_n) for r in range(3)]
            entry += [(far2, None, (4 * (rel - 1) + r) * rows_n, rows_n) for r in range(4)]
            blocks2.append(entry)
        add_second(1, [])
        parts = add_kernel(graph, infos[0], [second[0]["gs_mine"], got], rows_n, [second[1]["stat"]])
        arrived = [along(parts[r], -r) for r in range(1, 4)]
        add_second(2, [parts[0]])
        add_second(3, [])
        (total,) = add_kernel(graph, infos[0], [parts[0]] + arrived, rows_n, [second[3]["stat"]])
    else:
        for rel in range(1, 4):
            add_second(rel, [])
        total = lax.psum_scatter(second[0]["gs_mine"], "rows", scatter_dimension=0, tiled=True)
    sums = [total] + [across(total, rel) for rel in range(1, 4)]
    add_third(0, [])
    if direct:
        got = swap(third[0]["gs_far"])
        add_third(1, [])
        parts = add_kernel(graph, infos[0], [third[0]["gs_mine"], got], rows_n, [third[1]["token"]])
        arrived = [along(parts[r], -r) for r in range(1, 4)]
        add_third(2, [parts[0]])
        add_third(3, [])
    else:
        for rel in range(1, 4):
            add_third(rel, [])
    stats = ([entry["stat"] for entry in first], [entry["stat"] for entry in second])
    packed, piece = pack_kernel(graph, infos[0], third[3]["wg"], third[3]["vec"], stats, direct)
    if direct:
        (total,) = add_kernel(graph, infos[0], [parts[0]] + arrived, rows_n, [packed["mine"]])
    else:
        total = lax.psum_scatter(third[0]["gs_mine"], "rows", scatter_dimension=0, tiled=True)
    low = [total] + [lax.ppermute(total, "section", [(rel, 0)]) for rel in range(1, 4)]
    if direct:
        pieces = add_kernel(graph, infos[0], [packed["mine"], swap(packed["other"])], piece)
        (whole,) = add_kernel(graph, infos[0], [pieces[0]] + [along(pieces[r], -r) for r in range(1, 4)], piece)
        near = [whole] + lined_up(whole)
        grads = unpack_kernel(graph, infos[0], near, [swap(value) for value in near], piece)
    else:
        flat = lax.psum(packed["flat"], "rows")
        base = 3 * width + 2 * quarter
        sums_all = flat[base : base + TAIL_ROWS]
        rms = jnp.sqrt(sums_all[4:8, 0 : 2 * LANES : LANES] / (sums_all[4:8, 2 * LANES : 2 * LANES + 1] * width))
        rms = jnp.take(rms, jnp.arange(4, dtype=jnp.int32) ^ section, axis=0)
        grads = {
            "own": flat[:width],
            "other": flat[width : 2 * width],
            "out": flat[2 * width : 3 * width],
            "recv": flat[3 * width : base],
            "rms0": rms[:, 0][None],
            "rms1": rms[:, 1][None],
        }
        grads.update({f"vec{k}": sums_all[k : k + 1] for k in range(4)})
    node_grad = node_zero_kernel(
        graph, infos[0], [entry["node_part"] for entry in third], low, third[3]["node_grad"], graph.consts["wall"]
    )
    return (
        second[3]["node_out"][None],
        second[3]["edge_out"][None],
        node_grad[None],
        third[3]["edge_grad"][None],
        grads["own"][None],
        grads["other"][None],
        grads["recv"].reshape(2, quarter, width),
        grads["vec0"],
        grads["out"][None],
        grads["vec1"],
        grads["vec2"],
        grads["vec3"],
        grads["rms0"],
        grads["rms1"],
    )


def solution(mesh):
    whole = P("section", None, None)
    line = P("section", None)
    latents = P(None, "rows", None)
    outs = P("section", None, "rows", None)
    recv = P(None, "section", None)
    ends = P("rows")
    return jax.shard_map(
        on_device,
        mesh=mesh,
        in_specs=(latents,) * 4 + (whole, whole, recv, line, whole, line, line, line) + (ends,) * 4,
        out_specs=(outs,) * 4 + (whole, whole, recv, line, whole, line, line, line, line, line),
        check_vma=False,
    )
```

```python
import types

import jax
import jax.numpy as jnp
from jax import lax
from jax.experimental import pallas as pl
from jax.experimental.pallas import tpu as pltpu
from jax.sharding import PartitionSpec as P

F32 = jnp.float32
BF = jnp.bfloat16
CHUNK = 512
LANES = 128
VEC_ROWS = 16
ANY = pl.ANY
VMEM = pltpu.VMEM
HBM = pltpu.HBM


def dot(left, right):
    return jnp.dot(left, right, preferred_element_type=F32)


def dot_nt(left, right):
    return lax.dot_general(left, right, (((1,), (1,)), ((), ())), preferred_element_type=F32)


def dot_tn(left, right):
    return lax.dot_general(left, right, (((0,), (0,)), ((), ())), preferred_element_type=F32)


def sigmoid(value):
    return 0.5 * jnp.tanh(0.5 * value) + 0.5


def widen(column, width):
    return jnp.concatenate([column] * (width // column.shape[1]), axis=1)


def col_sum(value):
    return jnp.sum(value, axis=0, keepdims=True)


def tail(pre_act, weight_out, vecs):
    hidden = (pre_act * sigmoid(pre_act)).astype(BF)
    update = dot(hidden, weight_out) + vecs[1]
    mean = jnp.mean(update, axis=-1, keepdims=True)
    centre = update - mean
    spread = jnp.mean(centre * centre, axis=-1, keepdims=True)
    inverse = lax.rsqrt(spread + 1e-05)
    scaled = centre * inverse
    return hidden, scaled, inverse, spread + mean * mean, scaled * vecs[2] + vecs[3]


def norm_back(grad_normed, scaled, inverse, gain):
    weighted = grad_normed * gain
    mean_grad = jnp.mean(weighted, axis=-1, keepdims=True)
    mean_both = jnp.mean(weighted * scaled, axis=-1, keepdims=True)
    return inverse * (weighted - mean_grad - scaled * mean_both)


def silu_back(grad_hidden, pre_act):
    sig = sigmoid(pre_act)
    return grad_hidden * (sig * (1.0 + pre_act * (1.0 - sig))), sig


class Info:
    def __init__(self, table, rel):
        self.table, self.rel = table, rel

    def __getitem__(self, k):
        return self.table[self.rel, k]


V, H, A, B = range(4)
PLACES = (VMEM, HBM, pl.ANY, None)


def flat(entries):
    return [item for entry in entries.values() for item in (entry if isinstance(entry, list) else [entry])]


def named(entries, items):
    return {
        name: [next(items) for _ in entry] if isinstance(entry, list) else next(items)
        for name, entry in entries.items()
    }


def run_kernel(body, info, inputs, outputs, scratch, micros, limit):
    given, made = flat(inputs), flat(outputs)
    aliases = {}
    for index, entry in enumerate(made):
        if entry[3] is not None:
            aliases[1 + [array is entry[3] for array, _ in given].index(True)] = index

    def kernel(*refs):
        rest = iter(refs[1:])
        groups = [named(entries, rest) for entries in (inputs, outputs, scratch)]
        body(types.SimpleNamespace(info=Info(refs[0], info.rel), **groups[0], **groups[1], **groups[2]))

    arrays = [pltpu.with_memory_space_constraint(array, PLACES[kind]) for array, kind in given]
    results = pl.pallas_call(
        kernel,
        out_shape=[
            jax.ShapeDtypeStruct(entry[0], entry[1]) if entry[2] >= A else PLACES[entry[2]](entry[0], entry[1])
            for entry in made
        ],
        in_specs=[pl.BlockSpec(memory_space=pltpu.SMEM)] + [pl.BlockSpec(memory_space=PLACES[kind]) for _, kind in given],
        out_specs=[pl.BlockSpec() if entry[2] == B else pl.BlockSpec(memory_space=PLACES[entry[2]]) for entry in made],
        scratch_shapes=flat(scratch),
        input_output_aliases=aliases,
        compiler_params=pltpu.CompilerParams(vmem_limit_bytes=limit * 1024 * 1024),
        cost_estimate=pl.CostEstimate(flops=int(micros * 1.15e9), bytes_accessed=0, transcendentals=0),
    )(info.table, *arrays)
    return types.SimpleNamespace(**named(outputs, iter(results)))


def copy(source, target, sem):
    return pltpu.make_async_copy(source, target, sem)


def either(arrays):
    return [(array, A) for array in arrays]


class Graph:
    def __init__(self, rows_n, rows_e, blocks, width):
        self.rows_n, self.rows_e, self.blocks, self.width = rows_n, rows_e, blocks, width
        self.cap = rows_e // blocks
        self.chunk = min(CHUNK, rows_e)
        self.starts = range(0, rows_e, self.chunk)
        self.consts = {}
        self.extra = max(blocks - 8, 0) * rows_n * width * 2 >> 20

    def const_inputs(self):
        return {name: (array, V) for name, array in self.consts.items()}

    def weight_row(self, section_id, part):
        return (section_id * 3 + part) * self.width

    def weight(self, R, section_id, part, count=1):
        return R.wall[pl.ds(self.weight_row(section_id, part), count * self.width), :]

    def recv_weight(self, R, layer):
        return R.wall[pl.ds((12 + layer) * self.width, self.width), :]

    def vectors(self, R, section_id):
        block = R.wall[pl.ds(14 * self.width + section_id * VEC_ROWS, VEC_ROWS), :].astype(F32)
        return [block[k : k + 1] + block[4 + k : 5 + k] for k in range(4)]


OWN, OTHER, OUT = 0, 1, 2


def half_rows(width):
    half, eighth = width // 2, width // 8
    return half, eighth, 3 * half + 2 * eighth, 3 * half + 2 * eighth + VEC_ROWS


def half_kernel(graph, info, weights, recv, vecs):
    half, eighth, vec_row, rows = half_rows(graph.width)
    quarter = 2 * eighth

    def body(R):
        core, stage = R.info[1], R.stage
        for k in range(3):
            source = R.weights[k].at[pl.ds(pl.multiple_of(core * half, half), half)]
            copy(source, stage.at[pl.ds(k * half, half)], R.sem).start()
        for layer in range(2):
            source = R.recv.at[pl.ds(pl.multiple_of(layer * quarter + core * eighth, eighth), eighth)]
            copy(source, stage.at[pl.ds(3 * half + layer * eighth, eighth)], R.sem).start()
        for k in range(4):
            copy(R.vecs[k], R.rows.at[pl.ds(k, 1)], R.row_sem).start()
        copy(R.rows, R.rows, R.row_sem).wait()
        rows_here = R.rows[...]
        high = rows_here.astype(BF)
        low = (rows_here - high.astype(F32)).astype(BF)
        stage[vec_row : vec_row + VEC_ROWS, :] = jnp.concatenate([high, low, high, low], axis=0)
        loaded = stage.at[pl.ds(0, vec_row)]
        copy(loaded, loaded, R.sem).wait()
        move = copy(stage, R.half, R.sem)
        move.start()
        move.wait()

    inputs = dict(weights=[(array, H) for array in weights], recv=(recv, H), vecs=[(array, H) for array in vecs])
    outputs = dict(half=((rows, graph.width), BF, A, None))
    scratch = dict(
        stage=VMEM((rows, graph.width), BF),
        rows=VMEM((4, graph.width), F32),
        sem=pltpu.SemaphoreType.DMA,
        row_sem=pltpu.SemaphoreType.DMA,
    )
    return run_kernel(body, info, inputs, outputs, scratch, 1, 2).half


def wall_kernel(graph, info, weights, recv, mine, near, far):
    width = graph.width
    half, eighth, vec_row, rows = half_rows(width)
    quarter = 2 * eighth
    pieces = [piece for side in (near, far) for rel in range(1, 4) for piece in side[rel]]
    inputs = dict(
        weights=[(array, H) for array in weights], recv=(recv, H), mine=(mine, A), pieces=either([p[0] for p in pieces])
    )
    total = 14 * width + 4 * VEC_ROWS

    def body(R):
        section, core = R.info[0], R.info[1]
        wall, sem = R.wall, R.sem
        refs = iter(R.pieces)

        def put(source, row, count, unit):
            copy(source, wall.at[pl.ds(pl.multiple_of(row, unit), count)], sem).start()

        for k in range(3):
            put(R.weights[k], section * 3 * width + k * width, width, width)
        for layer in range(2):
            put(R.recv.at[pl.ds(layer * quarter, quarter)], (12 + layer) * width + section * quarter, quarter, quarter)
        put(R.mine.at[pl.ds(vec_row, VEC_ROWS)], 14 * width + section * VEC_ROWS, VEC_ROWS, VEC_ROWS)
        for side, pieces_of in ((core, near), (1 - core, far)):
            for rel in range(1, 4):
                there = section ^ rel
                parts = [(k * half, half, (there * 3 + k) * width + side * half) for k in range(3)]
                parts += [
                    (3 * half + layer * eighth, eighth, (12 + layer) * width + there * quarter + side * eighth)
                    for layer in range(2)
                ]
                if pieces_of is near:
                    parts.append((vec_row, VEC_ROWS, 14 * width + there * VEC_ROWS))
                first = 0
                for _, begin, held in pieces_of[rel]:
                    ref = next(refs)
                    for row, count, target in parts:
                        low, high = max(row, first), min(row + count, first + held)
                        if low < high:
                            put(ref.at[pl.ds(begin + low - first, high - low)], target + low - row, high - low, 16)
                    first += held
        copy(wall, wall, sem).wait()

    outputs = dict(wall=((total, width), BF, V, None))
    return run_kernel(body, info, inputs, outputs, dict(sem=pltpu.SemaphoreType.DMA), 3, 1).wall


def glue_kernel(graph, info, sources, plan, rows, after=()):
    width = graph.width
    inputs = dict(source=[(array, H if array.ndim > 2 else A) for array in sources], after=either(after))
    outputs = dict(out=[((count, width), BF, A, None) for count in rows])
    scratch = dict(stage=[VMEM((count, width), BF) for count in rows], sem=pltpu.SemaphoreType.DMA((len(rows),)))

    def body(R):
        for source, index, row, count, target, place in plan:
            ref = R.source[source] if index is None else R.source[source].at[R.info[0] ^ index]
            copy(ref.at[pl.ds(row, count)], R.stage[target].at[pl.ds(place, count)], R.sem.at[target]).start()
        moves = []
        for k, stage in enumerate(R.stage):
            copy(stage, stage, R.sem.at[k]).wait()
            moves.append(copy(stage, R.out[k], R.sem.at[k]))
            moves[-1].start()
        for move in moves:
            move.wait()

    return run_kernel(body, info, inputs, outputs, scratch, 2, 4).out


def summed_rows(stages, here):
    total = stages[0][here, :].astype(F32)
    for other in stages[1:]:
        total = total + other[here, :].astype(F32)
    return total.astype(BF)


def add_kernel(graph, info, arrays, rows, after=()):
    count, width = arrays[0].shape
    inputs = dict(source=either(arrays), after=either(after))
    outputs = dict(out=[((rows, width), BF, A, None)] * (count // rows))
    scratch = dict(stage=[VMEM((count, width), BF)] * len(arrays), sem=pltpu.SemaphoreType.DMA((len(arrays),)))

    def body(R):
        moves = [copy(source, stage, R.sem.at[k]) for k, (source, stage) in enumerate(zip(R.source, R.stage))]
        for move in moves:
            move.start()
        for move in moves:
            move.wait()
        moves = []
        for k in range(count // rows):
            here = pl.ds(k * rows, rows)
            R.stage[0][here, :] = summed_rows(R.stage, here)
            moves.append(copy(R.stage[0].at[here], R.out[k], R.sem.at[0]))
            moves[-1].start()
        for move in moves:
            move.wait()

    return run_kernel(body, info, inputs, outputs, scratch, 2, 6).out


def node_zero_kernel(graph, info, parts, sums, node_grad, wall):
    rows_n, width = graph.rows_n, graph.width
    inputs = dict(parts=either(parts), sums=either(sums), old=(node_grad, H), wall=(wall, V))
    outputs = dict(node_grad=(node_grad.shape, BF, H, node_grad), token=((8, LANES), F32, V, None))
    scratch = dict(
        part=VMEM((4 * rows_n, width), F32),
        sum=VMEM((4 * rows_n, width), BF),
        total=VMEM((4, rows_n, width), BF),
        sem=pltpu.SemaphoreType.DMA((3,)),
    )

    def body(R):
        R.token[...] = jnp.zeros_like(R.token)

        @pl.when(R.info[0] == 0)
        def _():
            for k in range(4):
                here = pl.ds(k * rows_n, rows_n)
                copy(R.parts[k], R.part.at[here], R.sem.at[0]).start()
                copy(R.sums[k], R.sum.at[here], R.sem.at[1]).start()
            copy(R.part, R.part, R.sem.at[0]).wait()
            copy(R.sum, R.sum, R.sem.at[1]).wait()
            total = R.part[...] + dot_nt(R.sum[...], graph.weight(R, 0, OTHER))
            R.total[...] = total.astype(BF).reshape(4, rows_n, width)
            move = copy(R.total, R.node_grad, R.sem.at[2])
            move.start()
            move.wait()

    return run_kernel(body, info, inputs, outputs, scratch, 2, 6)


def const_kernel(graph, info, arrays):
    inputs = dict(source=[(array, H) for array in arrays])
    outputs = dict(out=[(array.shape, array.dtype, V, None) for array in arrays])

    def body(R):
        moves = [copy(source, out, R.sem.at[k]) for k, (source, out) in enumerate(zip(R.source, R.out))]
        for move in moves:
            move.start()
        for move in moves:
            move.wait()

    scratch = dict(sem=pltpu.SemaphoreType.DMA((len(arrays),)))
    return run_kernel(body, info, inputs, outputs, scratch, 2, 1).out


def block_inputs(blocks):
    return [(array, H if index == MICRO else A) for array, index, _, _ in blocks]


MICRO = -1


def block_copies(graph, R, blocks, sem):
    moves = []
    place = 0
    for k, (_, index, row, rows) in enumerate(blocks):
        source = R.block[k]
        if index is not None:
            source = source.at[R.info[2] if index == MICRO else index]
        if rows == graph.rows_n:
            start = pl.multiple_of(R.info[3 + place] * graph.rows_n, graph.rows_n)
        else:
            start = 0
        moves.append(copy(source.at[pl.ds(row, rows)], R.hall.at[pl.ds(start, rows)], sem))
        place += rows // graph.rows_n
    return moves


def bucket_rows(graph, start):
    for bucket in range(start // graph.cap, (start + graph.chunk) // graph.cap):
        yield pl.ds(bucket * graph.cap, graph.cap), pl.ds(bucket * graph.rows_n, graph.rows_n)


def stack(pieces):
    return jnp.concatenate(pieces, axis=0) if len(pieces) > 1 else pieces[0]


def stat_pair(square, stream, mask):
    branch = col_sum(mask * square)
    total = col_sum(mask * jnp.sum(stream * stream, axis=-1, keepdims=True))
    return branch, total


def put_stats(stat, pairs, width):
    branch, total = pairs[0]
    for pair in pairs[1:]:
        branch, total = branch + pair[0], total + pair[1]
    stat[0:1, :] = jnp.broadcast_to(branch * width, (1, LANES))
    stat[1:2, :] = jnp.broadcast_to(total, (1, LANES))


def first_kernel(graph, info, edge_in, node_in, blocks, after):
    rows_e, rows_n, width = graph.rows_e, graph.rows_n, graph.width
    inputs = dict(
        edges=(edge_in, H), nodes=(node_in, H), block=block_inputs(blocks), after=either(after), **graph.const_inputs()
    )
    rows = ((rows_e, width), BF, V, None)
    few = ((rows_n, width), BF, V, None)
    outputs = dict(
        edge1=rows,
        z0=rows,
        x0=rows,
        q0=((rows_e, LANES), F32, V, None),
        s0=rows,
        node0=few,
        node1=few,
        g1=few,
        z1=few,
        x1=few,
        q1=((rows_n, LANES), F32, V, None),
        stat=((8, LANES), F32, V, None),
        t2=((rows_n, width), BF, A, None),
    )
    scratch = dict(
        edge=VMEM((rows_e, width), BF),
        hall=VMEM((graph.blocks * rows_n, width), BF),
        t2_here=VMEM((rows_n, width), BF),
        sem=pltpu.SemaphoreType.DMA((4,)),
    )

    def body(R):
        info = R.info
        section, micro = info[0], info[2]
        node_copy = copy(R.nodes.at[micro], R.node0, R.sem.at[0])
        hall_copies = block_copies(graph, R, blocks, R.sem.at[1])
        edge_copy = copy(R.edges.at[micro], R.edge, R.sem.at[2])
        node_copy.start()
        for move in hall_copies:
            move.start()
        edge_copy.start()
        node_copy.wait()
        node = R.node0[...]
        recv_node = dot(node, graph.recv_weight(R, 0)).astype(BF)
        copy(R.hall, R.hall, R.sem.at[1]).wait()
        edge_copy.wait()
        vecs = graph.vectors(R, 0)
        pairs = []
        for start in graph.starts:
            rows = pl.ds(start, graph.chunk)
            mask = R.emask[rows, :]
            edge = R.edge[rows, :]
            send = stack([dot(R.ohs[e, :], R.hall[n, :]).astype(BF) for e, n in bucket_rows(graph, start)])
            R.s0[rows, :] = send
            pre_act = dot(jnp.concatenate([edge, send], axis=1), graph.weight(R, 0, OWN, 2))
            pre_act = pre_act + dot(R.ohr[rows, :], recv_node) + vecs[0]
            hidden, scaled, inverse, square, normed = tail(pre_act, graph.weight(R, 0, OUT), vecs)
            stream = edge.astype(F32) + widen(mask, width) * normed
            R.edge1[rows, :] = stream.astype(BF)
            R.z0[rows, :] = pre_act.astype(BF)
            R.x0[rows, :] = scaled.astype(BF)
            R.q0[rows, :] = jnp.broadcast_to(inverse, (graph.chunk, LANES))
            pairs.append(stat_pair(square, stream, mask[:, :1]))
        summed = dot(R.ohrt[...], R.edge1[...]).astype(BF)
        R.g1[...] = summed
        vecs = graph.vectors(R, 1)
        pre_act = dot(jnp.concatenate([node, summed], axis=1), graph.weight(R, 1, OWN, 2)) + vecs[0]
        hidden, scaled, inverse, square, normed = tail(pre_act, graph.weight(R, 1, OUT), vecs)
        nmask = R.nmask[...]
        stream = node.astype(F32) + widen(nmask, width) * normed
        low = stream.astype(BF)
        R.t2_here[...] = dot(low, graph.weight(R, 2, OTHER)).astype(BF)
        out_copy = copy(R.t2_here, R.t2, R.sem.at[3])
        out_copy.start()
        R.node1[...] = low
        R.z1[...] = pre_act.astype(BF)
        R.x1[...] = scaled.astype(BF)
        R.q1[...] = jnp.broadcast_to(inverse, (rows_n, LANES))

        @pl.when(section == 0)
        def _():
            put_stats(R.stat, pairs, width)

        @pl.when(section != 0)
        def _():
            put_stats(R.stat, [stat_pair(square, stream, nmask[:, :1])], width)

        out_copy.wait()

    return run_kernel(body, info, inputs, outputs, scratch, 8, 10 + graph.extra)


def sender_outputs(graph, direct):
    rows = graph.blocks * graph.rows_n
    if direct:
        return dict(gs=[((rows // 2, graph.width), BF, A, None)] * 2)
    return dict(gs=[((rows, graph.width), BF, A, None)])


def sender_sums(graph, R, grads, stage, sem):
    for place in range(graph.blocks):
        bucket = R.info[3 + place]
        rows = pl.ds(pl.multiple_of(bucket * graph.cap, graph.cap), graph.cap)
        here = pl.ds(place * graph.rows_n, graph.rows_n)
        stage[here, :] = dot_tn(R.ohs[rows, :], grads[rows, :]).astype(BF)
    row = 0
    for target in R.gs:
        rows = target.shape[0]
        copy(stage.at[pl.ds(row, rows)], target, sem).start()
        row += rows
    copy(stage, stage, sem).wait()


def add_recv(graph, R, layer, node, grad_recv):
    quarter = graph.width // 4
    start = pl.multiple_of(R.info[0] * quarter, quarter)
    rows = pl.ds(3 * graph.width + layer * quarter, quarter)
    R.wg[rows, :] += dot_tn(node[:, pl.ds(start, quarter)], grad_recv)


def second_kernel(graph, info, first, blocks, node_cot, edge_cot, before, own_first, direct, after):
    rows_e, rows_n, width = graph.rows_e, graph.rows_n, graph.width
    micro_count = node_cot.shape[0]
    inputs = dict(
        edge1=(first.edge1, V),
        node0=(first.node0, V),
        node1=(first.node1, V),
        edge_cot=(edge_cot, H),
        node_cot=(node_cot, H),
        block=block_inputs(blocks),
        after=either(after),
        **graph.const_inputs(),
    )
    chain = [None] * 5
    if before is not None:
        chain = [before.edge_out, before.node_out, before.edge_grad, before.wg, before.vec]
        inputs.update(old=[(array, kind) for array, kind in zip(chain, (H, H, H, V, V))])
    rows = VMEM((rows_e, width), BF)
    few = VMEM((rows_n, width), BF)
    outputs = dict(
        edge_out=((micro_count, rows_e, width), BF, H, chain[0]),
        node_out=((micro_count, rows_n, width), BF, H, chain[1]),
        edge_grad=((micro_count, rows_e, width), BF, H, chain[2]),
        wg=((3 * width + width // 2, width), F32, V, chain[3]),
        vec=((8, width), F32, V, chain[4]),
        eg2=((rows_e, width), BF, V, None),
        ng=((rows_n, width), BF, V, None),
        gr=((rows_n, width), BF, V, None),
        stat=((8, LANES), F32, V, None),
    )
    if own_first:
        outputs.update(sender_outputs(graph, direct))
    scratch = dict(
        hall=VMEM((graph.blocks * rows_n, width), BF),
        cot=rows,
        ncot=few,
        edge2=rows,
        eg=rows,
        node_here=few,
        z=rows,
        x=rows,
        q=VMEM((rows_e, LANES), F32),
        a=rows,
        gu=rows,
        gz=rows,
        sem=pltpu.SemaphoreType.DMA((8,)),
    )

    def body(R):
        info = R.info
        section, micro = info[0], info[2]
        sem = R.sem
        hall_copies = block_copies(graph, R, blocks, sem.at[0])
        cot_copy = copy(R.edge_cot.at[micro], R.cot, sem.at[1])
        ncot_copy = copy(R.node_cot.at[micro], R.ncot, sem.at[2])
        for move in hall_copies:
            move.start()
        ncot_copy.start()
        cot_copy.start()
        if own_first:
            R.wg[...] = jnp.zeros_like(R.wg)
            R.vec[...] = jnp.zeros_like(R.vec)
        node = R.node1[...]
        recv_node = dot(node, graph.recv_weight(R, 1)).astype(BF)
        copy(R.hall, R.hall, sem.at[0]).wait()
        vecs = graph.vectors(R, 2)
        pairs = []
        for start in graph.starts:
            rows = pl.ds(start, graph.chunk)
            mask = R.emask[rows, :]
            edge = R.edge1[rows, :]
            ends = stack(
                [
                    dot(
                        jnp.concatenate([R.ohs[e, :], R.ohr[e, :]], axis=1),
                        jnp.concatenate([R.hall[n, :], recv_node], axis=0),
                    )
                    for e, n in bucket_rows(graph, start)
                ]
            )
            pre_act = dot(edge, graph.weight(R, 2, OWN)) + ends + vecs[0]
            hidden, scaled, inverse, square, normed = tail(pre_act, graph.weight(R, 2, OUT), vecs)
            stream = edge.astype(F32) + widen(mask, width) * normed
            R.edge2[rows, :] = stream.astype(BF)
            R.z[rows, :] = pre_act.astype(BF)
            R.x[rows, :] = scaled.astype(BF)
            R.q[rows, :] = jnp.broadcast_to(inverse, (graph.chunk, LANES))
            R.a[rows, :] = hidden
            pairs.append(stat_pair(square, stream, mask[:, :1]))

        @pl.when(section >= 2)
        def _():
            copy(R.edge2, R.edge_out.at[micro], sem.at[3]).start()

        @pl.when(section < 2)
        def _():
            copy(R.edge1, R.edge_out.at[micro], sem.at[3]).start()

        vecs = graph.vectors(R, 3)
        summed = dot(R.ohrt[...], R.edge2[...]).astype(BF)
        weight_out = graph.weight(R, 3, OUT)
        pre_act = dot(jnp.concatenate([node, summed], axis=1), graph.weight(R, 3, OWN, 2)) + vecs[0]
        hidden, scaled, inverse, square, normed = tail(pre_act, weight_out, vecs)
        nmask = R.nmask[...]
        wide_mask = widen(nmask, width)
        stream = node.astype(F32) + wide_mask * normed
        R.node_here[...] = jnp.where(
            section == 0, R.node0[...], jnp.where(section == 3, stream.astype(BF), node)
        )
        node_copy = copy(R.node_here, R.node_out.at[micro], sem.at[4])
        node_copy.start()

        @pl.when(section == 3)
        def _():
            put_stats(R.stat, [stat_pair(square, stream, nmask[:, :1])], width)

        @pl.when(section != 3)
        def _():
            put_stats(R.stat, pairs, width)

        ncot_copy.wait()
        grad = R.ncot[...].astype(F32)
        grad_normed = wide_mask * grad
        grad_update = norm_back(grad_normed, scaled, inverse, vecs[2])
        grad_low = grad_update.astype(BF)
        grad_pre, _ = silu_back(dot_nt(grad_low, weight_out), pre_act)
        pre_low = grad_pre.astype(BF)
        R.ng[...] = (grad + dot_nt(pre_low, graph.weight(R, 3, OWN))).astype(BF)
        grad_sum = dot_nt(pre_low, graph.weight(R, 3, OTHER))
        grad_high = grad_sum.astype(BF)
        grad_both = jnp.concatenate([grad_high, (grad_sum - grad_high.astype(F32)).astype(BF)], axis=0)

        @pl.when(section == 3)
        def _():
            R.wg[0:width, :] += dot_tn(node, pre_low)
            R.wg[width : 2 * width, :] += dot_tn(summed, pre_low)
            R.wg[2 * width : 3 * width, :] += dot_tn(hidden, grad_low)
            R.vec[0:1, :] += col_sum(grad_pre)
            R.vec[1:2, :] += col_sum(grad_update)
            R.vec[2:3, :] += col_sum(grad_normed * scaled)
            R.vec[3:4, :] += col_sum(grad_normed)

        cot_copy.wait()
        vecs = graph.vectors(R, 2)

        def arriving(rows, mask):
            onehot = R.ohr[rows, :]
            spread = dot(jnp.concatenate([onehot, onehot], axis=1), grad_both)
            return (R.cot[rows, :].astype(F32) + mask * spread).astype(BF)

        def edge_back(sums):
            totals = [jnp.zeros((1, width), F32)] * 4
            for start in graph.starts:
                rows = pl.ds(start, graph.chunk)
                mask = R.emask[rows, :]
                low = arriving(rows, widen(mask, width))
                R.eg[rows, :] = low
                wide = low.astype(F32)
                scaled = R.x[rows, :].astype(F32)
                pre_act = R.z[rows, :].astype(F32)
                inverse = widen(R.q[rows, :] * mask, width)
                grad_update = norm_back(wide, scaled, inverse, vecs[2])
                grad_low = grad_update.astype(BF)
                grad_pre, _ = silu_back(dot_nt(grad_low, graph.weight(R, 2, OUT)), pre_act)
                pre_low = grad_pre.astype(BF)
                R.gz[rows, :] = pre_low
                R.eg2[rows, :] = (wide + dot_nt(pre_low, graph.weight(R, 2, OWN))).astype(BF)
                if sums:
                    R.gu[rows, :] = grad_low
                    normed = widen(mask, width) * wide
                    parts = (grad_pre, grad_update, normed * scaled, normed)
                    totals = [total + col_sum(part) for total, part in zip(totals, parts)]
            if sums:
                R.wg[0:width, :] += dot_tn(R.edge1[...], R.gz[...])
                R.wg[2 * width : 3 * width, :] += dot_tn(R.a[...], R.gu[...])
                for k in range(4):
                    R.vec[k : k + 1, :] += totals[k]

        @pl.when(section == 2)
        def _():
            edge_back(True)

        @pl.when(section != 2)
        def _():
            edge_back(False)

        @pl.when(section == 2)
        def _():
            copy(R.eg2, R.edge_grad.at[micro], sem.at[6]).start()

        @pl.when(section == 3)
        def _():
            copy(R.eg, R.edge_grad.at[micro], sem.at[6]).start()

        grad_recv = dot(R.ohrt[...], R.gz[...]).astype(BF)
        R.gr[...] = grad_recv
        add_recv(graph, R, 1, R.node1, grad_recv)
        if own_first:
            sender_sums(graph, R, R.gz, R.hall, sem.at[5])
        node_copy.wait()
        copy(R.edge2, R.edge_out.at[micro], sem.at[3]).wait()

        @pl.when(section >= 2)
        def _():
            copy(R.eg, R.edge_grad.at[micro], sem.at[6]).wait()

    return run_kernel(body, info, inputs, outputs, scratch, 14, 15 + graph.extra)


def third_kernel(graph, info, first, second, sums, edge_in, before, own_first, direct, after):
    rows_e, rows_n, width = graph.rows_e, graph.rows_n, graph.width
    inputs = dict(
        second=[(array, V) for array in (second.eg2, second.ng, second.gr)],
        z0=(first.z0, V),
        x0=(first.x0, V),
        q0=(first.q0, V),
        s0=(first.s0, V),
        node0=(first.node0, V),
        node1=(first.node1, V),
        g1=(first.g1, V),
        z1=(first.z1, V),
        x1=(first.x1, V),
        q1=(first.q1, V),
        sums=either(sums),
        edges=(edge_in, H),
        after=either(after),
        **graph.const_inputs(),
    )
    node_grad = None if own_first else before.node_grad
    chain = [(before.edge_grad, H), (before.wg, V), (before.vec, V)]
    inputs.update(old=chain if own_first else chain + [(node_grad, H)])
    micro_count = before.edge_grad.shape[0]
    rows = VMEM((rows_e, width), BF)
    few = VMEM((rows_n, width), BF)
    outputs = dict(
        edge_grad=(before.edge_grad.shape, BF, H, before.edge_grad),
        node_grad=((micro_count, rows_n, width), BF, H, node_grad),
        wg=(before.wg.shape, F32, V, before.wg),
        vec=(before.vec.shape, F32, V, before.vec),
        node_part=((rows_n, width), F32, A, None),
        token=((8, LANES), F32, V, None),
    )
    if own_first:
        outputs.update(sender_outputs(graph, direct))
        outputs.update(total=((rows_n, width), BF, A, None))
    scratch = dict(
        edge=rows,
        stage=[few] * len(sums),
        out_edge=rows,
        out_node=few,
        gu=rows,
        a=rows,
        gz=rows,
        part=VMEM((rows_n, width), F32),
        sem=pltpu.SemaphoreType.DMA((7,)),
    )
    if own_first:
        scratch.update(sends=VMEM((graph.blocks * rows_n, width), BF))

    def body(R):
        info = R.info
        section, micro = info[0], info[2]
        sem = R.sem
        eg2, ng, gr = R.second
        R.token[...] = jnp.zeros_like(R.token)
        sums_copies = [copy(source, stage, sem.at[0]) for source, stage in zip(R.sums, R.stage)]
        for move in sums_copies:
            move.start()
        edge_copy = copy(R.edges.at[micro], R.edge, sem.at[1])

        @pl.when(section == 0)
        def _():
            edge_copy.start()

        for move in sums_copies:
            move.wait()
        if own_first:
            R.stage[0][...] = summed_rows(R.stage, slice(None))
            total_copy = copy(R.stage[0], R.total, sem.at[6])
            total_copy.start()
        gs2 = R.stage[0][...]
        grad_mid = (
            ng[...].astype(F32) + dot_nt(gr[...], graph.recv_weight(R, 1)) + dot_nt(gs2, graph.weight(R, 2, OTHER))
        ).astype(BF)
        R.out_node[...] = jnp.where(section == 3, ng[...], grad_mid)

        @pl.when(section == 2)
        def _():
            R.wg[width : 2 * width, :] += dot_tn(R.node1[...], gs2)

        vecs = graph.vectors(R, 1)
        wide = grad_mid.astype(F32)
        grad_normed = widen(R.nmask[...], width) * wide
        scaled = R.x1[...].astype(F32)
        pre_act = R.z1[...].astype(F32)
        grad_update = norm_back(grad_normed, scaled, widen(R.q1[...], width), vecs[2])
        grad_low = grad_update.astype(BF)
        grad_pre, sig = silu_back(dot_nt(grad_low, graph.weight(R, 1, OUT)), pre_act)
        pre_low = grad_pre.astype(BF)
        grad_node = (wide + dot_nt(pre_low, graph.weight(R, 1, OWN))).astype(BF)
        grad_sum = dot_nt(pre_low, graph.weight(R, 1, OTHER))
        grad_high = grad_sum.astype(BF)
        grad_both = jnp.concatenate([grad_high, (grad_sum - grad_high.astype(F32)).astype(BF)], axis=0)

        @pl.when(section == 1)
        def _():
            R.out_node[...] = grad_node
            R.wg[0:width, :] += dot_tn(R.node0[...], pre_low)
            R.wg[width : 2 * width, :] += dot_tn(R.g1[...], pre_low)
            R.wg[2 * width : 3 * width, :] += dot_tn((pre_act * sig).astype(BF), grad_low)
            R.vec[0:1, :] += col_sum(grad_pre)
            R.vec[1:2, :] += col_sum(grad_update)
            R.vec[2:3, :] += col_sum(grad_normed * scaled)
            R.vec[3:4, :] += col_sum(grad_normed)

        vecs = graph.vectors(R, 0)

        def arriving(rows, mask):
            onehot = R.ohr[rows, :]
            spread = dot(jnp.concatenate([onehot, onehot], axis=1), grad_both)
            return (eg2[rows, :].astype(F32) + mask * spread).astype(BF)

        def edge_back(sums):
            totals = [jnp.zeros((1, width), F32)] * 4
            for start in graph.starts:
                rows = pl.ds(start, graph.chunk)
                mask = R.emask[rows, :]
                wide = arriving(rows, widen(mask, width)).astype(F32)
                scaled = R.x0[rows, :].astype(F32)
                pre_act = R.z0[rows, :].astype(F32)
                inverse = widen(R.q0[rows, :] * mask, width)
                grad_update = norm_back(wide, scaled, inverse, vecs[2])
                grad_low = grad_update.astype(BF)
                grad_pre, sig = silu_back(dot_nt(grad_low, graph.weight(R, 0, OUT)), pre_act)
                pre_low = grad_pre.astype(BF)
                R.gz[rows, :] = pre_low
                if sums:
                    R.out_edge[rows, :] = (wide + dot_nt(pre_low, graph.weight(R, 0, OWN))).astype(BF)
                    R.gu[rows, :] = grad_low
                    R.a[rows, :] = (pre_act * sig).astype(BF)
                    normed = widen(mask, width) * wide
                    parts = (grad_pre, grad_update, normed * scaled, normed)
                    totals = [total + col_sum(part) for total, part in zip(totals, parts)]
            return totals

        @pl.when(section == 0)
        def _():
            totals = edge_back(True)
            copy(R.out_edge, R.edge_grad.at[micro], sem.at[2]).start()
            edge_copy.wait()
            R.wg[0:width, :] += dot_tn(R.edge[...], R.gz[...])
            R.wg[width : 2 * width, :] += dot_tn(R.s0[...], R.gz[...])
            R.wg[2 * width : 3 * width, :] += dot_tn(R.a[...], R.gu[...])
            for k in range(4):
                R.vec[k : k + 1, :] += totals[k]

        @pl.when(section == 1)
        def _():
            for start in graph.starts:
                rows = pl.ds(start, graph.chunk)
                R.out_edge[rows, :] = arriving(rows, widen(R.emask[rows, :], width))
            copy(R.out_edge, R.edge_grad.at[micro], sem.at[2]).start()

        @pl.when(section > 0)
        def _():
            edge_back(False)

        grad_recv = dot(R.ohrt[...], R.gz[...]).astype(BF)
        add_recv(graph, R, 0, R.node0, grad_recv)

        @pl.when(section == 0)
        def _():
            R.part[...] = grad_node.astype(F32) + dot_nt(grad_recv, graph.recv_weight(R, 0))

        node_copy = copy(R.out_node, R.node_grad.at[micro], sem.at[3])
        node_copy.start()
        part_copy = copy(R.part, R.node_part, sem.at[5])
        part_copy.start()
        if own_first:
            sender_sums(graph, R, R.gz, R.sends, sem.at[4])
            total_copy.wait()
        node_copy.wait()
        part_copy.wait()

        @pl.when(section < 2)
        def _():
            copy(R.out_edge, R.edge_grad.at[micro], sem.at[2]).wait()

    return run_kernel(body, info, inputs, outputs, scratch, 10, 13 + graph.extra)


PIECES = 8
TAIL_ROWS = 16


def stats_block(graph, R):
    section = R.info[0]
    edge_count = col_sum(R.emask[...])
    node_count = col_sum(R.nmask[...])
    even = (section & 1) == 0
    valid = jnp.where(even, edge_count, node_count)
    rows = [R.vec[0:4, :]]
    for k in range(4):
        pair = jnp.where(section < 2, R.first[k][0:2, :], R.second[k][0:2, :])
        rows.append(jnp.concatenate([pair[0:1], pair[1:2], valid, jnp.zeros_like(valid)], axis=1))
    rows.append(jnp.zeros((TAIL_ROWS - 8, graph.width), F32))
    return jnp.concatenate(rows, axis=0)


def pack_kernel(graph, info, wg, vec, stats, direct, after):
    width = graph.width
    held = wg.shape[0]
    piece = -(-(held + TAIL_ROWS) // (16 * PIECES)) * 16
    inputs = dict(
        wg=(wg, V),
        vec=(vec, V),
        emask=(graph.consts["emask"], V),
        nmask=(graph.consts["nmask"], V),
        first=[(stat, V) for stat in stats[0]],
        second=[(stat, V) for stat in stats[1]],
        after=either(after),
    )
    low = BF if direct else F32
    count = 2 if direct else 1
    outputs = dict(out=[((PIECES * piece // count, width), low, A, None)] * count)
    scratch = dict(stage=VMEM((PIECES * piece, width), low), sem=pltpu.SemaphoreType.DMA)

    def body(R):
        info, sem = R.info, R.sem
        core = info[1]
        R.stage[0:held, :] = R.wg[...].astype(low)
        R.stage[held : held + TAIL_ROWS, :] = stats_block(graph, R).astype(low)
        rest = PIECES * piece - held - TAIL_ROWS
        if rest:
            R.stage[held + TAIL_ROWS :, :] = jnp.zeros((rest, width), low)
        if direct:
            for k, side in ((1, 1 - core), (0, core)):
                for r in range(4):
                    line = lax.shift_right_logical(info[3 + r], 1)
                    start = pl.multiple_of((side * 4 + line) * piece, 16)
                    copy(R.stage.at[pl.ds(start, piece)], R.out[k].at[pl.ds(r * piece, piece)], sem).start()
        else:
            copy(R.stage, R.out[0], sem).start()
        copy(R.stage, R.stage, sem).wait()

    return run_kernel(body, info, inputs, outputs, scratch, 3, 8).out, piece


def unpack_kernel(graph, info, mine, far, piece):
    width = graph.width
    quarter = width // 4
    inputs = dict(mine=either(mine), far=either(far))
    big = ((width, width), F32, H, None)
    outputs = dict(
        grads=[big] * 3,
        recv=((2 * quarter, width), F32, H, None),
        vec=[((1, width), F32, B, None)] * 4,
        rms=[((1, 4), F32, B, None)] * 2,
    )
    scratch = dict(
        stage=VMEM((PIECES * piece, width), BF),
        wide=VMEM((3 * width, width), F32),
        wide_recv=VMEM((2 * quarter, width), F32),
        sem=pltpu.SemaphoreType.DMA((5,)),
    )

    def body(R):
        info, sem = R.info, R.sem
        core = info[1]
        for r in range(4):
            line = lax.shift_right_logical(info[3 + r], 1)
            for source, side in ((R.mine[r], core), (R.far[r], 1 - core)):
                start = pl.multiple_of((side * 4 + line) * piece, 16)
                copy(source, R.stage.at[pl.ds(start, piece)], sem.at[0]).start()
        copy(R.stage, R.stage, sem.at[0]).wait()
        moves = []
        for k in range(3):
            rows = pl.ds(k * width, width)
            R.wide[rows, :] = R.stage[rows, :].astype(F32)
            moves.append(copy(R.wide.at[rows], R.grads[k], sem.at[1 + k]))
            moves[-1].start()
        base = 3 * width + 2 * quarter
        sums = R.stage[base : base + TAIL_ROWS, :].astype(F32)
        micro = lax.broadcasted_iota(jnp.int32, (1, 4), 1) ^ info[0]
        for k in range(4):
            R.vec[k][...] = sums[k : k + 1]
        for which in range(2):
            total = jnp.zeros((1, 4), F32)
            for k in range(4):
                row = sums[4 + k : 5 + k]
                square = row[:, which * LANES : which * LANES + 4] / (row[:, 2 * LANES : 2 * LANES + 4] * width)
                total = total + jnp.where(micro == k, jnp.sqrt(square), 0.0)
            R.rms[which][...] = total
        R.wide_recv[...] = R.stage[3 * width : base, :].astype(F32)
        moves.append(copy(R.wide_recv, R.recv, sem.at[4]))
        moves[-1].start()
        for move in moves:
            move.wait()

    return run_kernel(body, info, inputs, outputs, scratch, 3, 10)


def on_device(
    node_in,
    edge_in,
    node_cot,
    edge_cot,
    own_weight,
    other_weight,
    recv_weight,
    first_bias,
    out_weight,
    out_bias,
    norm_gain,
    norm_bias,
    senders,
    receivers,
    node_valid,
    edge_valid,
):
    micro_count, rows_n, width = node_in.shape
    rows_e = edge_in.shape[1]
    blocks = lax.axis_size("rows")
    section = lax.axis_index("section")
    row_pos = lax.axis_index("rows")
    core = row_pos % 2
    here = row_pos // 2
    graph = Graph(rows_n, rows_e, blocks, width)
    lines = blocks // 2
    direct = lines == 4
    quarter = width // 4

    def swap(value):
        return lax.ppermute(value, "rows", [(i, i ^ 1) for i in range(blocks)])

    def along(value, distance, flip=0):
        route = [(i, (i // 2 + distance) % lines * 2 + (i % 2 ^ flip)) for i in range(blocks)]
        return lax.ppermute(value, "rows", route)

    def across(value, rel):
        return lax.ppermute(value, "section", [(i, i ^ rel) for i in range(4)])

    if direct:
        places = [((here - r) % 4) * 2 + core for r in range(4)] + [((here - r) % 4) * 2 + 1 - core for r in range(4)]
    else:
        places = [jnp.int32(k) for k in range(blocks)]
    table = jnp.stack([jnp.stack([section, core, section ^ rel] + places) for rel in range(4)]).astype(jnp.int32)
    infos = [Info(table, rel) for rel in range(4)]

    def as_blocks(arrays, index):
        return [(array, index, 0, array.shape[-2]) for array in arrays]

    def lined_up(value):
        return [along(value, r) for r in range(1, 4)]

    def pick(array, rel):
        return lax.dynamic_index_in_dim(array, section ^ rel, 0, keepdims=False)

    def as_blocks(arrays, index):
        return [(array, index, 0, array.shape[-2]) for array in arrays]

    def lined_up(value):
        return [along(value, r) for r in range(1, 4)]

    send_local = senders % rows_n
    recv_local = receivers % rows_n
    node_ids = jnp.arange(rows_n, dtype=jnp.int32)
    consts = const_kernel(
        graph,
        infos[0],
        [
            (send_local[:, None] == node_ids[None, :]).astype(BF),
            (recv_local[:, None] == node_ids[None, :]).astype(BF),
            ((recv_local[None, :] == node_ids[:, None]) & (edge_valid[None, :] != 0)).astype(BF),
            jnp.broadcast_to(edge_valid.astype(F32)[:, None], (rows_e, LANES)),
            jnp.broadcast_to(node_valid.astype(F32)[:, None], (rows_n, LANES)),
        ],
    )
    graph.consts = dict(ohs=consts[0], ohr=consts[1], ohrt=consts[2], emask=consts[3], nmask=consts[4])

    weights = (own_weight[0], other_weight[0], out_weight[0])
    recv_rows = recv_weight.reshape(2 * quarter, width)
    half = half_kernel(graph, infos[0], weights, recv_rows, (first_bias, out_bias, norm_gain, norm_bias))
    half_x, half_y = across(half, 1), across(half, 2)
    held = half.shape[0]
    cut = held // 32 * 16
    plan = [(0, None, 0, cut, 0, 0), (1, None, cut, held - cut, 1, 0)]
    plan += [(0, None, 0, held, 2, 0), (1, None, 0, held, 2, held)]
    rows = [cut, held - cut, 2 * held]
    send_da, send_db, cat = glue_kernel(graph, infos[0], [half_x, half_y], plan, rows, [consts[4]])
    half_da, half_db, far_xy = across(send_da, 2), across(send_db, 1), swap(cat)
    plan = [(0, None, 0, cut, 0, 0), (1, None, 0, held - cut, 0, cut)]
    if direct:
        nodes = jnp.stack([pick(node_in, 0), pick(node_in, 3)])
        row_lines = [nodes] + lined_up(nodes)
        flat_lines = [line.reshape(2 * rows_n, width) for line in row_lines]
        own_plan = [(r, None, 0, 2 * rows_n, 0, 2 * r * rows_n) for r in range(4)]
        (own_cat,) = glue_kernel(graph, infos[0], flat_lines, own_plan, [8 * rows_n])
        own_far = swap(own_cat)
        plan += [(2, None, 2 * r * rows_n, rows_n, 1, (r - 1) * rows_n) for r in range(1, 4)]
        cat, share = glue_kernel(graph, infos[0], [half_da, half_db, own_cat], plan, [held, 3 * rows_n])
        node_shared = {rel: across(share, rel) for rel in (1, 2)}
    else:
        node_all = lax.all_gather(jnp.stack([pick(node_in, rel) for rel in range(4)]), "rows", axis=1, tiled=True)
        (cat,) = glue_kernel(graph, infos[0], [half_da, half_db], plan, [held])
    far_d = swap(cat)
    near = {1: [(half_x, 0, held)], 2: [(half_y, 0, held)], 3: [(half_da, 0, cut), (half_db, 0, held - cut)]}
    far = {1: [(far_xy, 0, held)], 2: [(far_xy, held, held)], 3: [(far_d, 0, held)]}
    graph.consts.update(wall=wall_kernel(graph, infos[0], weights, recv_rows, half, near, far))

    first, second, third, node_far = {}, {}, {}, {}

    def add_first(rel, after):
        if not direct:
            blocks1 = as_blocks([node_all], rel)
        elif rel % 3 == 0:
            place = rel // 3
            blocks1 = [(line, place * rows_n, rows_n) for line in flat_lines]
            blocks1 += [(own_far, (2 * r + place) * rows_n, rows_n) for r in range(4)]
            blocks1 = [(array, None, row, count) for array, row, count in blocks1]
        else:
            blocks1 = [(node_in, MICRO, 0, rows_n)]
            blocks1 += [(node_shared[rel], None, r * rows_n, rows_n) for r in range(3)]
            blocks1 += [(node_far[0], None, (4 * (rel - 1) + r) * rows_n, rows_n) for r in range(4)]
        first[rel] = first_kernel(graph, infos[rel], edge_in, node_in, blocks1, after)

    blocks2 = {}
    add_first(0, [])
    if direct:
        lines2 = [first[0].t2] + lined_up(first[0].t2)
        add_first(3, [first[0].stat])
        plan = []
        for k in range(2):
            plan.append((0, k + 1, 0, rows_n, 0, 4 * k * rows_n))
            plan.append((1 + k, None, 0, 3 * rows_n, 0, (4 * k + 1) * rows_n))
        sources = [node_in, node_shared[1], node_shared[2]]
        (cat,) = glue_kernel(graph, infos[0], sources, plan, [8 * rows_n], [first[0].stat])
        node_far[0] = swap(cat)
        add_first(1, [first[3].stat])
        plan = [(r, None, 0, rows_n, 0, r * rows_n) for r in range(4)]
        plan += [(r, None, 0, rows_n, 1, (r - 1) * rows_n) for r in range(1, 4)]
        cat, share = glue_kernel(graph, infos[0], lines2, plan, [4 * rows_n, 3 * rows_n], [first[1].stat])
        far2 = swap(cat)
        shared = {rel: across(share, rel) for rel in range(1, 4)}
        add_first(2, [cat])
        blocks2[0] = as_blocks(lines2, None) + [(far2, None, r * rows_n, rows_n) for r in range(4)]
    else:
        for rel in range(1, 4):
            add_first(rel, [first[rel - 1].stat])
        for rel in range(4):
            blocks2[rel] = as_blocks([lax.all_gather(first[rel].t2, "rows", axis=0, tiled=True)], None)

    def add_second(rel, after):
        before = second.get(rel - 1)
        second[rel] = second_kernel(
            graph, infos[rel], first[rel], blocks2[rel], node_cot, edge_cot, before, rel == 0, direct, after
        )

    def add_third(rel, sums, after):
        before = third[rel - 1] if rel else second[3]
        third[rel] = third_kernel(
            graph, infos[rel], first[rel], second[rel], sums, edge_in, before, rel == 0, direct, after
        )

    add_second(0, [first[2].stat])
    if direct:
        got = swap(second[0].gs[1])
        plan = []
        for k in range(3):
            plan.append((k, None, 0, rows_n, 0, 4 * k * rows_n))
            plan.append((3 + k, None, 0, 3 * rows_n, 0, (4 * k + 1) * rows_n))
        sources = [first[rel].t2 for rel in range(1, 4)] + [shared[rel] for rel in range(1, 4)]
        (cat,) = glue_kernel(graph, infos[0], sources, plan, [12 * rows_n], [second[0].stat])
        far2 = swap(cat)
        for rel in range(1, 4):
            entry = [(first[rel].t2, None, 0, rows_n)] + [(shared[rel], None, r * rows_n, rows_n) for r in range(3)]
            entry += [(far2, None, (4 * (rel - 1) + r) * rows_n, rows_n) for r in range(4)]
            blocks2[rel] = entry
        parts = add_kernel(graph, infos[0], [second[0].gs[0], got], rows_n, [cat])
        sums = [parts[0]] + [along(parts[r], -r) for r in range(1, 4)]
        add_second(1, [parts[0]])
        add_second(2, [])
        add_second(3, [])
    else:
        for rel in range(1, 4):
            add_second(rel, [])
        sums = [lax.psum_scatter(second[0].gs[0], "rows", scatter_dimension=0, tiled=True)]
    add_third(0, sums, [])
    shared = {rel: across(third[0].total, rel) for rel in range(1, 4)}
    if direct:
        parts = add_kernel(graph, infos[0], [third[0].gs[0], swap(third[0].gs[1])], rows_n)
        sums = [parts[0]] + [along(parts[r], -r) for r in range(1, 4)]
        add_third(1, [shared[1]], [parts[0]])
    else:
        add_third(1, [shared[1]], [])
    add_third(2, [shared[2]], [])
    add_third(3, [shared[3]], [])
    last = third[3]
    stats = ([first[rel].stat for rel in range(4)], [second[rel].stat for rel in range(4)])
    packed, piece = pack_kernel(graph, infos[0], last.wg, last.vec, stats, direct, sums if direct else [])
    if direct:
        (total,) = add_kernel(graph, infos[0], sums, rows_n, [packed[0]])
    else:
        total = lax.psum_scatter(third[0].gs[0], "rows", scatter_dimension=0, tiled=True)
    low = [total] + [lax.ppermute(total, "section", [(rel, 0)]) for rel in range(1, 4)]
    zero = node_zero_kernel(
        graph, infos[0], [third[rel].node_part for rel in range(4)], low, last.node_grad, graph.consts["wall"]
    )
    if direct:
        pieces = add_kernel(graph, infos[0], [packed[0], swap(packed[1])], piece)
        row_lines = [pieces[0]] + [along(pieces[r], -r) for r in range(1, 4)]
        (whole,) = add_kernel(graph, infos[0], row_lines, piece, [zero.token])
        row_lines = [whole] + lined_up(whole)
        result = unpack_kernel(graph, infos[0], row_lines, [swap(line) for line in row_lines], piece)
        grads, recv, vec, rms = result.grads, result.recv, result.vec, result.rms
    else:
        full = lax.psum(packed[0], "rows")
        base = 3 * width + 2 * quarter
        grads = [full[k * width : (k + 1) * width] for k in range(3)]
        recv = full[3 * width : base]
        sums = full[base : base + TAIL_ROWS]
        vec = [sums[k : k + 1] for k in range(4)]
        rms = jnp.sqrt(sums[4:8, 0 : 2 * LANES : LANES] / (sums[4:8, 2 * LANES : 2 * LANES + 1] * width))
        rms = jnp.take(rms, jnp.arange(4, dtype=jnp.int32) ^ section, axis=0)
        rms = [rms[:, 0][None], rms[:, 1][None]]
    return (
        second[3].node_out[None],
        second[3].edge_out[None],
        zero.node_grad[None],
        last.edge_grad[None],
        grads[0][None],
        grads[1][None],
        recv.reshape(2, quarter, width),
        vec[0],
        grads[2][None],
        vec[1],
        vec[2],
        vec[3],
        rms[0],
        rms[1],
    )


def solution(mesh):
    whole = P("section", None, None)
    line = P("section", None)
    latents = P(None, "rows", None)
    outs = P("section", None, "rows", None)
    recv = P(None, "section", None)
    ends = P("rows")
    return jax.shard_map(
        on_device,
        mesh=mesh,
        in_specs=(latents,) * 4 + (whole, whole, recv, line, whole, line, line, line) + (ends,) * 4,
        out_specs=(outs,) * 4 + (whole, whole, recv, line, whole, line, line, line, line, line),
        check_vma=False,
    )
```

```python
import types

import jax
import jax.numpy as jnp
from jax import lax
from jax.experimental import pallas as pl
from jax.experimental.pallas import tpu as pltpu
from jax.sharding import PartitionSpec as P

F32 = jnp.float32
BF = jnp.bfloat16
CHUNK = 512
LANES = 128
VEC_ROWS = 16
ANY = pl.ANY
VMEM = pltpu.VMEM
HBM = pltpu.HBM


def dot(left, right):
    return jnp.dot(left, right, preferred_element_type=F32)


def dot_nt(left, right):
    return lax.dot_general(left, right, (((1,), (1,)), ((), ())), preferred_element_type=F32)


def dot_tn(left, right):
    return lax.dot_general(left, right, (((0,), (0,)), ((), ())), preferred_element_type=F32)


def sigmoid(value):
    return 0.5 * jnp.tanh(0.5 * value) + 0.5


def widen(column, width):
    return jnp.concatenate([column] * (width // column.shape[1]), axis=1)


def col_sum(value):
    return jnp.sum(value, axis=0, keepdims=True)


def tail(pre_act, weight_out, vecs):
    hidden = (pre_act * sigmoid(pre_act)).astype(BF)
    update = dot(hidden, weight_out) + vecs[1]
    mean = jnp.mean(update, axis=-1, keepdims=True)
    centre = update - mean
    spread = jnp.mean(centre * centre, axis=-1, keepdims=True)
    inverse = lax.rsqrt(spread + 1e-05)
    scaled = centre * inverse
    return hidden, scaled, inverse, spread + mean * mean, scaled * vecs[2] + vecs[3]


def norm_back(grad_normed, scaled, inverse, gain):
    weighted = grad_normed * gain
    mean_grad = jnp.mean(weighted, axis=-1, keepdims=True)
    mean_both = jnp.mean(weighted * scaled, axis=-1, keepdims=True)
    return inverse * (weighted - mean_grad - scaled * mean_both)


def silu_back(grad_hidden, pre_act):
    sig = sigmoid(pre_act)
    return grad_hidden * (sig * (1.0 + pre_act * (1.0 - sig))), sig


class Info:
    def __init__(self, table, rel):
        self.table, self.rel = table, rel

    def __getitem__(self, k):
        return self.table[self.rel, k]


V, H, A, B = range(4)
PLACES = (VMEM, HBM, pl.ANY, None)


def flat(entries):
    return [item for entry in entries.values() for item in (entry if isinstance(entry, list) else [entry])]


def named(entries, items):
    return {
        name: [next(items) for _ in entry] if isinstance(entry, list) else next(items)
        for name, entry in entries.items()
    }


def run_kernel(body, info, inputs, outputs, scratch, micros, limit):
    given, made = flat(inputs), flat(outputs)
    aliases = {}
    for index, entry in enumerate(made):
        if entry[3] is not None:
            aliases[1 + [array is entry[3] for array, _ in given].index(True)] = index

    def kernel(*refs):
        rest = iter(refs[1:])
        groups = [named(entries, rest) for entries in (inputs, outputs, scratch)]
        body(types.SimpleNamespace(info=Info(refs[0], info.rel), **groups[0], **groups[1], **groups[2]))

    arrays = [pltpu.with_memory_space_constraint(array, PLACES[kind]) for array, kind in given]
    results = pl.pallas_call(
        kernel,
        out_shape=[
            jax.ShapeDtypeStruct(entry[0], entry[1]) if entry[2] >= A else PLACES[entry[2]](entry[0], entry[1])
            for entry in made
        ],
        in_specs=[pl.BlockSpec(memory_space=pltpu.SMEM)] + [pl.BlockSpec(memory_space=PLACES[kind]) for _, kind in given],
        out_specs=[pl.BlockSpec() if entry[2] == B else pl.BlockSpec(memory_space=PLACES[entry[2]]) for entry in made],
        scratch_shapes=flat(scratch),
        input_output_aliases=aliases,
        compiler_params=pltpu.CompilerParams(vmem_limit_bytes=limit * 1024 * 1024),
        cost_estimate=pl.CostEstimate(flops=int(micros * 1.15e9), bytes_accessed=0, transcendentals=0),
    )(info.table, *arrays)
    return types.SimpleNamespace(**named(outputs, iter(results)))


def copy(source, target, sem):
    return pltpu.make_async_copy(source, target, sem)


def either(arrays):
    return [(array, A) for array in arrays]


class Graph:
    def __init__(self, rows_n, rows_e, blocks, width):
        self.rows_n, self.rows_e, self.blocks, self.width = rows_n, rows_e, blocks, width
        self.cap = rows_e // blocks
        self.chunk = min(CHUNK, rows_e)
        self.starts = range(0, rows_e, self.chunk)
        self.consts = {}

    def const_inputs(self):
        return {name: (array, V) for name, array in self.consts.items()}

    def weight_row(self, section_id, part):
        return (section_id * 3 + part) * self.width

    def weight(self, R, section_id, part, count=1):
        return R.wall[pl.ds(self.weight_row(section_id, part), count * self.width), :]

    def recv_weight(self, R, layer):
        return R.wall[pl.ds((12 + layer) * self.width, self.width), :]

    def vectors(self, R, section_id):
        block = R.wall[pl.ds(14 * self.width + section_id * VEC_ROWS, VEC_ROWS), :].astype(F32)
        return [block[k : k + 1] + block[4 + k : 5 + k] for k in range(4)]


OWN, OTHER, OUT = 0, 1, 2


def half_rows(width):
    half, eighth = width // 2, width // 8
    return half, eighth, 3 * half + 2 * eighth, 3 * half + 2 * eighth + VEC_ROWS


def half_kernel(graph, info, weights, recv, vecs):
    half, eighth, vec_row, rows = half_rows(graph.width)
    quarter = 2 * eighth

    def body(R):
        core, stage = R.info[1], R.half
        for k in range(3):
            source = R.weights[k].at[pl.ds(pl.multiple_of(core * half, half), half)]
            copy(source, stage.at[pl.ds(k * half, half)], R.sem).start()
        for layer in range(2):
            source = R.recv.at[pl.ds(pl.multiple_of(layer * quarter + core * eighth, eighth), eighth)]
            copy(source, stage.at[pl.ds(3 * half + layer * eighth, eighth)], R.sem).start()
        for k in range(4):
            copy(R.vecs[k], R.rows.at[pl.ds(k, 1)], R.row_sem).start()
        copy(R.rows, R.rows, R.row_sem).wait()
        rows_here = R.rows[...]
        high = rows_here.astype(BF)
        low = (rows_here - high.astype(F32)).astype(BF)
        stage[vec_row : vec_row + VEC_ROWS, :] = jnp.concatenate([high, low, high, low], axis=0)
        loaded = stage.at[pl.ds(0, vec_row)]
        copy(loaded, loaded, R.sem).wait()

    inputs = dict(weights=[(array, H) for array in weights], recv=(recv, H), vecs=[(array, H) for array in vecs])
    outputs = dict(half=((rows, graph.width), BF, V, None))
    scratch = dict(
        rows=VMEM((4, graph.width), F32),
        sem=pltpu.SemaphoreType.DMA,
        row_sem=pltpu.SemaphoreType.DMA,
    )
    return run_kernel(body, info, inputs, outputs, scratch, 1, 2).half


def wall_kernel(graph, info, weights, recv, mine, near, far):
    width = graph.width
    half, eighth, vec_row, rows = half_rows(width)
    quarter = 2 * eighth
    pieces = [piece for side in (near, far) for rel in range(1, 4) for piece in side[rel]]
    inputs = dict(
        weights=[(array, H) for array in weights], recv=(recv, H), mine=(mine, A), pieces=either([p[0] for p in pieces])
    )
    total = 14 * width + 4 * VEC_ROWS

    def body(R):
        section, core = R.info[0], R.info[1]
        wall, sem = R.wall, R.sem
        refs = iter(R.pieces)

        def put(source, row, count, unit):
            copy(source, wall.at[pl.ds(pl.multiple_of(row, unit), count)], sem).start()

        for k in range(3):
            put(R.weights[k], section * 3 * width + k * width, width, width)
        for layer in range(2):
            put(R.recv.at[pl.ds(layer * quarter, quarter)], (12 + layer) * width + section * quarter, quarter, quarter)
        put(R.mine.at[pl.ds(vec_row, VEC_ROWS)], 14 * width + section * VEC_ROWS, VEC_ROWS, VEC_ROWS)
        for side, pieces_of in ((core, near), (1 - core, far)):
            for rel in range(1, 4):
                there = section ^ rel
                parts = [(k * half, half, (there * 3 + k) * width + side * half) for k in range(3)]
                parts += [
                    (3 * half + layer * eighth, eighth, (12 + layer) * width + there * quarter + side * eighth)
                    for layer in range(2)
                ]
                if pieces_of is near:
                    parts.append((vec_row, VEC_ROWS, 14 * width + there * VEC_ROWS))
                first = 0
                for _, begin, held in pieces_of[rel]:
                    ref = next(refs)
                    for row, count, target in parts:
                        low, high = max(row, first), min(row + count, first + held)
                        if low < high:
                            put(ref.at[pl.ds(begin + low - first, high - low)], target + low - row, high - low, 16)
                    first += held
        copy(wall, wall, sem).wait()

    outputs = dict(wall=((total, width), BF, V, None))
    return run_kernel(body, info, inputs, outputs, dict(sem=pltpu.SemaphoreType.DMA), 3, 1).wall


def glue_kernel(graph, info, sources, plan, rows, after=()):
    width = graph.width
    inputs = dict(source=[(array, H if array.ndim > 2 else A) for array in sources], after=either(after))
    outputs = dict(out=[((count, width), BF, A, None) for count in rows])
    scratch = dict(sem=pltpu.SemaphoreType.DMA((len(rows),)))

    def body(R):
        for source, index, row, count, target, place in plan:
            ref = R.source[source] if index is None else R.source[source].at[R.info[0] ^ index]
            copy(ref.at[pl.ds(row, count)], R.out[target].at[pl.ds(place, count)], R.sem.at[target]).start()
        for k, out in enumerate(R.out):
            copy(out, out, R.sem.at[k]).wait()

    return run_kernel(body, info, inputs, outputs, scratch, 2, 1).out


def summed_rows(stages, here):
    total = stages[0][here, :].astype(F32)
    for other in stages[1:]:
        total = total + other[here, :].astype(F32)
    return total.astype(BF)


def add_kernel(graph, info, arrays, rows, after=()):
    count, width = arrays[0].shape
    inputs = dict(source=[(array, V) for array in arrays], after=either(after))
    outputs = dict(out=[((rows, width), BF, V, None)] * (count // rows))

    def body(R):
        for k in range(count // rows):
            R.out[k][...] = summed_rows(R.source, slice(k * rows, (k + 1) * rows))

    return run_kernel(body, info, inputs, outputs, {}, 2, 4).out


def node_zero_kernel(graph, info, parts, sums, node_grad, wall):
    rows_n, width = graph.rows_n, graph.width
    inputs = dict(
        parts=[(array, V) for array in parts], sums=[(array, V) for array in sums], old=(node_grad, H), wall=(wall, V)
    )
    outputs = dict(node_grad=(node_grad.shape, BF, H, node_grad), token=((8, LANES), F32, V, None))
    scratch = dict(total=VMEM((4, rows_n, width), BF), sem=pltpu.SemaphoreType.DMA)

    def body(R):
        R.token[...] = jnp.zeros_like(R.token)

        @pl.when(R.info[0] == 0)
        def _():
            for k in range(4):
                R.total[k] = (R.parts[k][...] + dot_nt(R.sums[k][...], graph.weight(R, 0, OTHER))).astype(BF)
            move = copy(R.total, R.node_grad, R.sem)
            move.start()
            move.wait()

    return run_kernel(body, info, inputs, outputs, scratch, 2, 6)


def const_kernel(graph, info, arrays):
    inputs = dict(source=[(array, H) for array in arrays])
    outputs = dict(out=[(array.shape, array.dtype, V, None) for array in arrays])

    def body(R):
        moves = [copy(source, out, R.sem.at[k]) for k, (source, out) in enumerate(zip(R.source, R.out))]
        for move in moves:
            move.start()
        for move in moves:
            move.wait()

    scratch = dict(sem=pltpu.SemaphoreType.DMA((len(arrays),)))
    return run_kernel(body, info, inputs, outputs, scratch, 2, 1).out


def block_inputs(blocks):
    return [(array, V) for array in block_arrays(blocks)]


def block_arrays(blocks):
    arrays = []
    for array, _, _ in blocks:
        if array is not None and all(array is not other for other in arrays):
            arrays.append(array)
    return arrays


def each_block(graph, R, blocks, work):
    arrays = block_arrays(blocks)
    cap, rows_n = graph.cap, graph.rows_n
    if len(arrays) == 1:

        @pl.loop(0, graph.blocks)
        def _(place):
            nodes = pl.ds(pl.multiple_of(place * rows_n, rows_n), rows_n)
            work(pl.ds(pl.multiple_of(place * cap, cap), cap), R.block[0][nodes, :])

        return
    for place, (array, index, row) in enumerate(blocks):
        nodes = pl.ds(row, rows_n)
        if array is None:
            block = R.node0[...]
        else:
            block = R.block[[array is other for other in arrays].index(True)][nodes, :]
        work(pl.ds(pl.multiple_of(R.info[3 + place] * cap, cap), cap), block)


def stat_pair(square, stream, mask):
    branch = col_sum(mask * square)
    total = col_sum(mask * jnp.sum(stream * stream, axis=-1, keepdims=True))
    return branch, total


def put_stats(stat, pairs, width):
    branch, total = pairs[0]
    for pair in pairs[1:]:
        branch, total = branch + pair[0], total + pair[1]
    stat[0:1, :] = jnp.broadcast_to(branch * width, (1, LANES))
    stat[1:2, :] = jnp.broadcast_to(total, (1, LANES))


def first_kernel(graph, info, edge_in, node_in, blocks, after):
    rows_e, rows_n, width = graph.rows_e, graph.rows_n, graph.width
    inputs = dict(
        edges=(edge_in, H), nodes=(node_in, H), block=block_inputs(blocks), after=either(after), **graph.const_inputs()
    )
    rows = ((rows_e, width), BF, V, None)
    few = ((rows_n, width), BF, V, None)
    outputs = dict(
        edge1=rows,
        z0=rows,
        x0=rows,
        q0=((rows_e, LANES), F32, V, None),
        s0=rows,
        node0=few,
        node1=few,
        g1=few,
        z1=few,
        x1=few,
        q1=((rows_n, LANES), F32, V, None),
        stat=((8, LANES), F32, V, None),
        t2=few,
    )
    scratch = dict(edge=VMEM((rows_e, width), BF), sem=pltpu.SemaphoreType.DMA((2,)))

    def body(R):
        info = R.info
        section, micro = info[0], info[2]
        node_copy = copy(R.nodes.at[micro], R.node0, R.sem.at[0])
        edge_copy = copy(R.edges.at[micro], R.edge, R.sem.at[1])
        node_copy.start()
        edge_copy.start()

        def send_rows(edges, block):
            R.s0[edges, :] = dot(R.ohs[edges, :], block).astype(BF)

        node_copy.wait()
        each_block(graph, R, blocks, send_rows)
        node = R.node0[...]
        vecs = graph.vectors(R, 0)
        recv_node = (dot(node, graph.recv_weight(R, 0)) + vecs[0]).astype(BF)
        edge_copy.wait()
        pairs = []
        for start in graph.starts:
            rows = pl.ds(start, graph.chunk)
            mask = R.emask[rows, :]
            edge = R.edge[rows, :]
            pre_act = dot(jnp.concatenate([edge, R.s0[rows, :]], axis=1), graph.weight(R, 0, OWN, 2))
            pre_act = pre_act + dot(R.ohr[rows, :], recv_node)
            hidden, scaled, inverse, square, normed = tail(pre_act, graph.weight(R, 0, OUT), vecs)
            stream = edge.astype(F32) + widen(mask, width) * normed
            R.edge1[rows, :] = stream.astype(BF)
            R.z0[rows, :] = pre_act.astype(BF)
            R.x0[rows, :] = scaled.astype(BF)
            R.q0[rows, :] = jnp.broadcast_to(inverse, (graph.chunk, LANES))
            pairs.append(stat_pair(square, stream, mask[:, :1]))
        summed = dot(R.ohrt[...], R.edge1[...]).astype(BF)
        R.g1[...] = summed
        vecs = graph.vectors(R, 1)
        pre_act = dot(jnp.concatenate([node, summed], axis=1), graph.weight(R, 1, OWN, 2)) + vecs[0]
        hidden, scaled, inverse, square, normed = tail(pre_act, graph.weight(R, 1, OUT), vecs)
        nmask = R.nmask[...]
        stream = node.astype(F32) + widen(nmask, width) * normed
        low = stream.astype(BF)
        R.t2[...] = dot(low, graph.weight(R, 2, OTHER)).astype(BF)
        R.node1[...] = low
        R.z1[...] = pre_act.astype(BF)
        R.x1[...] = scaled.astype(BF)
        R.q1[...] = jnp.broadcast_to(inverse, (rows_n, LANES))

        @pl.when(section == 0)
        def _():
            put_stats(R.stat, pairs, width)

        @pl.when(section != 0)
        def _():
            put_stats(R.stat, [stat_pair(square, stream, nmask[:, :1])], width)

    return run_kernel(body, info, inputs, outputs, scratch, 8, 10 if graph.blocks <= 8 else 20)


def sender_outputs(graph, direct):
    rows = graph.blocks * graph.rows_n
    if direct:
        return dict(gs=[((rows // 2, graph.width), BF, V, None)] * 2)
    return dict(gs=[((rows, graph.width), BF, A, None)])


def sender_sums(graph, R, grads):
    each = graph.blocks // len(R.gs)
    if each == graph.blocks:

        @pl.loop(0, each)
        def _(place):
            rows = pl.ds(pl.multiple_of(place * graph.cap, graph.cap), graph.cap)
            here = pl.ds(pl.multiple_of(place * graph.rows_n, graph.rows_n), graph.rows_n)
            R.sums_here[...] = dot_tn(R.ohs[rows, :], grads[rows, :]).astype(BF)
            move = copy(R.sums_here, R.gs[0].at[here], R.sums_sem)
            move.start()
            move.wait()

        return
    for place in range(graph.blocks):
        rows = pl.ds(pl.multiple_of(R.info[3 + place] * graph.cap, graph.cap), graph.cap)
        here = pl.ds(place % each * graph.rows_n, graph.rows_n)
        R.gs[place // each][here, :] = dot_tn(R.ohs[rows, :], grads[rows, :]).astype(BF)


def add_recv(graph, R, layer, node, grad_recv):
    quarter = graph.width // 4
    start = pl.multiple_of(R.info[0] * quarter, quarter)
    rows = pl.ds(3 * graph.width + layer * quarter, quarter)
    R.wg[rows, :] += dot_tn(node[:, pl.ds(start, quarter)], grad_recv)


def second_kernel(graph, info, first, blocks, node_cot, edge_cot, before, own_first, direct, after):
    rows_e, rows_n, width = graph.rows_e, graph.rows_n, graph.width
    micro_count = node_cot.shape[0]
    inputs = dict(
        edge1=(first.edge1, V),
        node0=(first.node0, V),
        node1=(first.node1, V),
        edge_cot=(edge_cot, H),
        node_cot=(node_cot, H),
        block=block_inputs(blocks),
        after=either(after),
        **graph.const_inputs(),
    )
    chain = [None] * 5
    if before is not None:
        chain = [before.edge_out, before.node_out, before.edge_grad, before.wg, before.vec]
        inputs.update(old=[(array, kind) for array, kind in zip(chain, (H, H, H, V, V))])
    rows = VMEM((rows_e, width), BF)
    few = VMEM((rows_n, width), BF)
    outputs = dict(
        edge_out=((micro_count, rows_e, width), BF, H, chain[0]),
        node_out=((micro_count, rows_n, width), BF, H, chain[1]),
        edge_grad=((micro_count, rows_e, width), BF, H, chain[2]),
        wg=((3 * width + width // 2, width), F32, V, chain[3]),
        vec=((8, width), F32, V, chain[4]),
        eg2=((rows_e, width), BF, V, None),
        ng=((rows_n, width), BF, V, None),
        gr=((rows_n, width), BF, V, None),
        stat=((8, LANES), F32, V, None),
    )
    if own_first:
        outputs.update(sender_outputs(graph, direct))
    scratch = dict(
        ends=VMEM((rows_e, width), F32),
        cot=rows,
        ncot=few,
        edge2=rows,
        eg=rows,
        node_here=few,
        z=rows,
        x=rows,
        q=VMEM((rows_e, LANES), F32),
        a=rows,
        gu=rows,
        gz=rows,
        sem=pltpu.SemaphoreType.DMA((8,)),
    )
    if own_first and not direct:
        scratch.update(sums_here=few, sums_sem=pltpu.SemaphoreType.DMA)

    def body(R):
        info = R.info
        section, micro = info[0], info[2]
        sem = R.sem
        cot_copy = copy(R.edge_cot.at[micro], R.cot, sem.at[1])
        ncot_copy = copy(R.node_cot.at[micro], R.ncot, sem.at[2])
        ncot_copy.start()
        cot_copy.start()
        if own_first:
            R.wg[...] = jnp.zeros_like(R.wg)
            R.vec[...] = jnp.zeros_like(R.vec)
        node = R.node1[...]
        vecs = graph.vectors(R, 2)
        recv_node = (dot(node, graph.recv_weight(R, 1)) + vecs[0]).astype(BF)

        def end_rows(edges, block):
            onehot = jnp.concatenate([R.ohs[edges, :], R.ohr[edges, :]], axis=1)
            R.ends[edges, :] = dot(onehot, jnp.concatenate([block, recv_node], axis=0))

        each_block(graph, R, blocks, end_rows)
        pairs = []
        for start in graph.starts:
            rows = pl.ds(start, graph.chunk)
            mask = R.emask[rows, :]
            edge = R.edge1[rows, :]
            pre_act = dot(edge, graph.weight(R, 2, OWN)) + R.ends[rows, :]
            hidden, scaled, inverse, square, normed = tail(pre_act, graph.weight(R, 2, OUT), vecs)
            stream = edge.astype(F32) + widen(mask, width) * normed
            R.edge2[rows, :] = stream.astype(BF)
            R.z[rows, :] = pre_act.astype(BF)
            R.x[rows, :] = scaled.astype(BF)
            R.q[rows, :] = jnp.broadcast_to(inverse, (graph.chunk, LANES))
            R.a[rows, :] = hidden
            pairs.append(stat_pair(square, stream, mask[:, :1]))

        @pl.when(section >= 2)
        def _():
            copy(R.edge2, R.edge_out.at[micro], sem.at[3]).start()

        @pl.when(section < 2)
        def _():
            copy(R.edge1, R.edge_out.at[micro], sem.at[3]).start()

        vecs = graph.vectors(R, 3)
        summed = dot(R.ohrt[...], R.edge2[...]).astype(BF)
        weight_out = graph.weight(R, 3, OUT)
        pre_act = dot(jnp.concatenate([node, summed], axis=1), graph.weight(R, 3, OWN, 2)) + vecs[0]
        hidden, scaled, inverse, square, normed = tail(pre_act, weight_out, vecs)
        nmask = R.nmask[...]
        wide_mask = widen(nmask, width)
        stream = node.astype(F32) + wide_mask * normed
        R.node_here[...] = jnp.where(
            section == 0, R.node0[...], jnp.where(section == 3, stream.astype(BF), node)
        )
        node_copy = copy(R.node_here, R.node_out.at[micro], sem.at[4])
        node_copy.start()

        @pl.when(section == 3)
        def _():
            put_stats(R.stat, [stat_pair(square, stream, nmask[:, :1])], width)

        @pl.when(section != 3)
        def _():
            put_stats(R.stat, pairs, width)

        ncot_copy.wait()
        grad = R.ncot[...].astype(F32)
        grad_normed = wide_mask * grad
        grad_update = norm_back(grad_normed, scaled, inverse, vecs[2])
        grad_low = grad_update.astype(BF)
        grad_pre, _ = silu_back(dot_nt(grad_low, weight_out), pre_act)
        pre_low = grad_pre.astype(BF)
        R.ng[...] = (grad + dot_nt(pre_low, graph.weight(R, 3, OWN))).astype(BF)
        grad_sum = dot_nt(pre_low, graph.weight(R, 3, OTHER))
        grad_high = grad_sum.astype(BF)
        grad_both = jnp.concatenate([grad_high, (grad_sum - grad_high.astype(F32)).astype(BF)], axis=0)

        @pl.when(section == 3)
        def _():
            R.wg[0:width, :] += dot_tn(node, pre_low)
            R.wg[width : 2 * width, :] += dot_tn(summed, pre_low)
            R.wg[2 * width : 3 * width, :] += dot_tn(hidden, grad_low)
            R.vec[0:1, :] += col_sum(grad_pre)
            R.vec[1:2, :] += col_sum(grad_update)
            R.vec[2:3, :] += col_sum(grad_normed * scaled)
            R.vec[3:4, :] += col_sum(grad_normed)

        cot_copy.wait()
        vecs = graph.vectors(R, 2)

        def arriving(rows, mask):
            onehot = R.ohr[rows, :]
            spread = dot(jnp.concatenate([onehot, onehot], axis=1), grad_both)
            return (R.cot[rows, :].astype(F32) + mask * spread).astype(BF)

        def edge_back(sums):
            totals = [jnp.zeros((1, width), F32)] * 4
            for start in graph.starts:
                rows = pl.ds(start, graph.chunk)
                mask = R.emask[rows, :]
                low = arriving(rows, widen(mask, width))
                R.eg[rows, :] = low
                wide = low.astype(F32)
                scaled = R.x[rows, :].astype(F32)
                pre_act = R.z[rows, :].astype(F32)
                inverse = widen(R.q[rows, :] * mask, width)
                grad_update = norm_back(wide, scaled, inverse, vecs[2])
                grad_low = grad_update.astype(BF)
                grad_pre, _ = silu_back(dot_nt(grad_low, graph.weight(R, 2, OUT)), pre_act)
                pre_low = grad_pre.astype(BF)
                R.gz[rows, :] = pre_low
                R.eg2[rows, :] = (wide + dot_nt(pre_low, graph.weight(R, 2, OWN))).astype(BF)
                if sums:
                    R.gu[rows, :] = grad_low
                    normed = widen(mask, width) * wide
                    parts = (grad_pre, grad_update, normed * scaled, normed)
                    totals = [total + col_sum(part) for total, part in zip(totals, parts)]
            if sums:
                R.wg[0:width, :] += dot_tn(R.edge1[...], R.gz[...])
                R.wg[2 * width : 3 * width, :] += dot_tn(R.a[...], R.gu[...])
                for k in range(4):
                    R.vec[k : k + 1, :] += totals[k]

        @pl.when(section == 2)
        def _():
            edge_back(True)

        @pl.when(section != 2)
        def _():
            edge_back(False)

        @pl.when(section == 2)
        def _():
            copy(R.eg2, R.edge_grad.at[micro], sem.at[6]).start()

        @pl.when(section == 3)
        def _():
            copy(R.eg, R.edge_grad.at[micro], sem.at[6]).start()

        grad_recv = dot(R.ohrt[...], R.gz[...]).astype(BF)
        R.gr[...] = grad_recv
        add_recv(graph, R, 1, R.node1, grad_recv)
        if own_first:
            sender_sums(graph, R, R.gz)
        node_copy.wait()
        copy(R.edge2, R.edge_out.at[micro], sem.at[3]).wait()

        @pl.when(section >= 2)
        def _():
            copy(R.eg, R.edge_grad.at[micro], sem.at[6]).wait()

    return run_kernel(body, info, inputs, outputs, scratch, 14, 18 if graph.blocks <= 8 else 28)


def third_kernel(graph, info, first, second, sums, edge_in, before, own_first, direct, after):
    rows_e, rows_n, width = graph.rows_e, graph.rows_n, graph.width
    inputs = dict(
        second=[(array, V) for array in (second.eg2, second.ng, second.gr)],
        z0=(first.z0, V),
        x0=(first.x0, V),
        q0=(first.q0, V),
        s0=(first.s0, V),
        node0=(first.node0, V),
        node1=(first.node1, V),
        g1=(first.g1, V),
        z1=(first.z1, V),
        x1=(first.x1, V),
        q1=(first.q1, V),
        sums=[(array, V) for array in sums],
        edges=(edge_in, H),
        after=either(after),
        **graph.const_inputs(),
    )
    node_grad = None if own_first else before.node_grad
    chain = [(before.edge_grad, H), (before.wg, V), (before.vec, V)]
    inputs.update(old=chain if own_first else chain + [(node_grad, H)])
    micro_count = before.edge_grad.shape[0]
    rows = VMEM((rows_e, width), BF)
    few = VMEM((rows_n, width), BF)
    outputs = dict(
        edge_grad=(before.edge_grad.shape, BF, H, before.edge_grad),
        node_grad=((micro_count, rows_n, width), BF, H, node_grad),
        wg=(before.wg.shape, F32, V, before.wg),
        vec=(before.vec.shape, F32, V, before.vec),
        node_part=((rows_n, width), F32, V, None),
        token=((8, LANES), F32, V, None),
    )
    if own_first:
        outputs.update(sender_outputs(graph, direct))
        outputs.update(total=((rows_n, width), BF, V, None))
    scratch = dict(
        edge=rows,
        out_edge=rows,
        out_node=few,
        gu=rows,
        a=rows,
        gz=rows,
        sem=pltpu.SemaphoreType.DMA((4,)),
    )
    if own_first and not direct:
        scratch.update(sums_here=few, sums_sem=pltpu.SemaphoreType.DMA)

    def body(R):
        info = R.info
        section, micro = info[0], info[2]
        sem = R.sem
        eg2, ng, gr = R.second
        R.token[...] = jnp.zeros_like(R.token)
        edge_copy = copy(R.edges.at[micro], R.edge, sem.at[1])

        @pl.when(section == 0)
        def _():
            edge_copy.start()

        if own_first:
            R.total[...] = summed_rows(R.sums, slice(None))
        gs2 = (R.total if own_first else R.sums[0])[...]
        grad_mid = (
            ng[...].astype(F32) + dot_nt(gr[...], graph.recv_weight(R, 1)) + dot_nt(gs2, graph.weight(R, 2, OTHER))
        ).astype(BF)
        R.out_node[...] = jnp.where(section == 3, ng[...], grad_mid)

        @pl.when(section == 2)
        def _():
            R.wg[width : 2 * width, :] += dot_tn(R.node1[...], gs2)

        vecs = graph.vectors(R, 1)
        wide = grad_mid.astype(F32)
        grad_normed = widen(R.nmask[...], width) * wide
        scaled = R.x1[...].astype(F32)
        pre_act = R.z1[...].astype(F32)
        grad_update = norm_back(grad_normed, scaled, widen(R.q1[...], width), vecs[2])
        grad_low = grad_update.astype(BF)
        grad_pre, sig = silu_back(dot_nt(grad_low, graph.weight(R, 1, OUT)), pre_act)
        pre_low = grad_pre.astype(BF)
        grad_node = (wide + dot_nt(pre_low, graph.weight(R, 1, OWN))).astype(BF)
        grad_sum = dot_nt(pre_low, graph.weight(R, 1, OTHER))
        grad_high = grad_sum.astype(BF)
        grad_both = jnp.concatenate([grad_high, (grad_sum - grad_high.astype(F32)).astype(BF)], axis=0)

        @pl.when(section == 1)
        def _():
            R.out_node[...] = grad_node
            R.wg[0:width, :] += dot_tn(R.node0[...], pre_low)
            R.wg[width : 2 * width, :] += dot_tn(R.g1[...], pre_low)
            R.wg[2 * width : 3 * width, :] += dot_tn((pre_act * sig).astype(BF), grad_low)
            R.vec[0:1, :] += col_sum(grad_pre)
            R.vec[1:2, :] += col_sum(grad_update)
            R.vec[2:3, :] += col_sum(grad_normed * scaled)
            R.vec[3:4, :] += col_sum(grad_normed)

        vecs = graph.vectors(R, 0)

        def arriving(rows, mask):
            onehot = R.ohr[rows, :]
            spread = dot(jnp.concatenate([onehot, onehot], axis=1), grad_both)
            return (eg2[rows, :].astype(F32) + mask * spread).astype(BF)

        def edge_back(sums):
            totals = [jnp.zeros((1, width), F32)] * 4
            for start in graph.starts:
                rows = pl.ds(start, graph.chunk)
                mask = R.emask[rows, :]
                wide = arriving(rows, widen(mask, width)).astype(F32)
                scaled = R.x0[rows, :].astype(F32)
                pre_act = R.z0[rows, :].astype(F32)
                inverse = widen(R.q0[rows, :] * mask, width)
                grad_update = norm_back(wide, scaled, inverse, vecs[2])
                grad_low = grad_update.astype(BF)
                grad_pre, sig = silu_back(dot_nt(grad_low, graph.weight(R, 0, OUT)), pre_act)
                pre_low = grad_pre.astype(BF)
                R.gz[rows, :] = pre_low
                if sums:
                    R.out_edge[rows, :] = (wide + dot_nt(pre_low, graph.weight(R, 0, OWN))).astype(BF)
                    R.gu[rows, :] = grad_low
                    R.a[rows, :] = (pre_act * sig).astype(BF)
                    normed = widen(mask, width) * wide
                    parts = (grad_pre, grad_update, normed * scaled, normed)
                    totals = [total + col_sum(part) for total, part in zip(totals, parts)]
            return totals

        @pl.when(section == 0)
        def _():
            totals = edge_back(True)
            copy(R.out_edge, R.edge_grad.at[micro], sem.at[2]).start()
            edge_copy.wait()
            R.wg[0:width, :] += dot_tn(R.edge[...], R.gz[...])
            R.wg[width : 2 * width, :] += dot_tn(R.s0[...], R.gz[...])
            R.wg[2 * width : 3 * width, :] += dot_tn(R.a[...], R.gu[...])
            for k in range(4):
                R.vec[k : k + 1, :] += totals[k]

        @pl.when(section == 1)
        def _():
            for start in graph.starts:
                rows = pl.ds(start, graph.chunk)
                R.out_edge[rows, :] = arriving(rows, widen(R.emask[rows, :], width))
            copy(R.out_edge, R.edge_grad.at[micro], sem.at[2]).start()

        @pl.when(section > 0)
        def _():
            edge_back(False)

        grad_recv = dot(R.ohrt[...], R.gz[...]).astype(BF)
        add_recv(graph, R, 0, R.node0, grad_recv)

        @pl.when(section == 0)
        def _():
            R.node_part[...] = grad_node.astype(F32) + dot_nt(grad_recv, graph.recv_weight(R, 0))

        node_copy = copy(R.out_node, R.node_grad.at[micro], sem.at[3])
        node_copy.start()
        if own_first:
            sender_sums(graph, R, R.gz)
        node_copy.wait()

        @pl.when(section < 2)
        def _():
            copy(R.out_edge, R.edge_grad.at[micro], sem.at[2]).wait()

    return run_kernel(body, info, inputs, outputs, scratch, 10, 13 if graph.blocks <= 8 else 16)


PIECES = 8
TAIL_ROWS = 16


def stats_block(graph, R):
    section = R.info[0]
    edge_count = col_sum(R.emask[...])
    node_count = col_sum(R.nmask[...])
    even = (section & 1) == 0
    valid = jnp.where(even, edge_count, node_count)
    rows = [R.vec[0:4, :]]
    for k in range(4):
        pair = jnp.where(section < 2, R.first[k][0:2, :], R.second[k][0:2, :])
        rows.append(jnp.concatenate([pair[0:1], pair[1:2], valid, jnp.zeros_like(valid)], axis=1))
    rows.append(jnp.zeros((TAIL_ROWS - 8, graph.width), F32))
    return jnp.concatenate(rows, axis=0)


def pack_kernel(graph, info, wg, vec, stats, direct, after):
    width = graph.width
    held = wg.shape[0]
    piece = -(-(held + TAIL_ROWS) // (16 * PIECES)) * 16
    inputs = dict(
        wg=(wg, V),
        vec=(vec, V),
        emask=(graph.consts["emask"], V),
        nmask=(graph.consts["nmask"], V),
        first=[(stat, V) for stat in stats[0]],
        second=[(stat, V) for stat in stats[1]],
        after=either(after),
    )
    low = BF if direct else F32
    count = 2 if direct else 1
    outputs = dict(out=[((PIECES * piece // count, width), low, V, None)] * count)
    scratch = dict(stage=VMEM((PIECES * piece, width), low))

    def body(R):
        info = R.info
        core = info[1]
        R.stage[0:held, :] = R.wg[...].astype(low)
        R.stage[held : held + TAIL_ROWS, :] = stats_block(graph, R).astype(low)
        rest = PIECES * piece - held - TAIL_ROWS
        if rest:
            R.stage[held + TAIL_ROWS :, :] = jnp.zeros((rest, width), low)
        if direct:
            for k, side in ((1, 1 - core), (0, core)):
                for r in range(4):
                    line = lax.shift_right_logical(info[3 + r], 1)
                    start = pl.multiple_of((side * 4 + line) * piece, 16)
                    R.out[k][r * piece : (r + 1) * piece, :] = R.stage[pl.ds(start, piece), :]
        else:
            R.out[0][...] = R.stage[...]

    return run_kernel(body, info, inputs, outputs, scratch, 3, 8 if direct else 12).out, piece


def unpack_kernel(graph, info, mine, far, piece):
    width = graph.width
    quarter = width // 4
    inputs = dict(mine=[(array, V) for array in mine], far=[(array, V) for array in far])
    big = ((width, width), F32, H, None)
    outputs = dict(
        grads=[big] * 3,
        recv=((2 * quarter, width), F32, H, None),
        vec=[((1, width), F32, B, None)] * 4,
        rms=[((1, 4), F32, B, None)] * 2,
    )
    scratch = dict(
        wide=VMEM((PIECES * piece, width), F32),
        sem=pltpu.SemaphoreType.DMA((4,)),
    )

    def body(R):
        info, sem = R.info, R.sem
        core = info[1]
        for r in range(4):
            line = lax.shift_right_logical(info[3 + r], 1)
            for source, side in ((R.mine[r], core), (R.far[r], 1 - core)):
                start = pl.multiple_of((side * 4 + line) * piece, 16)
                R.wide[pl.ds(start, piece), :] = source[...].astype(F32)
        moves = [copy(R.wide.at[pl.ds(k * width, width)], R.grads[k], sem.at[k]) for k in range(3)]
        moves.append(copy(R.wide.at[pl.ds(3 * width, 2 * quarter)], R.recv, sem.at[3]))
        for move in moves:
            move.start()
        base = 3 * width + 2 * quarter
        sums = R.wide[base : base + TAIL_ROWS, :]
        micro = lax.broadcasted_iota(jnp.int32, (1, 4), 1) ^ info[0]
        for k in range(4):
            R.vec[k][...] = sums[k : k + 1]
        for which in range(2):
            total = jnp.zeros((1, 4), F32)
            for k in range(4):
                row = sums[4 + k : 5 + k]
                square = row[:, which * LANES : which * LANES + 4] / (row[:, 2 * LANES : 2 * LANES + 4] * width)
                total = total + jnp.where(micro == k, jnp.sqrt(square), 0.0)
            R.rms[which][...] = total
        for move in moves:
            move.wait()

    return run_kernel(body, info, inputs, outputs, scratch, 3, 10)


def on_device(
    node_in,
    edge_in,
    node_cot,
    edge_cot,
    own_weight,
    other_weight,
    recv_weight,
    first_bias,
    out_weight,
    out_bias,
    norm_gain,
    norm_bias,
    senders,
    receivers,
    node_valid,
    edge_valid,
):
    micro_count, rows_n, width = node_in.shape
    rows_e = edge_in.shape[1]
    blocks = lax.axis_size("rows")
    section = lax.axis_index("section")
    row_pos = lax.axis_index("rows")
    core = row_pos % 2
    here = row_pos // 2
    graph = Graph(rows_n, rows_e, blocks, width)
    lines = blocks // 2
    direct = lines == 4
    quarter = width // 4

    def swap(value):
        return lax.ppermute(value, "rows", [(i, i ^ 1) for i in range(blocks)])

    def along(value, distance, flip=0):
        route = [(i, (i // 2 + distance) % lines * 2 + (i % 2 ^ flip)) for i in range(blocks)]
        return lax.ppermute(value, "rows", route)

    def across(value, rel):
        return lax.ppermute(value, "section", [(i, i ^ rel) for i in range(4)])

    if direct:
        places = [((here - r) % 4) * 2 + core for r in range(4)] + [((here - r) % 4) * 2 + 1 - core for r in range(4)]
    else:
        places = [jnp.int32(k) for k in range(blocks)]
    table = jnp.stack([jnp.stack([section, core, section ^ rel] + places) for rel in range(4)]).astype(jnp.int32)
    infos = [Info(table, rel) for rel in range(4)]

    def as_blocks(arrays, index):
        return [(array, index, row) for array in arrays for row in range(0, array.shape[-2], rows_n)]

    def pick(array, rel):
        return lax.dynamic_index_in_dim(array, section ^ rel, 0, keepdims=False)

    def lined_up(value):
        return [along(value, r) for r in range(1, 4)]

    send_local = senders % rows_n
    recv_local = receivers % rows_n
    node_ids = jnp.arange(rows_n, dtype=jnp.int32)
    consts = const_kernel(
        graph,
        infos[0],
        [
            (send_local[:, None] == node_ids[None, :]).astype(BF),
            (recv_local[:, None] == node_ids[None, :]).astype(BF),
            ((recv_local[None, :] == node_ids[:, None]) & (edge_valid[None, :] != 0)).astype(BF),
            jnp.broadcast_to(edge_valid.astype(F32)[:, None], (rows_e, LANES)),
            jnp.broadcast_to(node_valid.astype(F32)[:, None], (rows_n, LANES)),
        ],
    )
    graph.consts = dict(ohs=consts[0], ohr=consts[1], ohrt=consts[2], emask=consts[3], nmask=consts[4])

    weights = (own_weight[0], other_weight[0], out_weight[0])
    recv_rows = recv_weight.reshape(2 * quarter, width)
    half = half_kernel(graph, infos[0], weights, recv_rows, (first_bias, out_bias, norm_gain, norm_bias))
    half_x, half_y = across(half, 1), across(half, 2)
    held = half.shape[0]
    cut = held // 32 * 16
    plan = [(0, None, 0, cut, 0, 0), (1, None, cut, held - cut, 1, 0)]
    plan += [(0, None, 0, held, 2, 0), (1, None, 0, held, 2, held)]
    rows = [cut, held - cut, 2 * held]
    send_da, send_db, cat = glue_kernel(graph, infos[0], [half_x, half_y], plan, rows, [consts[4]])
    half_da, half_db, far_xy = across(send_da, 2), across(send_db, 1), swap(cat)
    plan = [(0, None, 0, cut, 0, 0), (1, None, 0, held - cut, 0, cut)]
    if direct:
        nodes = jnp.stack([pick(node_in, 0), pick(node_in, 3)])
        row_lines = [nodes] + lined_up(nodes)
        flat_lines = [line.reshape(2 * rows_n, width) for line in row_lines]
        own_plan = [(r, None, 0, 2 * rows_n, 0, 2 * r * rows_n) for r in range(4)]
        (own_cat,) = glue_kernel(graph, infos[0], flat_lines, own_plan, [8 * rows_n])
        own_far = swap(own_cat)
        plan += [(2, None, 2 * r * rows_n, rows_n, 1, (r - 1) * rows_n) for r in range(1, 4)]
        cat, share = glue_kernel(graph, infos[0], [half_da, half_db, own_cat], plan, [held, 3 * rows_n])
        node_shared = {rel: across(share, rel) for rel in (1, 2)}
    else:
        node_all = [lax.all_gather(pick(node_in, rel), "rows", axis=0, tiled=True) for rel in range(4)]
        (cat,) = glue_kernel(graph, infos[0], [half_da, half_db], plan, [held])
    far_d = swap(cat)
    near = {1: [(half_x, 0, held)], 2: [(half_y, 0, held)], 3: [(half_da, 0, cut), (half_db, 0, held - cut)]}
    far = {1: [(far_xy, 0, held)], 2: [(far_xy, held, held)], 3: [(far_d, 0, held)]}
    graph.consts.update(wall=wall_kernel(graph, infos[0], weights, recv_rows, half, near, far))

    first, second, third, node_far = {}, {}, {}, {}

    def add_first(rel, after):
        if not direct:
            blocks1 = as_blocks([node_all[rel]], None)
        elif rel % 3 == 0:
            place = rel // 3
            blocks1 = [(line, None, place * rows_n) for line in flat_lines]
            blocks1 += [(own_far, None, (2 * r + place) * rows_n) for r in range(4)]
        else:
            blocks1 = [(None, None, 0)]
            blocks1 += [(node_shared[rel], None, r * rows_n) for r in range(3)]
            blocks1 += [(node_far[0], None, (4 * (rel - 1) + r) * rows_n) for r in range(4)]
        first[rel] = first_kernel(graph, infos[rel], edge_in, node_in, blocks1, after)

    blocks2 = {}
    add_first(0, [])
    if direct:
        lines2 = [first[0].t2] + lined_up(first[0].t2)
        add_first(3, [first[0].stat])
        plan = []
        for k in range(2):
            plan.append((0, k + 1, 0, rows_n, 0, 4 * k * rows_n))
            plan.append((1 + k, None, 0, 3 * rows_n, 0, (4 * k + 1) * rows_n))
        sources = [node_in, node_shared[1], node_shared[2]]
        (cat,) = glue_kernel(graph, infos[0], sources, plan, [8 * rows_n], [first[0].stat])
        node_far[0] = swap(cat)
        add_first(1, [first[3].stat])
        plan = [(r, None, 0, rows_n, 0, r * rows_n) for r in range(4)]
        plan += [(r, None, 0, rows_n, 1, (r - 1) * rows_n) for r in range(1, 4)]
        cat, share = glue_kernel(graph, infos[0], lines2, plan, [4 * rows_n, 3 * rows_n], [first[1].stat])
        far2 = swap(cat)
        shared = {rel: across(share, rel) for rel in range(1, 4)}
        add_first(2, [cat])
        blocks2[0] = as_blocks(lines2, None) + [(far2, None, r * rows_n) for r in range(4)]
    else:
        for rel in range(1, 4):
            add_first(rel, [first[rel - 1].stat])
        for rel in range(4):
            blocks2[rel] = as_blocks([lax.all_gather(first[rel].t2, "rows", axis=0, tiled=True)], None)

    def add_second(rel, after):
        before = second.get(rel - 1)
        second[rel] = second_kernel(
            graph, infos[rel], first[rel], blocks2[rel], node_cot, edge_cot, before, rel == 0, direct, after
        )

    def add_third(rel, sums, after):
        before = third[rel - 1] if rel else second[3]
        third[rel] = third_kernel(
            graph, infos[rel], first[rel], second[rel], sums, edge_in, before, rel == 0, direct, after
        )

    add_second(0, [first[2].stat])
    if direct:
        got = swap(second[0].gs[1])
        plan = []
        for k in range(3):
            plan.append((k, None, 0, rows_n, 0, 4 * k * rows_n))
            plan.append((3 + k, None, 0, 3 * rows_n, 0, (4 * k + 1) * rows_n))
        sources = [first[rel].t2 for rel in range(1, 4)] + [shared[rel] for rel in range(1, 4)]
        (cat,) = glue_kernel(graph, infos[0], sources, plan, [12 * rows_n], [second[0].stat])
        far2 = swap(cat)
        for rel in range(1, 4):
            entry = [(first[rel].t2, None, 0)] + [(shared[rel], None, r * rows_n) for r in range(3)]
            entry += [(far2, None, (4 * (rel - 1) + r) * rows_n) for r in range(4)]
            blocks2[rel] = entry
        parts = add_kernel(graph, infos[0], [second[0].gs[0], got], rows_n, [cat])
        sums = [parts[0]] + [along(parts[r], -r) for r in range(1, 4)]
        add_second(1, [parts[0]])
        add_second(2, [])
        add_second(3, [])
    else:
        for rel in range(1, 4):
            add_second(rel, [])
        sums = [lax.psum_scatter(second[0].gs[0], "rows", scatter_dimension=0, tiled=True)]
    add_third(0, sums, [])
    shared = {rel: across(third[0].total, rel) for rel in range(1, 4)}
    if direct:
        parts = add_kernel(graph, infos[0], [third[0].gs[0], swap(third[0].gs[1])], rows_n)
        sums = [parts[0]] + [along(parts[r], -r) for r in range(1, 4)]
        add_third(1, [shared[1]], [parts[0]])
    else:
        add_third(1, [shared[1]], [])
    add_third(2, [shared[2]], [])
    add_third(3, [shared[3]], [])
    last = third[3]
    stats = ([first[rel].stat for rel in range(4)], [second[rel].stat for rel in range(4)])
    packed, piece = pack_kernel(graph, infos[0], last.wg, last.vec, stats, direct, sums if direct else [])
    if direct:
        (total,) = add_kernel(graph, infos[0], sums, rows_n, [packed[0]])
    else:
        total = lax.psum_scatter(third[0].gs[0], "rows", scatter_dimension=0, tiled=True)
    low = [total] + [lax.ppermute(total, "section", [(rel, 0)]) for rel in range(1, 4)]
    zero = node_zero_kernel(
        graph, infos[0], [third[rel].node_part for rel in range(4)], low, last.node_grad, graph.consts["wall"]
    )
    if direct:
        pieces = add_kernel(graph, infos[0], [packed[0], swap(packed[1])], piece)
        row_lines = [pieces[0]] + [along(pieces[r], -r) for r in range(1, 4)]
        (whole,) = add_kernel(graph, infos[0], row_lines, piece, [zero.token])
        row_lines = [whole] + lined_up(whole)
        result = unpack_kernel(graph, infos[0], row_lines, [swap(line) for line in row_lines], piece)
        grads, recv, vec, rms = result.grads, result.recv, result.vec, result.rms
    else:
        full = lax.psum(packed[0], "rows")
        base = 3 * width + 2 * quarter
        grads = [full[k * width : (k + 1) * width] for k in range(3)]
        recv = full[3 * width : base]
        sums = full[base : base + TAIL_ROWS]
        vec = [sums[k : k + 1] for k in range(4)]
        rms = jnp.sqrt(sums[4:8, 0 : 2 * LANES : LANES] / (sums[4:8, 2 * LANES : 2 * LANES + 1] * width))
        rms = jnp.take(rms, jnp.arange(4, dtype=jnp.int32) ^ section, axis=0)
        rms = [rms[:, 0][None], rms[:, 1][None]]
    return (
        second[3].node_out[None],
        second[3].edge_out[None],
        zero.node_grad[None],
        last.edge_grad[None],
        grads[0][None],
        grads[1][None],
        recv.reshape(2, quarter, width),
        vec[0],
        grads[2][None],
        vec[1],
        vec[2],
        vec[3],
        rms[0],
        rms[1],
    )


def solution(mesh):
    whole = P("section", None, None)
    line = P("section", None)
    latents = P(None, "rows", None)
    outs = P("section", None, "rows", None)
    recv = P(None, "section", None)
    ends = P("rows")
    return jax.shard_map(
        on_device,
        mesh=mesh,
        in_specs=(latents,) * 4 + (whole, whole, recv, line, whole, line, line, line) + (ends,) * 4,
        out_specs=(outs,) * 4 + (whole, whole, recv, line, whole, line, line, line, line, line),
        check_vma=False,
    )
```

```python
import types

import jax
import jax.numpy as jnp
from jax import lax
from jax.experimental import pallas as pl
from jax.experimental.pallas import tpu as pltpu
from jax.sharding import PartitionSpec as P

F32 = jnp.float32
BF = jnp.bfloat16
CHUNK = 512
LANES = 128
VEC_ROWS = 16
ANY = pl.ANY
VMEM = pltpu.VMEM
HBM = pltpu.HBM


def dot(left, right):
    return jnp.dot(left, right, preferred_element_type=F32)


def dot_nt(left, right):
    return lax.dot_general(left, right, (((1,), (1,)), ((), ())), preferred_element_type=F32)


def dot_tn(left, right):
    return lax.dot_general(left, right, (((0,), (0,)), ((), ())), preferred_element_type=F32)


def sigmoid(value):
    return 0.5 * jnp.tanh(0.5 * value) + 0.5


def widen(column, width):
    return jnp.concatenate([column] * (width // column.shape[1]), axis=1)


def col_sum(value):
    return jnp.sum(value, axis=0, keepdims=True)


def tail(pre_act, weight_out, vecs):
    hidden = (pre_act * sigmoid(pre_act)).astype(BF)
    update = dot(hidden, weight_out) + vecs[1]
    mean = jnp.mean(update, axis=-1, keepdims=True)
    centre = update - mean
    spread = jnp.mean(centre * centre, axis=-1, keepdims=True)
    inverse = lax.rsqrt(spread + 1e-05)
    scaled = centre * inverse
    return hidden, scaled, inverse, spread + mean * mean, scaled * vecs[2] + vecs[3]


def norm_back(grad_normed, scaled, inverse, gain):
    weighted = grad_normed * gain
    mean_grad = jnp.mean(weighted, axis=-1, keepdims=True)
    mean_both = jnp.mean(weighted * scaled, axis=-1, keepdims=True)
    return inverse * (weighted - mean_grad - scaled * mean_both)


def silu_back(grad_hidden, pre_act):
    sig = sigmoid(pre_act)
    return grad_hidden * (sig * (1.0 + pre_act * (1.0 - sig))), sig


class Info:
    def __init__(self, table, rel):
        self.table, self.rel = table, rel

    def __getitem__(self, k):
        return self.table[self.rel, k]


V, H, A, B = range(4)
PLACES = (VMEM, HBM, pl.ANY, None)


def flat(entries):
    return [item for entry in entries.values() for item in (entry if isinstance(entry, list) else [entry])]


def named(entries, items):
    return {
        name: [next(items) for _ in entry] if isinstance(entry, list) else next(items)
        for name, entry in entries.items()
    }


def run_kernel(body, info, inputs, outputs, scratch, micros, limit):
    given, made = flat(inputs), flat(outputs)
    aliases = {}
    for index, entry in enumerate(made):
        if entry[3] is not None:
            aliases[1 + [array is entry[3] for array, _ in given].index(True)] = index

    def kernel(*refs):
        rest = iter(refs[1:])
        groups = [named(entries, rest) for entries in (inputs, outputs, scratch)]
        body(types.SimpleNamespace(info=Info(refs[0], info.rel), **groups[0], **groups[1], **groups[2]))

    arrays = [pltpu.with_memory_space_constraint(array, PLACES[kind]) for array, kind in given]
    results = pl.pallas_call(
        kernel,
        out_shape=[
            jax.ShapeDtypeStruct(entry[0], entry[1]) if entry[2] >= A else PLACES[entry[2]](entry[0], entry[1])
            for entry in made
        ],
        in_specs=[pl.BlockSpec(memory_space=pltpu.SMEM)] + [pl.BlockSpec(memory_space=PLACES[kind]) for _, kind in given],
        out_specs=[pl.BlockSpec() if entry[2] == B else pl.BlockSpec(memory_space=PLACES[entry[2]]) for entry in made],
        scratch_shapes=flat(scratch),
        input_output_aliases=aliases,
        compiler_params=pltpu.CompilerParams(vmem_limit_bytes=limit * 1024 * 1024),
        cost_estimate=pl.CostEstimate(flops=int(micros * 1.15e9), bytes_accessed=0, transcendentals=0),
    )(info.table, *arrays)
    return types.SimpleNamespace(**named(outputs, iter(results)))


def copy(source, target, sem):
    return pltpu.make_async_copy(source, target, sem)


def either(arrays):
    return [(array, A) for array in arrays]


class Graph:
    def __init__(self, rows_n, rows_e, blocks, width):
        self.rows_n, self.rows_e, self.blocks, self.width = rows_n, rows_e, blocks, width
        self.cap = rows_e // blocks
        self.chunk = min(CHUNK, rows_e)
        self.starts = range(0, rows_e, self.chunk)
        self.consts = {}

    def const_inputs(self):
        return {name: (array, V) for name, array in self.consts.items()}

    def weight_row(self, section_id, part):
        return (section_id * 3 + part) * self.width

    def weight(self, R, section_id, part, count=1):
        return R.wall[pl.ds(self.weight_row(section_id, part), count * self.width), :]

    def recv_weight(self, R, layer):
        return R.wall[pl.ds((12 + layer) * self.width, self.width), :]

    def vectors(self, R, section_id):
        block = R.wall[pl.ds(14 * self.width + section_id * VEC_ROWS, VEC_ROWS), :].astype(F32)
        return [block[k : k + 1] + block[4 + k : 5 + k] for k in range(4)]


OWN, OTHER, OUT = 0, 1, 2


def half_rows(width):
    half, eighth = width // 2, width // 8
    return half, eighth, 3 * half + 2 * eighth, 3 * half + 2 * eighth + VEC_ROWS


def half_kernel(graph, info, weights, recv, vecs):
    half, eighth, vec_row, rows = half_rows(graph.width)
    quarter = 2 * eighth

    def body(R):
        core, stage = R.info[1], R.half
        for k in range(3):
            source = R.weights[k].at[pl.ds(pl.multiple_of(core * half, half), half)]
            copy(source, stage.at[pl.ds(k * half, half)], R.sem).start()
        for layer in range(2):
            source = R.recv.at[pl.ds(pl.multiple_of(layer * quarter + core * eighth, eighth), eighth)]
            copy(source, stage.at[pl.ds(3 * half + layer * eighth, eighth)], R.sem).start()
        for k in range(4):
            copy(R.vecs[k], R.rows.at[pl.ds(k, 1)], R.row_sem).start()
        copy(R.rows, R.rows, R.row_sem).wait()
        rows_here = R.rows[...]
        high = rows_here.astype(BF)
        low = (rows_here - high.astype(F32)).astype(BF)
        stage[vec_row : vec_row + VEC_ROWS, :] = jnp.concatenate([high, low, high, low], axis=0)
        loaded = stage.at[pl.ds(0, vec_row)]
        copy(loaded, loaded, R.sem).wait()

    inputs = dict(weights=[(array, H) for array in weights], recv=(recv, H), vecs=[(array, H) for array in vecs])
    outputs = dict(half=((rows, graph.width), BF, V, None))
    scratch = dict(
        rows=VMEM((4, graph.width), F32),
        sem=pltpu.SemaphoreType.DMA,
        row_sem=pltpu.SemaphoreType.DMA,
    )
    return run_kernel(body, info, inputs, outputs, scratch, 1, 2).half


def wall_kernel(graph, info, weights, recv, mine, near, far):
    width = graph.width
    half, eighth, vec_row, rows = half_rows(width)
    quarter = 2 * eighth
    pieces = [piece for side in (near, far) for rel in range(1, 4) for piece in side[rel]]
    inputs = dict(
        weights=[(array, H) for array in weights], recv=(recv, H), mine=(mine, A), pieces=either([p[0] for p in pieces])
    )
    total = 14 * width + 4 * VEC_ROWS

    def body(R):
        section, core = R.info[0], R.info[1]
        wall, sem = R.wall, R.sem
        refs = iter(R.pieces)

        def put(source, row, count, unit):
            copy(source, wall.at[pl.ds(pl.multiple_of(row, unit), count)], sem).start()

        for k in range(3):
            put(R.weights[k], section * 3 * width + k * width, width, width)
        for layer in range(2):
            put(R.recv.at[pl.ds(layer * quarter, quarter)], (12 + layer) * width + section * quarter, quarter, quarter)
        put(R.mine.at[pl.ds(vec_row, VEC_ROWS)], 14 * width + section * VEC_ROWS, VEC_ROWS, VEC_ROWS)
        for side, pieces_of in ((core, near), (1 - core, far)):
            for rel in range(1, 4):
                there = section ^ rel
                parts = [(k * half, half, (there * 3 + k) * width + side * half) for k in range(3)]
                parts += [
                    (3 * half + layer * eighth, eighth, (12 + layer) * width + there * quarter + side * eighth)
                    for layer in range(2)
                ]
                if pieces_of is near:
                    parts.append((vec_row, VEC_ROWS, 14 * width + there * VEC_ROWS))
                first = 0
                for _, begin, held in pieces_of[rel]:
                    ref = next(refs)
                    for row, count, target in parts:
                        low, high = max(row, first), min(row + count, first + held)
                        if low < high:
                            put(ref.at[pl.ds(begin + low - first, high - low)], target + low - row, high - low, 16)
                    first += held
        copy(wall, wall, sem).wait()

    outputs = dict(wall=((total, width), BF, V, None))
    return run_kernel(body, info, inputs, outputs, dict(sem=pltpu.SemaphoreType.DMA), 3, 1).wall


def glue_kernel(graph, info, sources, plan, rows, after=()):
    width = graph.width
    inputs = dict(source=[(array, H if array.ndim > 2 else A) for array in sources], after=either(after))
    outputs = dict(out=[((count, width), BF, A, None) for count in rows])
    scratch = dict(sem=pltpu.SemaphoreType.DMA((len(rows),)))

    def body(R):
        for source, index, row, count, target, place in plan:
            ref = R.source[source] if index is None else R.source[source].at[R.info[0] ^ index]
            copy(ref.at[pl.ds(row, count)], R.out[target].at[pl.ds(place, count)], R.sem.at[target]).start()
        for k, out in enumerate(R.out):
            copy(out, out, R.sem.at[k]).wait()

    return run_kernel(body, info, inputs, outputs, scratch, 2, 1).out


def summed_rows(stages, here):
    total = stages[0][here, :].astype(F32)
    for other in stages[1:]:
        total = total + other[here, :].astype(F32)
    return total.astype(BF)


def add_kernel(graph, info, arrays, rows, after=()):
    count, width = arrays[0].shape
    inputs = dict(source=[(array, V) for array in arrays], after=either(after))
    outputs = dict(out=[((rows, width), BF, V, None)] * (count // rows))

    def body(R):
        for k in range(count // rows):
            R.out[k][...] = summed_rows(R.source, slice(k * rows, (k + 1) * rows))

    return run_kernel(body, info, inputs, outputs, {}, 2, 4).out


def node_zero_kernel(graph, info, third, sums, node_grad, wall, after):
    rows_n, width = graph.rows_n, graph.width
    inputs = dict(
        ng1=[(kernel.ng1, V) for kernel in third],
        gr0=[(kernel.gr0, V) for kernel in third],
        sums=[(array, V) for array in sums],
        old=(node_grad, H),
        wall=(wall, V),
        after=either(after),
    )
    outputs = dict(node_grad=(node_grad.shape, BF, H, node_grad), token=((8, LANES), F32, V, None))
    scratch = dict(total=VMEM((4, rows_n, width), BF), sem=pltpu.SemaphoreType.DMA)

    def body(R):
        R.token[...] = jnp.zeros_like(R.token)

        @pl.when(R.info[0] == 0)
        def _():
            for k in range(4):
                grad = R.ng1[k][...].astype(F32) + dot_nt(R.gr0[k][...], graph.recv_weight(R, 0))
                R.total[k] = (grad + dot_nt(R.sums[k][...], graph.weight(R, 0, OTHER))).astype(BF)
            move = copy(R.total, R.node_grad, R.sem)
            move.start()
            move.wait()

    return run_kernel(body, info, inputs, outputs, scratch, 2, 6)


def edge_zero_kernel(graph, info, third, edge_grad, wall, after):
    rows_e, width = graph.rows_e, graph.width
    inputs = dict(
        eg1=[(kernel.eg1, V) for kernel in third],
        gz=[(kernel.gz, V) for kernel in third],
        old=(edge_grad, H),
        wall=(wall, V),
        after=either(after),
    )
    outputs = dict(edge_grad=(edge_grad.shape, BF, H, edge_grad), token=((8, LANES), F32, V, None))
    scratch = dict(total=[VMEM((rows_e, width), BF)] * 4, sem=pltpu.SemaphoreType.DMA((4,)))

    def body(R):
        R.token[...] = jnp.zeros_like(R.token)

        @pl.when(R.info[0] == 0)
        def _():
            moves = [copy(R.total[k], R.edge_grad.at[k], R.sem.at[k]) for k in range(4)]
            for k in range(4):
                for start in graph.starts:
                    rows = pl.ds(start, graph.chunk)
                    grad = dot_nt(R.gz[k][rows, :], graph.weight(R, 0, OWN))
                    R.total[k][rows, :] = (R.eg1[k][rows, :].astype(F32) + grad).astype(BF)
                moves[k].start()
            for move in moves:
                move.wait()

    return run_kernel(body, info, inputs, outputs, scratch, 5, 9)


def const_kernel(graph, info, arrays):
    inputs = dict(source=[(array, H) for array in arrays])
    outputs = dict(out=[(array.shape, array.dtype, V, None) for array in arrays])

    def body(R):
        moves = [copy(source, out, R.sem.at[k]) for k, (source, out) in enumerate(zip(R.source, R.out))]
        for move in moves:
            move.start()
        for move in moves:
            move.wait()

    scratch = dict(sem=pltpu.SemaphoreType.DMA((len(arrays),)))
    return run_kernel(body, info, inputs, outputs, scratch, 2, 1).out


def block_inputs(blocks):
    return [(array, V) for array in block_arrays(blocks)]


def block_arrays(blocks):
    arrays = []
    for array, _, _ in blocks:
        if array is not None and all(array is not other for other in arrays):
            arrays.append(array)
    return arrays


def each_block(graph, R, blocks, work):
    arrays = block_arrays(blocks)
    cap, rows_n = graph.cap, graph.rows_n
    if len(arrays) == 1:

        @pl.loop(0, graph.blocks)
        def _(place):
            nodes = pl.ds(pl.multiple_of(place * rows_n, rows_n), rows_n)
            work(pl.ds(pl.multiple_of(place * cap, cap), cap), R.block[0][nodes, :])

        return
    for place, (array, index, row) in enumerate(blocks):
        nodes = pl.ds(row, rows_n)
        if array is None:
            block = R.node0[...]
        else:
            block = R.block[[array is other for other in arrays].index(True)][nodes, :]
        work(pl.ds(pl.multiple_of(R.info[3 + place] * cap, cap), cap), block)


def stat_pair(square, stream, mask):
    branch = col_sum(mask * square)
    total = col_sum(mask * jnp.sum(stream * stream, axis=-1, keepdims=True))
    return branch, total


def put_stats(stat, pairs, width):
    branch, total = pairs[0]
    for pair in pairs[1:]:
        branch, total = branch + pair[0], total + pair[1]
    stat[0:1, :] = jnp.broadcast_to(branch * width, (1, LANES))
    stat[1:2, :] = jnp.broadcast_to(total, (1, LANES))


def first_kernel(graph, info, edge_in, node_in, blocks, after):
    rows_e, rows_n, width = graph.rows_e, graph.rows_n, graph.width
    inputs = dict(
        edges=(edge_in, H), nodes=(node_in, H), block=block_inputs(blocks), after=either(after), **graph.const_inputs()
    )
    rows = ((rows_e, width), BF, V, None)
    few = ((rows_n, width), BF, V, None)
    outputs = dict(
        edge1=rows,
        z0=rows,
        x0=rows,
        q0=((rows_e, LANES), F32, V, None),
        s0=rows,
        node0=few,
        node1=few,
        g1=few,
        z1=few,
        x1=few,
        q1=((rows_n, LANES), F32, V, None),
        stat=((8, LANES), F32, V, None),
        t2=few,
    )
    scratch = dict(edge=VMEM((rows_e, width), BF), sem=pltpu.SemaphoreType.DMA((2,)))

    def body(R):
        info = R.info
        section, micro = info[0], info[2]
        node_copy = copy(R.nodes.at[micro], R.node0, R.sem.at[0])
        edge_copy = copy(R.edges.at[micro], R.edge, R.sem.at[1])
        node_copy.start()
        edge_copy.start()

        def send_rows(edges, block):
            R.s0[edges, :] = dot(R.ohs[edges, :], block).astype(BF)

        node_copy.wait()
        each_block(graph, R, blocks, send_rows)
        node = R.node0[...]
        vecs = graph.vectors(R, 0)
        recv_node = (dot(node, graph.recv_weight(R, 0)) + vecs[0]).astype(BF)
        edge_copy.wait()
        pairs = []
        for start in graph.starts:
            rows = pl.ds(start, graph.chunk)
            mask = R.emask[rows, :]
            edge = R.edge[rows, :]
            pre_act = dot(jnp.concatenate([edge, R.s0[rows, :]], axis=1), graph.weight(R, 0, OWN, 2))
            pre_act = pre_act + dot(R.ohr[rows, :], recv_node)
            hidden, scaled, inverse, square, normed = tail(pre_act, graph.weight(R, 0, OUT), vecs)
            stream = edge.astype(F32) + widen(mask, width) * normed
            R.edge1[rows, :] = stream.astype(BF)
            R.z0[rows, :] = pre_act.astype(BF)
            R.x0[rows, :] = scaled.astype(BF)
            R.q0[rows, :] = jnp.broadcast_to(inverse, (graph.chunk, LANES))
            pairs.append(stat_pair(square, stream, mask[:, :1]))
        summed = dot(R.ohrt[...], R.edge1[...]).astype(BF)
        R.g1[...] = summed
        vecs = graph.vectors(R, 1)
        pre_act = dot(jnp.concatenate([node, summed], axis=1), graph.weight(R, 1, OWN, 2)) + vecs[0]
        hidden, scaled, inverse, square, normed = tail(pre_act, graph.weight(R, 1, OUT), vecs)
        nmask = R.nmask[...]
        stream = node.astype(F32) + widen(nmask, width) * normed
        low = stream.astype(BF)
        R.t2[...] = dot(low, graph.weight(R, 2, OTHER)).astype(BF)
        R.node1[...] = low
        R.z1[...] = pre_act.astype(BF)
        R.x1[...] = scaled.astype(BF)
        R.q1[...] = jnp.broadcast_to(inverse, (rows_n, LANES))

        @pl.when(section == 0)
        def _():
            put_stats(R.stat, pairs, width)

        @pl.when(section != 0)
        def _():
            put_stats(R.stat, [stat_pair(square, stream, nmask[:, :1])], width)

    return run_kernel(body, info, inputs, outputs, scratch, 8, 10 if graph.blocks <= 8 else 20)


def sender_outputs(graph, direct):
    rows = graph.blocks * graph.rows_n
    if direct:
        return dict(gs=[((rows // 2, graph.width), BF, V, None)] * 2)
    return dict(gs=[((rows, graph.width), BF, A, None)])


def sender_sums(graph, R, grads):
    each = graph.blocks // len(R.gs)
    if each == graph.blocks:

        @pl.loop(0, each)
        def _(place):
            rows = pl.ds(pl.multiple_of(place * graph.cap, graph.cap), graph.cap)
            here = pl.ds(pl.multiple_of(place * graph.rows_n, graph.rows_n), graph.rows_n)
            R.sums_here[...] = dot_tn(R.ohs[rows, :], grads[rows, :]).astype(BF)
            move = copy(R.sums_here, R.gs[0].at[here], R.sums_sem)
            move.start()
            move.wait()

        return
    for place in range(graph.blocks):
        rows = pl.ds(pl.multiple_of(R.info[3 + place] * graph.cap, graph.cap), graph.cap)
        here = pl.ds(place % each * graph.rows_n, graph.rows_n)
        R.gs[place // each][here, :] = dot_tn(R.ohs[rows, :], grads[rows, :]).astype(BF)


def add_recv(graph, R, layer, node, grad_recv):
    quarter = graph.width // 4
    start = pl.multiple_of(R.info[0] * quarter, quarter)
    rows = pl.ds(3 * graph.width + layer * quarter, quarter)
    R.wg[rows, :] += dot_tn(node[:, pl.ds(start, quarter)], grad_recv)


def second_kernel(graph, info, first, blocks, node_cot, edge_cot, before, own_first, direct, after):
    rows_e, rows_n, width = graph.rows_e, graph.rows_n, graph.width
    micro_count = node_cot.shape[0]
    inputs = dict(
        edge1=(first.edge1, V),
        node0=(first.node0, V),
        node1=(first.node1, V),
        edge_cot=(edge_cot, H),
        node_cot=(node_cot, H),
        block=block_inputs(blocks),
        after=either(after),
        **graph.const_inputs(),
    )
    chain = [None] * 5
    if before is not None:
        chain = [before.edge_out, before.node_out, before.edge_grad, before.wg, before.vec]
        inputs.update(old=[(array, kind) for array, kind in zip(chain, (H, H, H, V, V))])
    rows = VMEM((rows_e, width), BF)
    few = VMEM((rows_n, width), BF)
    outputs = dict(
        edge_out=((micro_count, rows_e, width), BF, H, chain[0]),
        node_out=((micro_count, rows_n, width), BF, H, chain[1]),
        edge_grad=((micro_count, rows_e, width), BF, H, chain[2]),
        wg=((3 * width + width // 2, width), F32, V, chain[3]),
        vec=((8, width), F32, V, chain[4]),
        eg2=((rows_e, width), BF, V, None),
        ng=((rows_n, width), BF, V, None),
        gr=((rows_n, width), BF, V, None),
        stat=((8, LANES), F32, V, None),
    )
    if own_first:
        outputs.update(sender_outputs(graph, direct))
    scratch = dict(
        ends=VMEM((rows_e, width), F32),
        cot=rows,
        ncot=few,
        edge2=rows,
        eg=rows,
        node_here=few,
        z=rows,
        x=rows,
        q=VMEM((rows_e, LANES), F32),
        a=rows,
        gu=rows,
        gz=rows,
        sem=pltpu.SemaphoreType.DMA((8,)),
    )
    if own_first and not direct:
        scratch.update(sums_here=few, sums_sem=pltpu.SemaphoreType.DMA)

    def body(R):
        info = R.info
        section, micro = info[0], info[2]
        sem = R.sem
        cot_copy = copy(R.edge_cot.at[micro], R.cot, sem.at[1])
        ncot_copy = copy(R.node_cot.at[micro], R.ncot, sem.at[2])
        ncot_copy.start()
        cot_copy.start()
        if own_first:
            R.wg[...] = jnp.zeros_like(R.wg)
            R.vec[...] = jnp.zeros_like(R.vec)
        node = R.node1[...]
        vecs = graph.vectors(R, 2)
        recv_node = (dot(node, graph.recv_weight(R, 1)) + vecs[0]).astype(BF)

        def end_rows(edges, block):
            onehot = jnp.concatenate([R.ohs[edges, :], R.ohr[edges, :]], axis=1)
            R.ends[edges, :] = dot(onehot, jnp.concatenate([block, recv_node], axis=0))

        each_block(graph, R, blocks, end_rows)
        pairs = []
        for start in graph.starts:
            rows = pl.ds(start, graph.chunk)
            mask = R.emask[rows, :]
            edge = R.edge1[rows, :]
            pre_act = dot(edge, graph.weight(R, 2, OWN)) + R.ends[rows, :]
            hidden, scaled, inverse, square, normed = tail(pre_act, graph.weight(R, 2, OUT), vecs)
            stream = edge.astype(F32) + widen(mask, width) * normed
            R.edge2[rows, :] = stream.astype(BF)
            R.z[rows, :] = pre_act.astype(BF)
            R.x[rows, :] = scaled.astype(BF)
            R.q[rows, :] = jnp.broadcast_to(inverse, (graph.chunk, LANES))
            R.a[rows, :] = hidden
            pairs.append(stat_pair(square, stream, mask[:, :1]))

        @pl.when(section >= 2)
        def _():
            copy(R.edge2, R.edge_out.at[micro], sem.at[3]).start()

        @pl.when(section < 2)
        def _():
            copy(R.edge1, R.edge_out.at[micro], sem.at[3]).start()

        vecs = graph.vectors(R, 3)
        summed = dot(R.ohrt[...], R.edge2[...]).astype(BF)
        weight_out = graph.weight(R, 3, OUT)
        pre_act = dot(jnp.concatenate([node, summed], axis=1), graph.weight(R, 3, OWN, 2)) + vecs[0]
        hidden, scaled, inverse, square, normed = tail(pre_act, weight_out, vecs)
        nmask = R.nmask[...]
        wide_mask = widen(nmask, width)
        stream = node.astype(F32) + wide_mask * normed
        R.node_here[...] = jnp.where(
            section == 0, R.node0[...], jnp.where(section == 3, stream.astype(BF), node)
        )
        node_copy = copy(R.node_here, R.node_out.at[micro], sem.at[4])
        node_copy.start()

        @pl.when(section == 3)
        def _():
            put_stats(R.stat, [stat_pair(square, stream, nmask[:, :1])], width)

        @pl.when(section != 3)
        def _():
            put_stats(R.stat, pairs, width)

        ncot_copy.wait()
        grad = R.ncot[...].astype(F32)
        grad_normed = wide_mask * grad
        grad_update = norm_back(grad_normed, scaled, inverse, vecs[2])
        grad_low = grad_update.astype(BF)
        grad_pre, _ = silu_back(dot_nt(grad_low, weight_out), pre_act)
        pre_low = grad_pre.astype(BF)
        R.ng[...] = (grad + dot_nt(pre_low, graph.weight(R, 3, OWN))).astype(BF)
        grad_sum = dot_nt(pre_low, graph.weight(R, 3, OTHER))
        grad_high = grad_sum.astype(BF)
        grad_both = jnp.concatenate([grad_high, (grad_sum - grad_high.astype(F32)).astype(BF)], axis=0)

        @pl.when(section == 3)
        def _():
            R.wg[0:width, :] += dot_tn(node, pre_low)
            R.wg[width : 2 * width, :] += dot_tn(summed, pre_low)
            R.wg[2 * width : 3 * width, :] += dot_tn(hidden, grad_low)
            R.vec[0:1, :] += col_sum(grad_pre)
            R.vec[1:2, :] += col_sum(grad_update)
            R.vec[2:3, :] += col_sum(grad_normed * scaled)
            R.vec[3:4, :] += col_sum(grad_normed)

        cot_copy.wait()
        vecs = graph.vectors(R, 2)

        def arriving(rows, mask):
            onehot = R.ohr[rows, :]
            spread = dot(jnp.concatenate([onehot, onehot], axis=1), grad_both)
            return (R.cot[rows, :].astype(F32) + mask * spread).astype(BF)

        def edge_back(sums):
            totals = [jnp.zeros((1, width), F32)] * 4
            for start in graph.starts:
                rows = pl.ds(start, graph.chunk)
                mask = R.emask[rows, :]
                low = arriving(rows, widen(mask, width))
                R.eg[rows, :] = low
                wide = low.astype(F32)
                scaled = R.x[rows, :].astype(F32)
                pre_act = R.z[rows, :].astype(F32)
                inverse = widen(R.q[rows, :] * mask, width)
                grad_update = norm_back(wide, scaled, inverse, vecs[2])
                grad_low = grad_update.astype(BF)
                grad_pre, _ = silu_back(dot_nt(grad_low, graph.weight(R, 2, OUT)), pre_act)
                pre_low = grad_pre.astype(BF)
                R.gz[rows, :] = pre_low
                R.eg2[rows, :] = (wide + dot_nt(pre_low, graph.weight(R, 2, OWN))).astype(BF)
                if sums:
                    R.gu[rows, :] = grad_low
                    normed = widen(mask, width) * wide
                    parts = (grad_pre, grad_update, normed * scaled, normed)
                    totals = [total + col_sum(part) for total, part in zip(totals, parts)]
            if sums:
                R.wg[0:width, :] += dot_tn(R.edge1[...], R.gz[...])
                R.wg[2 * width : 3 * width, :] += dot_tn(R.a[...], R.gu[...])
                for k in range(4):
                    R.vec[k : k + 1, :] += totals[k]

        @pl.when(section == 2)
        def _():
            edge_back(True)

        @pl.when(section != 2)
        def _():
            edge_back(False)

        @pl.when(section == 2)
        def _():
            copy(R.eg2, R.edge_grad.at[micro], sem.at[6]).start()

        @pl.when(section == 3)
        def _():
            copy(R.eg, R.edge_grad.at[micro], sem.at[6]).start()

        grad_recv = dot(R.ohrt[...], R.gz[...]).astype(BF)
        R.gr[...] = grad_recv
        add_recv(graph, R, 1, R.node1, grad_recv)
        if own_first:
            sender_sums(graph, R, R.gz)
        node_copy.wait()
        copy(R.edge2, R.edge_out.at[micro], sem.at[3]).wait()

        @pl.when(section >= 2)
        def _():
            copy(R.eg, R.edge_grad.at[micro], sem.at[6]).wait()

    return run_kernel(body, info, inputs, outputs, scratch, 14, 18 if graph.blocks <= 8 else 28)


def third_kernel(graph, info, first, second, sums, edge_in, before, own_first, direct, after):
    rows_e, rows_n, width = graph.rows_e, graph.rows_n, graph.width
    inputs = dict(
        second=[(array, V) for array in (second.eg2, second.ng, second.gr)],
        z0=(first.z0, V),
        x0=(first.x0, V),
        q0=(first.q0, V),
        s0=(first.s0, V),
        node0=(first.node0, V),
        node1=(first.node1, V),
        g1=(first.g1, V),
        z1=(first.z1, V),
        x1=(first.x1, V),
        q1=(first.q1, V),
        sums=[(array, V) for array in sums],
        edges=(edge_in, H),
        after=either(after),
        **graph.const_inputs(),
    )
    node_grad = None if own_first else before.node_grad
    chain = [(before.edge_grad, H), (before.wg, V), (before.vec, V)]
    inputs.update(old=chain if own_first else chain + [(node_grad, H)])
    micro_count = before.edge_grad.shape[0]
    rows = VMEM((rows_e, width), BF)
    few = VMEM((rows_n, width), BF)
    outputs = dict(
        edge_grad=(before.edge_grad.shape, BF, H, before.edge_grad),
        node_grad=((micro_count, rows_n, width), BF, H, node_grad),
        wg=(before.wg.shape, F32, V, before.wg),
        vec=(before.vec.shape, F32, V, before.vec),
        eg1=((rows_e, width), BF, V, None),
        gz=((rows_e, width), BF, V, None),
        ng1=((rows_n, width), BF, V, None),
        gr0=((rows_n, width), BF, V, None),
        token=((8, LANES), F32, V, None),
    )
    if own_first:
        outputs.update(sender_outputs(graph, direct))
        outputs.update(total=((rows_n, width), BF, V, None))
    scratch = dict(
        edge=rows,
        out_node=few,
        gu=rows,
        a=rows,
        sem=pltpu.SemaphoreType.DMA((4,)),
    )
    if own_first and not direct:
        scratch.update(sums_here=few, sums_sem=pltpu.SemaphoreType.DMA)

    def body(R):
        info = R.info
        section, micro = info[0], info[2]
        sem = R.sem
        eg2, ng, gr = R.second
        R.token[...] = jnp.zeros_like(R.token)
        edge_copy = copy(R.edges.at[micro], R.edge, sem.at[1])

        @pl.when(section == 0)
        def _():
            edge_copy.start()

        if own_first:
            R.total[...] = summed_rows(R.sums, slice(None))
        gs2 = (R.total if own_first else R.sums[0])[...]
        grad_mid = (
            ng[...].astype(F32) + dot_nt(gr[...], graph.recv_weight(R, 1)) + dot_nt(gs2, graph.weight(R, 2, OTHER))
        ).astype(BF)
        R.out_node[...] = jnp.where(section == 3, ng[...], grad_mid)

        @pl.when(section == 2)
        def _():
            R.wg[width : 2 * width, :] += dot_tn(R.node1[...], gs2)

        vecs = graph.vectors(R, 1)
        wide = grad_mid.astype(F32)
        grad_normed = widen(R.nmask[...], width) * wide
        scaled = R.x1[...].astype(F32)
        pre_act = R.z1[...].astype(F32)
        grad_update = norm_back(grad_normed, scaled, widen(R.q1[...], width), vecs[2])
        grad_low = grad_update.astype(BF)
        grad_pre, sig = silu_back(dot_nt(grad_low, graph.weight(R, 1, OUT)), pre_act)
        pre_low = grad_pre.astype(BF)
        grad_node = (wide + dot_nt(pre_low, graph.weight(R, 1, OWN))).astype(BF)
        grad_sum = dot_nt(pre_low, graph.weight(R, 1, OTHER))
        grad_high = grad_sum.astype(BF)
        grad_both = jnp.concatenate([grad_high, (grad_sum - grad_high.astype(F32)).astype(BF)], axis=0)

        @pl.when(section == 1)
        def _():
            R.out_node[...] = grad_node
            R.wg[0:width, :] += dot_tn(R.node0[...], pre_low)
            R.wg[width : 2 * width, :] += dot_tn(R.g1[...], pre_low)
            R.wg[2 * width : 3 * width, :] += dot_tn((pre_act * sig).astype(BF), grad_low)
            R.vec[0:1, :] += col_sum(grad_pre)
            R.vec[1:2, :] += col_sum(grad_update)
            R.vec[2:3, :] += col_sum(grad_normed * scaled)
            R.vec[3:4, :] += col_sum(grad_normed)

        vecs = graph.vectors(R, 0)

        def arriving(rows, mask):
            onehot = R.ohr[rows, :]
            spread = dot(jnp.concatenate([onehot, onehot], axis=1), grad_both)
            return (eg2[rows, :].astype(F32) + mask * spread).astype(BF)

        def edge_back(sums):
            totals = [jnp.zeros((1, width), F32)] * 4
            for start in graph.starts:
                rows = pl.ds(start, graph.chunk)
                mask = R.emask[rows, :]
                low = arriving(rows, widen(mask, width))
                R.eg1[rows, :] = low
                wide = low.astype(F32)
                scaled = R.x0[rows, :].astype(F32)
                pre_act = R.z0[rows, :].astype(F32)
                inverse = widen(R.q0[rows, :] * mask, width)
                grad_update = norm_back(wide, scaled, inverse, vecs[2])
                grad_low = grad_update.astype(BF)
                grad_pre, sig = silu_back(dot_nt(grad_low, graph.weight(R, 0, OUT)), pre_act)
                R.gz[rows, :] = grad_pre.astype(BF)
                if sums:
                    R.gu[rows, :] = grad_low
                    R.a[rows, :] = (pre_act * sig).astype(BF)
                    normed = widen(mask, width) * wide
                    parts = (grad_pre, grad_update, normed * scaled, normed)
                    totals = [total + col_sum(part) for total, part in zip(totals, parts)]
            return totals

        @pl.when(section == 0)
        def _():
            totals = edge_back(True)
            edge_copy.wait()
            R.wg[0:width, :] += dot_tn(R.edge[...], R.gz[...])
            R.wg[width : 2 * width, :] += dot_tn(R.s0[...], R.gz[...])
            R.wg[2 * width : 3 * width, :] += dot_tn(R.a[...], R.gu[...])
            for k in range(4):
                R.vec[k : k + 1, :] += totals[k]

        @pl.when(section > 0)
        def _():
            edge_back(False)

        @pl.when(section == 1)
        def _():
            copy(R.eg1, R.edge_grad.at[micro], sem.at[2]).start()

        grad_recv = dot(R.ohrt[...], R.gz[...]).astype(BF)
        add_recv(graph, R, 0, R.node0, grad_recv)

        R.ng1[...] = grad_node
        R.gr0[...] = grad_recv
        node_copy = copy(R.out_node, R.node_grad.at[micro], sem.at[3])
        node_copy.start()
        if own_first:
            sender_sums(graph, R, R.gz)
        node_copy.wait()

        @pl.when(section == 1)
        def _():
            copy(R.eg1, R.edge_grad.at[micro], sem.at[2]).wait()

    return run_kernel(body, info, inputs, outputs, scratch, 10, 13 if graph.blocks <= 8 else 16)


PIECES = 8
TAIL_ROWS = 16


def stats_block(graph, R):
    section = R.info[0]
    edge_count = col_sum(R.emask[...])
    node_count = col_sum(R.nmask[...])
    even = (section & 1) == 0
    valid = jnp.where(even, edge_count, node_count)
    rows = [R.vec[0:4, :]]
    for k in range(4):
        pair = jnp.where(section < 2, R.first[k][0:2, :], R.second[k][0:2, :])
        rows.append(jnp.concatenate([pair[0:1], pair[1:2], valid, jnp.zeros_like(valid)], axis=1))
    rows.append(jnp.zeros((TAIL_ROWS - 8, graph.width), F32))
    return jnp.concatenate(rows, axis=0)


def pack_kernel(graph, info, wg, vec, stats, direct, after):
    width = graph.width
    held = wg.shape[0]
    piece = -(-(held + TAIL_ROWS) // (16 * PIECES)) * 16
    inputs = dict(
        wg=(wg, V),
        vec=(vec, V),
        emask=(graph.consts["emask"], V),
        nmask=(graph.consts["nmask"], V),
        first=[(stat, V) for stat in stats[0]],
        second=[(stat, V) for stat in stats[1]],
        after=either(after),
    )
    low = BF if direct else F32
    count = 2 if direct else 1
    outputs = dict(out=[((PIECES * piece // count, width), low, V, None)] * count)
    scratch = dict(stage=VMEM((PIECES * piece, width), low))

    def body(R):
        info = R.info
        core = info[1]
        R.stage[0:held, :] = R.wg[...].astype(low)
        R.stage[held : held + TAIL_ROWS, :] = stats_block(graph, R).astype(low)
        rest = PIECES * piece - held - TAIL_ROWS
        if rest:
            R.stage[held + TAIL_ROWS :, :] = jnp.zeros((rest, width), low)
        if direct:
            for k, side in ((1, 1 - core), (0, core)):
                for r in range(4):
                    line = lax.shift_right_logical(info[3 + r], 1)
                    start = pl.multiple_of((side * 4 + line) * piece, 16)
                    R.out[k][r * piece : (r + 1) * piece, :] = R.stage[pl.ds(start, piece), :]
        else:
            R.out[0][...] = R.stage[...]

    return run_kernel(body, info, inputs, outputs, scratch, 3, 8 if direct else 12).out, piece


def unpack_kernel(graph, info, mine, far, piece):
    width = graph.width
    quarter = width // 4
    inputs = dict(mine=[(array, V) for array in mine], far=[(array, V) for array in far])
    big = ((width, width), F32, H, None)
    outputs = dict(
        grads=[big] * 3,
        recv=((2 * quarter, width), F32, H, None),
        vec=[((1, width), F32, B, None)] * 4,
        rms=[((1, 4), F32, B, None)] * 2,
    )
    scratch = dict(
        wide=VMEM((PIECES * piece, width), F32),
        sem=pltpu.SemaphoreType.DMA((4,)),
    )

    def body(R):
        info, sem = R.info, R.sem
        core = info[1]
        for r in range(4):
            line = lax.shift_right_logical(info[3 + r], 1)
            for source, side in ((R.mine[r], core), (R.far[r], 1 - core)):
                start = pl.multiple_of((side * 4 + line) * piece, 16)
                R.wide[pl.ds(start, piece), :] = source[...].astype(F32)
        moves = [copy(R.wide.at[pl.ds(k * width, width)], R.grads[k], sem.at[k]) for k in range(3)]
        moves.append(copy(R.wide.at[pl.ds(3 * width, 2 * quarter)], R.recv, sem.at[3]))
        for move in moves:
            move.start()
        base = 3 * width + 2 * quarter
        sums = R.wide[base : base + TAIL_ROWS, :]
        micro = lax.broadcasted_iota(jnp.int32, (1, 4), 1) ^ info[0]
        for k in range(4):
            R.vec[k][...] = sums[k : k + 1]
        for which in range(2):
            total = jnp.zeros((1, 4), F32)
            for k in range(4):
                row = sums[4 + k : 5 + k]
                square = row[:, which * LANES : which * LANES + 4] / (row[:, 2 * LANES : 2 * LANES + 4] * width)
                total = total + jnp.where(micro == k, jnp.sqrt(square), 0.0)
            R.rms[which][...] = total
        for move in moves:
            move.wait()

    return run_kernel(body, info, inputs, outputs, scratch, 3, 10)


def on_device(
    node_in,
    edge_in,
    node_cot,
    edge_cot,
    own_weight,
    other_weight,
    recv_weight,
    first_bias,
    out_weight,
    out_bias,
    norm_gain,
    norm_bias,
    senders,
    receivers,
    node_valid,
    edge_valid,
):
    micro_count, rows_n, width = node_in.shape
    rows_e = edge_in.shape[1]
    blocks = lax.axis_size("rows")
    section = lax.axis_index("section")
    row_pos = lax.axis_index("rows")
    core = row_pos % 2
    here = row_pos // 2
    graph = Graph(rows_n, rows_e, blocks, width)
    lines = blocks // 2
    direct = lines == 4
    quarter = width // 4

    def swap(value):
        return lax.ppermute(value, "rows", [(i, i ^ 1) for i in range(blocks)])

    def along(value, distance, flip=0):
        route = [(i, (i // 2 + distance) % lines * 2 + (i % 2 ^ flip)) for i in range(blocks)]
        return lax.ppermute(value, "rows", route)

    def across(value, rel):
        return lax.ppermute(value, "section", [(i, i ^ rel) for i in range(4)])

    if direct:
        places = [((here - r) % 4) * 2 + core for r in range(4)] + [((here - r) % 4) * 2 + 1 - core for r in range(4)]
    else:
        places = [jnp.int32(k) for k in range(blocks)]
    table = jnp.stack([jnp.stack([section, core, section ^ rel] + places) for rel in range(4)]).astype(jnp.int32)
    infos = [Info(table, rel) for rel in range(4)]

    def as_blocks(arrays, index):
        return [(array, index, row) for array in arrays for row in range(0, array.shape[-2], rows_n)]

    def pick(array, rel):
        return lax.dynamic_index_in_dim(array, section ^ rel, 0, keepdims=False)

    def lined_up(value):
        return [along(value, r) for r in range(1, 4)]

    send_local = senders % rows_n
    recv_local = receivers % rows_n
    node_ids = jnp.arange(rows_n, dtype=jnp.int32)
    consts = const_kernel(
        graph,
        infos[0],
        [
            (send_local[:, None] == node_ids[None, :]).astype(BF),
            (recv_local[:, None] == node_ids[None, :]).astype(BF),
            ((recv_local[None, :] == node_ids[:, None]) & (edge_valid[None, :] != 0)).astype(BF),
            jnp.broadcast_to(edge_valid.astype(F32)[:, None], (rows_e, LANES)),
            jnp.broadcast_to(node_valid.astype(F32)[:, None], (rows_n, LANES)),
        ],
    )
    graph.consts = dict(ohs=consts[0], ohr=consts[1], ohrt=consts[2], emask=consts[3], nmask=consts[4])

    weights = (own_weight[0], other_weight[0], out_weight[0])
    recv_rows = recv_weight.reshape(2 * quarter, width)
    half = half_kernel(graph, infos[0], weights, recv_rows, (first_bias, out_bias, norm_gain, norm_bias))
    half_x, half_y = across(half, 1), across(half, 2)
    held = half.shape[0]
    cut = held // 32 * 16
    plan = [(0, None, 0, cut, 0, 0), (1, None, cut, held - cut, 1, 0)]
    plan += [(0, None, 0, held, 2, 0), (1, None, 0, held, 2, held)]
    rows = [cut, held - cut, 2 * held]
    send_da, send_db, cat = glue_kernel(graph, infos[0], [half_x, half_y], plan, rows, [consts[4]])
    half_da, half_db, far_xy = across(send_da, 2), across(send_db, 1), swap(cat)
    plan = [(0, None, 0, cut, 0, 0), (1, None, 0, held - cut, 0, cut)]
    if direct:
        nodes = jnp.stack([pick(node_in, 0), pick(node_in, 3)])
        row_lines = [nodes] + lined_up(nodes)
        flat_lines = [line.reshape(2 * rows_n, width) for line in row_lines]
        own_plan = [(r, None, 0, 2 * rows_n, 0, 2 * r * rows_n) for r in range(4)]
        (own_cat,) = glue_kernel(graph, infos[0], flat_lines, own_plan, [8 * rows_n])
        own_far = swap(own_cat)
        plan += [(2, None, 2 * r * rows_n, rows_n, 1, (r - 1) * rows_n) for r in range(1, 4)]
        cat, share = glue_kernel(graph, infos[0], [half_da, half_db, own_cat], plan, [held, 3 * rows_n])
        node_shared = {rel: across(share, rel) for rel in (1, 2)}
    else:
        node_all = [lax.all_gather(pick(node_in, rel), "rows", axis=0, tiled=True) for rel in range(4)]
        (cat,) = glue_kernel(graph, infos[0], [half_da, half_db], plan, [held])
    far_d = swap(cat)
    near = {1: [(half_x, 0, held)], 2: [(half_y, 0, held)], 3: [(half_da, 0, cut), (half_db, 0, held - cut)]}
    far = {1: [(far_xy, 0, held)], 2: [(far_xy, held, held)], 3: [(far_d, 0, held)]}
    graph.consts.update(wall=wall_kernel(graph, infos[0], weights, recv_rows, half, near, far))

    first, second, third, node_far = {}, {}, {}, {}

    def add_first(rel, after):
        if not direct:
            blocks1 = as_blocks([node_all[rel]], None)
        elif rel % 3 == 0:
            place = rel // 3
            blocks1 = [(line, None, place * rows_n) for line in flat_lines]
            blocks1 += [(own_far, None, (2 * r + place) * rows_n) for r in range(4)]
        else:
            blocks1 = [(None, None, 0)]
            blocks1 += [(node_shared[rel], None, r * rows_n) for r in range(3)]
            blocks1 += [(node_far[0], None, (4 * (rel - 1) + r) * rows_n) for r in range(4)]
        first[rel] = first_kernel(graph, infos[rel], edge_in, node_in, blocks1, after)

    blocks2 = {}
    add_first(0, [])
    if direct:
        lines2 = [first[0].t2] + lined_up(first[0].t2)
        add_first(3, [first[0].stat])
        plan = []
        for k in range(2):
            plan.append((0, k + 1, 0, rows_n, 0, 4 * k * rows_n))
            plan.append((1 + k, None, 0, 3 * rows_n, 0, (4 * k + 1) * rows_n))
        sources = [node_in, node_shared[1], node_shared[2]]
        (cat,) = glue_kernel(graph, infos[0], sources, plan, [8 * rows_n], [first[0].stat])
        node_far[0] = swap(cat)
        add_first(1, [first[3].stat])
        plan = [(r, None, 0, rows_n, 0, r * rows_n) for r in range(4)]
        plan += [(r, None, 0, rows_n, 1, (r - 1) * rows_n) for r in range(1, 4)]
        cat, share = glue_kernel(graph, infos[0], lines2, plan, [4 * rows_n, 3 * rows_n], [first[1].stat])
        far2 = swap(cat)
        shared = {rel: across(share, rel) for rel in (1, 2)}
        blocks2[0] = as_blocks(lines2, None) + [(far2, None, r * rows_n) for r in range(4)]
    else:
        for rel in range(1, 4):
            add_first(rel, [first[rel - 1].stat])
        for rel in range(4):
            blocks2[rel] = as_blocks([lax.all_gather(first[rel].t2, "rows", axis=0, tiled=True)], None)

    def add_second(rel, after):
        before = second.get(rel - 1)
        second[rel] = second_kernel(
            graph, infos[rel], first[rel], blocks2[rel], node_cot, edge_cot, before, rel == 0, direct, after
        )

    def add_third(rel, sums, after):
        before = third[rel - 1] if rel else second[3]
        third[rel] = third_kernel(
            graph, infos[rel], first[rel], second[rel], sums, edge_in, before, rel == 0, direct, after
        )

    def share_blocks(rel, after, extra=()):
        plan = [(0, None, 0, rows_n, 0, 0), (1, None, 0, 3 * rows_n, 0, rows_n)]
        plan += [(2 + k, None, 0, 3 * rows_n, 1 + k, 0) for k in range(len(extra))]
        rows = [4 * rows_n] + [3 * rows_n] * len(extra)
        cat, *rest = glue_kernel(graph, infos[0], [first[rel].t2, shared[rel], *extra], plan, rows, after)
        far2 = swap(cat)
        entry = [(first[rel].t2, None, 0)] + [(shared[rel], None, r * rows_n) for r in range(3)]
        blocks2[rel] = entry + [(far2, None, r * rows_n) for r in range(4)]
        return [cat] + rest

    add_second(0, [first[1 if direct else 2].stat])
    if direct:
        got = swap(second[0].gs[1])
        cat, share = share_blocks(1, [second[0].stat], [share])
        shared[3] = across(share, 3)
        add_first(2, [cat])
        parts = add_kernel(graph, infos[0], [second[0].gs[0], got], rows_n, [first[2].stat])
        sums = [parts[0]] + [along(parts[r], -r) for r in range(1, 4)]
        share_blocks(2, [parts[0]])
        add_second(1, [parts[0]])
        share_blocks(3, [second[1].stat])
        add_second(2, [])
        add_second(3, [])
    else:
        for rel in range(1, 4):
            add_second(rel, [])
        sums = [lax.psum_scatter(second[0].gs[0], "rows", scatter_dimension=0, tiled=True)]
    add_third(0, sums, [])
    shared = {rel: across(third[0].total, rel) for rel in range(1, 4)}
    add_third(1, [shared[1]], [])
    if direct:
        parts = add_kernel(graph, infos[0], [third[0].gs[0], swap(third[0].gs[1])], rows_n, [third[1].token])
        sums = [parts[0]] + [along(parts[r], -r) for r in range(1, 4)]
        add_third(2, [shared[2]], [parts[0]])
    else:
        add_third(2, [shared[2]], [])
    add_third(3, [shared[3]], [])
    last = third[3]
    stats = ([first[rel].stat for rel in range(4)], [second[rel].stat for rel in range(4)])
    packed, piece = pack_kernel(graph, infos[0], last.wg, last.vec, stats, direct, sums if direct else [])
    if direct:
        (total,) = add_kernel(graph, infos[0], sums, rows_n, [packed[0]])
    else:
        total = lax.psum_scatter(third[0].gs[0], "rows", scatter_dimension=0, tiled=True)
    low = [total] + [lax.ppermute(total, "section", [(rel, 0)]) for rel in range(1, 4)]
    thirds = [third[rel] for rel in range(4)]
    wall = graph.consts["wall"]
    if direct:
        pieces = add_kernel(graph, infos[0], [packed[0], swap(packed[1])], piece)
        edge_zero = edge_zero_kernel(graph, infos[0], thirds, last.edge_grad, wall, [pieces[0]])
        zero = node_zero_kernel(graph, infos[0], thirds, low, last.node_grad, wall, [edge_zero.token])
        row_lines = [pieces[0]] + [along(pieces[r], -r) for r in range(1, 4)]
        (whole,) = add_kernel(graph, infos[0], row_lines, piece, [zero.token])
        row_lines = [whole] + lined_up(whole)
        result = unpack_kernel(graph, infos[0], row_lines, [swap(line) for line in row_lines], piece)
        grads, recv, vec, rms = result.grads, result.recv, result.vec, result.rms
    else:
        edge_zero = edge_zero_kernel(graph, infos[0], thirds, last.edge_grad, wall, [])
        zero = node_zero_kernel(graph, infos[0], thirds, low, last.node_grad, wall, [])
        full = lax.psum(packed[0], "rows")
        base = 3 * width + 2 * quarter
        grads = [full[k * width : (k + 1) * width] for k in range(3)]
        recv = full[3 * width : base]
        sums = full[base : base + TAIL_ROWS]
        vec = [sums[k : k + 1] for k in range(4)]
        rms = jnp.sqrt(sums[4:8, 0 : 2 * LANES : LANES] / (sums[4:8, 2 * LANES : 2 * LANES + 1] * width))
        rms = jnp.take(rms, jnp.arange(4, dtype=jnp.int32) ^ section, axis=0)
        rms = [rms[:, 0][None], rms[:, 1][None]]
    return (
        second[3].node_out[None],
        second[3].edge_out[None],
        zero.node_grad[None],
        edge_zero.edge_grad[None],
        grads[0][None],
        grads[1][None],
        recv.reshape(2, quarter, width),
        vec[0],
        grads[2][None],
        vec[1],
        vec[2],
        vec[3],
        rms[0],
        rms[1],
    )


def solution(mesh):
    whole = P("section", None, None)
    line = P("section", None)
    latents = P(None, "rows", None)
    outs = P("section", None, "rows", None)
    recv = P(None, "section", None)
    ends = P("rows")
    return jax.shard_map(
        on_device,
        mesh=mesh,
        in_specs=(latents,) * 4 + (whole, whole, recv, line, whole, line, line, line) + (ends,) * 4,
        out_specs=(outs,) * 4 + (whole, whole, recv, line, whole, line, line, line, line, line),
        check_vma=False,
    )
```
